32 devices in a mesh: wide: 8 (over y, x, core), narrow: 4 (over z).
Axes of the slice: x: 2, y: 2, z: 4, core: 2. Of those that a mesh axis runs over, the one named last changes fastest.
Arguments:
- tokens: bfloat16 [32768, 768], P(('wide', 'narrow')), may hold values from -6 to 6
- first_values: bfloat16 [32768, 384], P(('wide', 'narrow')), may hold values from -6 to 6
- cotangent: bfloat16 [32768, 768], P(('wide', 'narrow')), may hold values from -6 to 6
- attend_gain: bfloat16 [768], P(('wide', 'narrow')), may hold values from 0.5 to 1.5
- attend_shift: bfloat16 [768], P(('wide', 'narrow')), may hold values from -4 to 4
- joint_weight: bfloat16 [768, 1920], P(('wide', 'narrow')), may hold values from -0.21875 to 0.21875
- query_bias: bfloat16 [768], P(('wide', 'narrow')), may hold values from -6 to 6
- value_bias: bfloat16 [768], P(('wide', 'narrow')), may hold values from -4 to 4
- output_weight: bfloat16 [768, 768], P(('wide', 'narrow')), may hold values from -2.5 to 2.5
- output_bias: bfloat16 [768], P(('wide', 'narrow')), may hold values from -4 to 4
- feed_gain: bfloat16 [768], P(('wide', 'narrow')), may hold values from 0.5 to 1.5
- feed_shift: bfloat16 [768], P(('wide', 'narrow')), may hold values from -4 to 4
- expand_weight: bfloat16 [768, 3072], P(('wide', 'narrow')), may hold values from -0.21875 to 0.21875
- expand_bias: bfloat16 [3072], P(('wide', 'narrow')), may hold values from -4 to 4
- contract_weight: bfloat16 [3072, 768], P(('wide', 'narrow')), may hold values from -0.109375 to 0.109375
- contract_bias: bfloat16 [768], P(('wide', 'narrow')), may hold values from -4 to 4
Outputs:
- block_output: bfloat16 [32768, 768], P(('wide', 'narrow'))
- grad_tokens: bfloat16 [32768, 768], P(('wide', 'narrow'))
- grad_first_values: bfloat16 [32768, 384], P(('wide', 'narrow'))
- grad_attend_gain: float32 [768], P(('wide', 'narrow'))
- grad_attend_shift: float32 [768], P(('wide', 'narrow'))
- grad_joint_weight: float32 [768, 1920], P(('wide', 'narrow'))
- grad_query_bias: float32 [768], P(('wide', 'narrow'))
- grad_value_bias: float32 [768], P(('wide', 'narrow'))
- grad_output_weight: float32 [768, 768], P(('wide', 'narrow'))
- grad_output_bias: float32 [768], P(('wide', 'narrow'))
- grad_feed_gain: float32 [768], P(('wide', 'narrow'))
- grad_feed_shift: float32 [768], P(('wide', 'narrow'))
- grad_expand_weight: float32 [768, 3072], P(('wide', 'narrow'))
- grad_expand_bias: float32 [3072], P(('wide', 'narrow'))
- grad_contract_weight: float32 [3072, 768], P(('wide', 'narrow'))
- grad_contract_bias: float32 [768], P(('wide', 'narrow'))
The draws below stay inside these ranges and needn't reach their ends.
All inputs are finite; a program needn't handle non-finite values.
Results may differ from the reference program's by a relative error of at most 0.012.
Values may be sent and summed in bfloat16 or wider, within the bound.
A program may use at most 256 MiB of HBM per device.

```python
import jax
import jax.numpy as jnp
from jax import lax

D = 768
HEADS = 12
HEAD = 64
FF = 3072
LEN = 1024
TOKENS = 32768


def raised(array, rng, source, target, blocks, factor):
    owner, partner = [(jnp.arange(array.shape[position]) // (array.shape[position] // blocks)).reshape([-1 if axis == position else 1 for axis in range(array.ndim)]) for position in (source, target)]
    chosen = jax.random.permutation(rng, blocks)[partner]
    strong = (owner == chosen) | (owner == (partner + blocks // 2) % blocks)
    return jnp.where(strong, factor * array, array)


def block_scale(rng, shape, shards, smallest, largest):
    level, own = 1.0, jax.random.fold_in(rng, 6)
    for axis_at, shards_of in shards:
        draws = jnp.exp(jax.random.uniform(jax.random.fold_in(own, axis_at), (shards_of,), jnp.float32, smallest / len(shards), largest / len(shards)))
        level = level * jnp.repeat(draws, shape[axis_at] // shards_of).reshape([-1 if axis == axis_at else 1 for axis in range(len(shape))])
    return level


def gaussian(own_key, dims, scale, bound, split=(), kind=jnp.bfloat16):
    loudness = block_scale(own_key, dims, split, -0.22, 0.18) if split else 1.0
    values = jax.random.normal(own_key, dims, jnp.float32) * scale * loudness
    return jnp.minimum(jnp.maximum(values, -bound), bound).astype(kind)


def heavy_noise(stream_key, dims, scale, most, pieces, heavy, held_as=jnp.bfloat16):
    drawn = scale * jax.random.normal(stream_key, dims, jnp.float32)
    if pieces:
        drawn = drawn * block_scale(stream_key, dims, pieces, -0.22, 0.18)
    return jnp.clip(raised(drawn, jax.random.fold_in(stream_key, 3), *heavy), -most, most).astype(held_as)


def setup_inputs(seed: int = 0) -> dict:
    streams_of = jax.random.split(jax.random.key(seed), 17)
    return {
        "tokens": gaussian(streams_of[0], (TOKENS, D), 1.0, 6.0, ((0, 32),)),
        "first_values": gaussian(streams_of[1], (TOKENS, D // 2), 1.0, 6.0, ((0, 32),)),
        "cotangent": heavy_noise(streams_of[2], (TOKENS, D), 1.0, 6.0, ((0, 32),), (0, 1, 32, 2.75)),
        "attend_gain": jnp.clip(1.0 + 0.1 * jax.random.normal(streams_of[3], (D,), jnp.float32), 0.5, 1.5).astype(jnp.bfloat16),
        "attend_shift": gaussian(streams_of[4], (D,), 0.3, 4.0, ((0, 32),)),
        "joint_weight": gaussian(streams_of[5], (D, 2 * D + D // 2), D ** -0.5, 0.21875, ((0, 32),)),
        "query_bias": gaussian(streams_of[6], (D,), 0.5, 6.0, ((0, 32),)),
        "value_bias": gaussian(streams_of[7], (D,), 0.3, 4.0, ((0, 32),)),
        "output_weight": gaussian(streams_of[8], (D, D), (D * 8 // LEN) ** -0.5, 2.5, ((0, 32),)),
        "output_bias": gaussian(streams_of[9], (D,), 0.3, 4.0, ((0, 32),)),
        "feed_gain": jnp.clip(1.0 + 0.1 * jax.random.normal(streams_of[10], (D,), jnp.float32), 0.5, 1.5).astype(jnp.bfloat16),
        "feed_shift": gaussian(streams_of[11], (D,), 0.3, 4.0, ((0, 32),)),
        "expand_weight": gaussian(streams_of[12], (D, FF), D ** -0.5, 0.21875, ((0, 32),)),
        "expand_bias": gaussian(streams_of[13], (FF,), 0.3, 4.0, ((0, 32),)),
        "contract_weight": gaussian(streams_of[14], (FF, D), FF ** -0.5, 0.109375, ((0, 32),)),
        "contract_bias": gaussian(streams_of[15], (D,), 0.3, 4.0, ((0, 32),)),
    }


highest = lax.Precision.HIGHEST
epsilon = 1e-05

@jax.custom_vjp
def low(v):
    return lax.optimization_barrier(v.astype(jnp.bfloat16)).astype(jnp.float32)

@jax.custom_vjp
def low_back(v):
    return v

def low_keep(v):
    return (low(v), None)

def low_pass(kept, grad):
    return (grad,)

def back_keep(v):
    return (v, None)

def back_low(kept, grad):
    return (low(grad),)
low.defvjp(low_keep, low_pass)
low_back.defvjp(back_keep, back_low)

def layer_norm(values, gain, shift):
    center = values - lax.optimization_barrier(jnp.mean(values, axis=-1, keepdims=True))
    spread = lax.optimization_barrier(jnp.mean(center * center, axis=-1, keepdims=True))
    return center * lax.rsqrt(spread + epsilon) * gain + shift

def product(left, right):
    return jnp.dot(left, right, precision=highest)

def attend_one(packed):
    queries, key_rows, value_rows = packed
    scores = jnp.einsum('qhd,khd->hqk', queries, key_rows, precision=highest) * HEAD ** (-0.5)
    scores = low_back(scores)
    positions = jnp.arange(LEN, dtype=jnp.int32)
    allowed = positions[:, None] >= positions[None, :]
    scores = jnp.where(allowed[None], scores, -jnp.inf)
    attn_probs = low(jax.nn.softmax(scores, axis=-1))
    return jnp.einsum('hqk,khd->qhd', attn_probs, value_rows, precision=highest)

def forward(tokens, first_values, attend_gain, attend_shift, joint_weight, query_bias, value_bias, output_weight, output_bias, feed_gain, feed_shift, expand_weight, expand_bias, contract_weight, contract_bias):
    hidden_one = low(layer_norm(tokens, attend_gain, attend_shift))
    projected = product(hidden_one, joint_weight)
    queries = low_back(low(projected[:, :D] + query_bias))
    key_rows = low_back(low(projected[:, D:2 * D]))
    value_rows = low_back(low(jnp.concatenate([projected[:, 2 * D:], first_values], axis=1) + value_bias))
    seq_count = tokens.shape[0] // LEN

    def heads_view(matrix):
        return matrix.reshape(seq_count, LEN, HEADS, HEAD)
    mixed = lax.map(jax.checkpoint(attend_one), (heads_view(queries), heads_view(key_rows), heads_view(value_rows)))
    mixed = low_back(low(mixed.reshape(tokens.shape[0], D)))
    resid = tokens + low_back(product(mixed, output_weight) + output_bias)
    hidden_two = low(layer_norm(resid, feed_gain, feed_shift))
    pre_act = low_back(product(hidden_two, expand_weight) + expand_bias)
    activated = low(jax.nn.gelu(pre_act, approximate=True))
    return resid + product(activated, contract_weight) + contract_bias

def reference(tokens, first_values, cotangent, attend_gain, attend_shift, joint_weight, query_bias, value_bias, output_weight, output_bias, feed_gain, feed_shift, expand_weight, expand_bias, contract_weight, contract_bias):
    inputs = [tokens, first_values, attend_gain, attend_shift, joint_weight, query_bias, value_bias, output_weight, output_bias, feed_gain, feed_shift, expand_weight, expand_bias, contract_weight, contract_bias]
    floats = [item.astype(jnp.float32) for item in inputs]
    result, pull_back = jax.vjp(forward, *floats)
    grads = pull_back(cotangent.astype(jnp.float32))
    return (result.astype(jnp.bfloat16), grads[0].astype(jnp.bfloat16), grads[1].astype(jnp.bfloat16), grads[2], grads[3], grads[4], grads[5], grads[6], grads[7], grads[8], grads[9], grads[10], grads[11], grads[12], grads[13], grads[14])
```

```python
import functools

import jax
import jax.numpy as jnp
from jax import lax
from jax.experimental import pallas as pl
from jax.experimental.pallas import tpu as pltpu
from jax.sharding import PartitionSpec as P

D = 768
HEAD = 64
FF = 3072
LEN = 1024
HALF = D // 2
SLAB = D // 8
PAIRS = D // (2 * HEAD)
QB = 256
EPS = 1e-05
BF = jnp.bfloat16
F32 = jnp.float32
MESH = pl.DeviceIdType.MESH
AXES = ("wide", "narrow")

UNITS = 15
JOINT_COLS = (0, 768, 1536, 384, 1152)
GAIN1, SHIFT1, QBIAS, VBIAS, OBIAS, GAIN2, SHIFT2, CBIAS, EBIAS = range(9)
VROWS = 16


def dot(left, right, left_dim=1, right_dim=0):
    return lax.dot_general(left, right, (((left_dim,), (right_dim,)), ((), ())), preferred_element_type=F32)


def loop(count, step):
    lax.fori_loop(0, count, lambda i, c: (step(i), c)[1], 0)


def rows_of(index, size):
    return pl.ds(pl.multiple_of(index * size, size), size)


def norm_parts(values):
    center = values - jnp.mean(values, axis=-1, keepdims=True)
    inv = lax.rsqrt(jnp.mean(center * center, axis=-1, keepdims=True) + EPS)
    return center * inv, inv


def norm_back(values, grad, gain):
    unit, inv = norm_parts(values)
    scaled = grad * gain
    mean_one = jnp.mean(scaled, axis=-1, keepdims=True)
    mean_two = jnp.mean(scaled * unit, axis=-1, keepdims=True)
    grad_in = inv * (scaled - mean_one - unit * mean_two)
    return grad_in, jnp.sum(grad * unit, axis=0, keepdims=True), jnp.sum(grad, axis=0, keepdims=True)


class Nothing:
    def __getattr__(self, name):
        return lambda *a, **k: None


def two_units(ref, unit):
    return jnp.concatenate([ref[unit].reshape(D, HALF), ref[unit + 1].reshape(D, HALF)], axis=1)


def stages(r, comm):
    vec = r.vec

    def vrow(i):
        return vec[i : i + 1, :]

    order = []

    def stage(function):
        order.append(function)
        return function


    def norm_one(i):
        rows = rows_of(i, 128)
        unit, _ = norm_parts(r.tokens[rows, :].astype(F32))
        r.h1[rows, :] = (unit * vrow(GAIN1) + vrow(SHIFT1)).astype(BF)

    @stage
    def run_norm_one():
        loop(LEN // 128, norm_one)


    def project_a(i):
        rows = rows_of(i, 512)
        weights = jnp.concatenate([r.wall[u].reshape(D, HALF) for u in (0, 1, 2)], axis=1)
        out = dot(r.h1[rows, :], weights)
        r.q[rows, 0:HALF] = ((out[:, 0:HALF] + vec[QBIAS : QBIAS + 1, 0:HALF]).astype(BF) * HEAD ** (-0.5)).astype(BF)
        r.k[rows, 0:HALF] = out[:, HALF:D].astype(BF)
        r.v[rows, 0:HALF] = (out[:, D:] + vec[VBIAS : VBIAS + 1, 0:HALF]).astype(BF)

    @stage
    def run_project_a():
        loop(LEN // 512, project_a)

    def project_b(i):
        rows = rows_of(i, 512)
        out = dot(r.h1[rows, :], two_units(r.wall, 3))
        r.q[rows, HALF:D] = ((out[:, 0:HALF] + vec[QBIAS : QBIAS + 1, HALF:D]).astype(BF) * HEAD ** (-0.5)).astype(BF)
        r.k[rows, HALF:D] = out[:, HALF:D].astype(BF)
        r.v[rows, HALF:D] = (r.v[rows, HALF:D].astype(F32) + vec[VBIAS : VBIAS + 1, HALF:D]).astype(BF)

    lanes = lax.broadcasted_iota(jnp.int32, (QB, 128), 1)
    first_lanes = lanes < HEAD
    lane_row = lax.broadcasted_iota(jnp.int32, (1, 128), 1)
    head_mask = [(lane_row < HEAD).astype(F32).astype(BF), (lane_row >= HEAD).astype(F32).astype(BF)]
    tri = lax.broadcasted_iota(jnp.int32, (QB, QB), 0) >= lax.broadcasted_iota(jnp.int32, (QB, QB), 1)

    def attend(pair):
        cols = rows_of(pair, 128)
        for block in range(LEN // QB):
            first, finish = block * QB, (block + 1) * QB
            qp = r.q[first:finish, cols]
            outs = []
            logs = r.logs[first:finish, :]
            for h in range(2):
                scores = dot(qp * head_mask[h], r.k[0:finish, cols], 1, 1)
                diag = jnp.where(tri, scores[:, first:finish], -jnp.inf)
                scores = diag if block == 0 else jnp.concatenate([scores[:, :first], diag], axis=1)
                peak = jnp.max(scores, axis=-1, keepdims=True)
                raised = jnp.exp(scores - peak)
                total = jnp.sum(raised, axis=-1, keepdims=True)
                outs.append(dot(raised.astype(BF), r.v[0:finish, cols]) * (1.0 / total))
                logs = jnp.where(lanes == 2 * pair + h, peak + jnp.log(total), logs)
            r.logs[first:finish, :] = logs
            r.mixed[first:finish, cols] = jnp.where(first_lanes, outs[0], outs[1]).astype(BF)

    @stage
    def run_attend():
        def step(i):
            @pl.when(i == PAIRS // 2)
            def _():
                comm.before("project_b")
                loop(LEN // 512, project_b)

            attend(i)
            comm.tick("attend", i)

        loop(PAIRS, step)

    def out_project(i):
        rows = rows_of(i, 256)
        resid = r.tokens[rows, :].astype(F32) + dot(r.mixed[rows, :], two_units(r.wall, 5)) + vrow(OBIAS)
        r.resid[rows, :] = resid
        unit, _ = norm_parts(resid)
        r.tokens[rows, :] = (unit * vrow(GAIN2) + vrow(SHIFT2)).astype(BF)

    @stage
    def run_out_project():
        loop(LEN // 256, out_project)
    h2 = r.tokens

    alpha = 0.7978845608028654
    beta = alpha * 0.044715

    def expand(j):
        comm.tick("expand", j)
        cols = rows_of(j, D)
        bias = vec[pl.ds(EBIAS + j, 1), :]

        def step(i):
            rows = rows_of(i, 256)
            pre = dot(h2[rows, :], two_units(r.wall, 7 + 2 * j)) + bias
            square = pre * pre
            bent = jnp.tanh(pre * (alpha + beta * square))
            half = 0.5 * bent + 0.5
            slope = half + (pre * (0.5 - 0.5 * bent * bent)) * (alpha + (3.0 * beta) * square)
            r.act[rows, cols] = (pre * half).astype(BF)
            r.gp[rows, cols] = slope.astype(BF)

        loop(LEN // 256, step)

    @stage
    def run_expand():
        loop(4, expand)

    def grad_contract(w):
        y, x, c = w // 4, (w // 2) % 2, w % 2
        grad = dot(r.act[:, rows_of(w, HALF)], r.cot[...], 0, 0)
        r.gc[0, y, x, c] = grad[:, :HALF].astype(BF)
        r.gc[1, y, x, c] = grad[:, HALF:].astype(BF)
        comm.tick("grad_contract", w)

    @stage
    def run_grad_contract():
        loop(8, grad_contract)

    def column_sum(i, total):
        return total + jnp.sum(r.cot[rows_of(i, 128), :].astype(F32), axis=0, keepdims=True)

    @stage
    def run_contract_bias():
        r.gvec[...] = jnp.zeros_like(r.gvec)
        r.gvec[CBIAS : CBIAS + 1, :] = lax.fori_loop(0, LEN // 128, column_sum, jnp.zeros((1, D), F32))

    def block_out(i):
        rows = rows_of(i, 256)
        weights = jnp.concatenate([r.wc[0].reshape(FF, HALF), r.wc[1].reshape(FF, HALF)], axis=1)
        r.leaving[rows, :] = (r.resid[rows, :] + dot(r.act[rows, :], weights) + vrow(CBIAS)).astype(BF)
        comm.tick("block_out", i)

    @stage
    def run_block_out():
        loop(LEN // 256, block_out)

    def grad_pre(j):
        y, x = j // 2, j % 2
        cols = rows_of(j, D)
        sums = jnp.zeros((1, D), F32)

        def step(i, sums):
            rows = rows_of(i, 512)
            weights = jnp.concatenate([r.wc[0, y, x].reshape(D, HALF), r.wc[1, y, x].reshape(D, HALF)], axis=1)
            grad = (dot(r.cot[rows, :], weights, 1, 1) * r.gp[rows, cols].astype(F32)).astype(BF)
            r.gp[rows, cols] = grad
            return sums + jnp.sum(grad.astype(F32), axis=0, keepdims=True)

        r.gvec[pl.ds(EBIAS + j, 1), :] = lax.fori_loop(0, LEN // 512, step, sums)
        comm.tick("grad_pre", j)

    @stage
    def run_grad_pre():
        loop(4, grad_pre)

    def grad_expand(j):
        grad = dot(h2[...], r.gp[:, rows_of(j, D)], 0, 0).astype(BF)
        for side in range(2):
            part = grad[:, side * HALF : (side + 1) * HALF].reshape(2, 2, 2, SLAB, HALF)
            r.ge[j // 2, :, :, :, rows_of(2 * (j % 2) + side, SLAB), :] = part
        comm.tick("grad_expand", j)

    @stage
    def run_grad_expand():
        loop(4, grad_expand)

    def grad_norm_two(i, sums):
        rows = rows_of(i, 256)
        weights = jnp.concatenate([r.wall[u].reshape(D, HALF) for u in range(7, 15)], axis=1)
        grad_in, gain, shift = norm_back(r.resid[rows, :], dot(r.gp[rows, :], weights, 1, 1), vrow(GAIN2))
        grad = r.cot[rows, :].astype(F32) + grad_in
        low = grad.astype(BF)
        r.resid[rows, :] = grad
        r.tokens[rows, :] = low
        comm.tick("grad_norm_two", i)
        return sums[0] + gain, sums[1] + shift, sums[2] + jnp.sum(low.astype(F32), axis=0, keepdims=True)

    @stage
    def run_grad_norm_two():
        zero = jnp.zeros((1, D), F32)
        gain, shift, obias = lax.fori_loop(0, LEN // 256, grad_norm_two, (zero, zero, zero))
        r.gvec[GAIN2 : GAIN2 + 1, :] = gain
        r.gvec[SHIFT2 : SHIFT2 + 1, :] = shift
        r.gvec[OBIAS : OBIAS + 1, :] = obias
    gattn = r.tokens

    def grad_output(i):
        grad = dot(r.mixed[:, rows_of(i, HALF)], gattn[...], 0, 0).astype(BF)
        for side in range(2):
            r.wall[12 + side, i] = grad[:, side * HALF : (side + 1) * HALF].reshape(2, 2, SLAB, HALF)

    @stage
    def run_grad_output():
        loop(2, grad_output)

    def grad_mixed(i):
        rows = rows_of(i, 512)
        grad = dot(gattn[rows, :], two_units(r.wall, 5), 1, 1).astype(BF)
        r.cot[rows, :] = grad

    @stage
    def run_grad_mixed():
        loop(LEN // 512, grad_mixed)

    def attend_back(pair):
        cols = rows_of(pair, 128)
        qsum = jnp.zeros((1, 128), F32)
        for block in reversed(range(LEN // QB)):
            first, finish = block * QB, (block + 1) * QB
            qp = r.q[first:finish, cols]
            gm = r.cot[first:finish, cols]
            kp = r.k[0:finish, cols]
            vp = r.v[0:finish, cols]
            logs = r.logs[first:finish, :]
            inner = gm.astype(F32) * r.mixed[first:finish, cols].astype(F32)
            parts = []
            for h in range(2):
                qm, gh = qp * head_mask[h], gm * head_mask[h]
                log_total = jnp.sum(jnp.where(lanes == 2 * pair + h, logs, 0.0), axis=-1, keepdims=True)
                mine = first_lanes if h == 0 else jnp.logical_not(first_lanes)
                inner_sum = jnp.sum(jnp.where(mine, inner, 0.0), axis=-1, keepdims=True)
                probs = jnp.exp(dot(qm, kp, 1, 1) - log_total)
                diag = jnp.where(tri, probs[:, first:finish], 0.0)
                probs = diag if block == 0 else jnp.concatenate([probs[:, :first], diag], axis=1)
                grad_scores = (probs * (dot(gh, vp, 1, 1) - inner_sum)).astype(BF)
                parts.append((probs.astype(BF), grad_scores, qm, gh, dot(grad_scores, kp)))
            gq = (jnp.where(first_lanes, parts[0][4], parts[1][4]) * HEAD ** (-0.5)).astype(BF)
            r.act[first:finish, cols] = gq
            qsum = qsum + jnp.sum(gq.astype(F32), axis=0, keepdims=True)
            both = [jnp.concatenate([a, b], axis=0) for a, b in zip(parts[0][:4], parts[1][:4])]
            gk = dot(both[1], both[2], 0, 0)
            gv = dot(both[0], both[3], 0, 0)
            if finish == LEN:
                r.gk[...] = gk
                r.gv[...] = gv
            else:
                r.gk[0:finish, :] += gk
                r.gv[0:finish, :] += gv
        low = r.gv[...].astype(BF)
        r.act[:, rows_of(PAIRS + pair, 128)] = r.gk[...].astype(BF)
        r.act[:, rows_of(2 * PAIRS + pair, 128)] = low
        r.gvec[QBIAS : QBIAS + 1, cols] = qsum
        r.gvec[VBIAS : VBIAS + 1, cols] = jnp.sum(low.astype(F32), axis=0, keepdims=True)

    def grad_joint(unit):
        start = JOINT_COLS[unit]
        grad = dot(r.h1[...], r.act[:, start : start + HALF], 0, 0).astype(BF)
        r.wall[7 + unit] = grad.reshape(2, 2, 2, SLAB, HALF)

    @stage
    def run_attend_back():
        def step(i):
            attend_back(i)

            @pl.when(i == PAIRS // 2 - 1)
            def _():
                for unit in (0, 1, 2):
                    grad_joint(unit)

            comm.tick("attend_back", i)

        loop(PAIRS, step)

    @stage
    def run_grad_joint():
        for unit in (3, 4):
            grad_joint(unit)

    def grad_norm_one(i, sums):
        rows = rows_of(i, 256)
        weights = jnp.concatenate([r.wall[u].reshape(D, HALF) for u in (0, 3, 1, 4, 2)], axis=1)
        grad_hidden = dot(r.act[rows, 0 : 2 * D + HALF], weights, 1, 1)
        grad_in, gain, shift = norm_back(r.mixed[rows, :].astype(F32), grad_hidden, vrow(GAIN1))
        r.leaving[rows, :] = (r.resid[rows, :] + grad_in).astype(BF)
        comm.tick("grad_norm_one", i)
        return sums[0] + gain, sums[1] + shift

    @stage
    def run_grad_norm_one():
        zero = jnp.zeros((1, D), F32)
        gain, shift = lax.fori_loop(0, LEN // 256, grad_norm_one, (zero, zero))
        r.gvec[GAIN1 : GAIN1 + 1, :] = gain
        r.gvec[SHIFT1 : SHIFT1 + 1, :] = shift
    return order


def compute(r, comm):
    comm.start()
    for run in stages(r, comm):
        name = run.__name__.removeprefix("run_")
        comm.before(name)
        run()
        comm.after(name)
    comm.finish()


class Refs:
    def __init__(self, **refs):
        self.__dict__.update(refs)


STATE = dict(
    tokens=((LEN, D), BF),
    cot=((LEN, D), BF),
    wall=((UNITS, 2, 2, 2, SLAB, HALF), BF),
    wc=((2, 2, 2, 2, FF // 8, HALF), BF),
    vec=((VROWS, D), F32),
    gvec=((VROWS, D), F32),
    h1=((LEN, D), BF),
    q=((LEN, D), BF),
    k=((LEN, D), BF),
    v=((LEN, D), BF),
    mixed=((LEN, D), BF),
    logs=((LEN, 128), F32),
    resid=((LEN, D), F32),
    leaving=((LEN, D), BF),
    act=((LEN, FF), BF),
    gp=((LEN, FF), BF),
    gc=((2, 2, 2, 2, FF // 8, HALF), BF),
    gk=((LEN, 128), F32),
    gv=((LEN, 128), F32),
)
ANY = pl.BlockSpec(memory_space=pl.ANY)
VMEM = pl.BlockSpec(memory_space=pltpu.VMEM)


class Whole(Nothing):
    def __init__(self, r, sem):
        self.r, self.sem = r, sem

    def move(self, source, target):
        copy = pltpu.make_async_copy(source, target, self.sem)
        copy.start()
        copy.wait()

    def start(self):
        r = self.r
        for source, target in (
            (r.tokens_in, r.tokens), (r.first_in, r.v.at[:, HALF:D]), (r.cot_in, r.cot),
            (r.wall_in, r.wall), (r.wc_in, r.wc), (r.vec_in, r.vec),
        ):
            self.move(source, target)

    def before(self, what):
        if what == "grad_norm_one":
            self.move(self.r.tokens_in, self.r.mixed)

    def after(self, what):
        r = self.r
        if what == "block_out":
            self.move(r.leaving, r.block_output)
        elif what == "grad_norm_one":
            self.move(r.leaving, r.grad_tokens)
        elif what == "grad_contract":
            self.move(r.gc, r.gc_out)
        elif what == "grad_expand":
            self.move(r.ge, r.ge_out)
        elif what == "grad_output":
            self.move(r.wall.at[12:14], r.gjo_out.at[5:7])
        elif what == "grad_joint":
            self.move(r.wall.at[7:12], r.gjo_out.at[0:5])
            self.move(r.act.at[:, 2 * D + HALF : 3 * D], r.grad_first)

    def finish(self):
        self.move(self.r.gvec, self.r.gvec_out)


def whole_kernel(*refs):
    names = ["tokens_in", "first_in", "cot_in", "wall_in", "wc_in", "vec_in"]
    names += ["block_output", "grad_tokens", "grad_first", "gc_out", "ge_out", "gjo_out", "gvec_out"]
    names += list(STATE) + ["sem"]
    r = Refs(**dict(zip(names, refs)))
    r.ge = r.wc
    compute(r, Whole(r, r.sem))


def units_of(matrix):
    count = matrix.shape[1] // HALF
    return matrix.reshape(2, 2, 2, SLAB, count, HALF).transpose(4, 0, 1, 2, 3, 5)


def matrix_of(units):
    count = units.shape[0]
    return units.transpose(1, 2, 3, 4, 0, 5).reshape(D, count * HALF)


def outside(args):
    (tokens, first_values, cotangent, gain1, shift1, joint, qbias, vbias, output, obias,
     gain2, shift2, expand, ebias, contract, cbias) = args
    gather = functools.partial(lax.all_gather, axis_name=AXES, axis=0, tiled=True)
    scatter = functools.partial(lax.psum_scatter, axis_name=AXES, scatter_dimension=0, tiled=True)
    joint_units = units_of(gather(joint))
    wall = jnp.concatenate(
        [jnp.stack([joint_units[start // HALF] for start in JOINT_COLS]), units_of(gather(output)), units_of(gather(expand))]
    )
    wc = gather(contract).reshape(2, 2, 2, FF // 8, 2, HALF).transpose(4, 0, 1, 2, 3, 5)
    vec = jnp.stack([gather(v) for v in (gain1, shift1, qbias, vbias, obias, gain2, shift2, cbias)])
    vec = jnp.concatenate([vec, gather(ebias).reshape(4, D), jnp.zeros((4, D), BF)]).astype(F32)
    sds = jax.ShapeDtypeStruct
    block_output, grad_tokens, grad_first, gc, ge, gjo, gvec = pl.pallas_call(
        whole_kernel,
        out_shape=(
            sds((LEN, D), BF), sds((LEN, D), BF), sds((LEN, HALF), BF), sds(wc.shape, BF), sds(wc.shape, BF),
            sds((7,) + wall.shape[1:], BF), sds((VROWS, D), F32),
        ),
        in_specs=[ANY] * 6,
        out_specs=(ANY,) * 7,
        scratch_shapes=[pltpu.VMEM(*item) for item in STATE.values()] + [pltpu.SemaphoreType.DMA],
        compiler_params=pltpu.CompilerParams(vmem_limit_bytes=64 * 2**20),
    )(tokens, first_values, cotangent, wall, wc, vec)
    gc = gc.transpose(1, 2, 3, 4, 0, 5).reshape(FF, D).astype(F32)
    ge = ge.reshape(2, 8, 4, SLAB, HALF).transpose(1, 3, 0, 2, 4).reshape(D, FF).astype(F32)
    order = [JOINT_COLS.index(start * HALF) for start in range(5)]
    gj = jnp.concatenate([matrix_of(gjo[u : u + 1]) for u in order], axis=1).astype(F32)
    go = matrix_of(gjo[5:7]).astype(F32)
    small = [scatter(gvec[i]) for i in range(8)]
    return (
        block_output, grad_tokens, grad_first, small[GAIN1], small[SHIFT1], scatter(gj), small[QBIAS], small[VBIAS],
        scatter(go), small[OBIAS], small[GAIN2], small[SHIFT2], scatter(ge), scatter(gvec[8:12].reshape(FF)),
        scatter(gc), small[CBIAS],
    )


class Linked:
    def __init__(self, r, depth):
        self.r, self.depth = r, depth
        wide, self.mz = lax.axis_index("wide"), lax.axis_index("narrow")
        self.my, self.mx, self.mc = wide // 4, (wide // 2) % 2, wide % 2
        self.wide = wide
        self.peer = {
            "c": (wide + 1 - 2 * self.mc, self.mz),
            "x": (wide + 2 - 4 * self.mx, self.mz),
            "y": (wide + 4 - 8 * self.my, self.mz),
        }
        for d in range(1, depth):
            self.peer["z%d" % d] = (wide, lax.rem(self.mz + d, depth))
        self.far = [lax.rem(self.mz + d, depth) for d in range(depth)]

    def remote(self, source, target, sems, place, where):
        send, recv = sems
        return pltpu.make_async_remote_copy(
            src_ref=source, dst_ref=target, send_sem=send.at[place], recv_sem=recv.at[place],
            device_id=self.peer[where], device_id_type=MESH,
        )

    def gather_z(self, g):
        r, mz, out = self.r, self.mz, []
        for d in range(1, self.depth):
            where = "z%d" % d
            if g in ("C0", "C1"):
                h = int(g[1])
                parts = [(
                    r.wc_in.at[:, h * HALF : (h + 1) * HALF],
                    r.wc.at[h, self.my, self.mx, self.mc, rows_of(mz, SLAB), :],
                )]
            else:
                source, stage, spans = self.small(g)
                parts = [(source.at[:, a:b], stage.at[mz, :, a:b]) for a, b in spans]
            for part, (source, target) in enumerate(parts):
                out.append(self.remote(source, target, (r.gz_send, r.gz_recv), (GROUPS.index(g), d - 1, part), where))
        return out

    def small(self, g):
        r = self.r
        if g[0] == "J":
            return r.wj_in, r.sj, [(c, c + HALF) for c in (JOINT_COLS[0:3] if g == "J0" else JOINT_COLS[3:5])]
        if g[0] == "O":
            return r.wo_in, r.so, [(0, D)]
        j = int(g[1])
        return r.we_in, r.se, [(j * D, (j + 1) * D)]

    def assemble(self, g):
        r = self.r
        if g in ("C0", "C1"):
            h = int(g[1])
            r.wc[h, self.my, self.mx, self.mc, rows_of(self.mz, SLAB), :] = r.wc_in[:, h * HALF : (h + 1) * HALF]
            return
        source, stage, spans = self.small(g)
        unit = UNIT_SPAN[g][0]
        for a, b in spans:
            stage[self.mz, :, a:b] = source[:, a:b]
            for c in range(a, b, HALF):
                rows = jnp.concatenate([stage[z, :, c : c + HALF].astype(F32) for z in range(self.depth)], axis=0)
                r.wall[unit, self.my, self.mx, self.mc] = rows.astype(BF)
                unit += 1

    def views(self, g):
        if g[0] == "C":
            return self.r.wc, (int(g[1]),), pl.ds(0, FF // 16), pl.ds(FF // 16, FF // 16)
        a, b = UNIT_SPAN[g]
        return self.r.wall, (pl.ds(a, b - a),), pl.ds(0, SLAB // 2), pl.ds(SLAB // 2, SLAB // 2)

    def gather_copies(self, g, step):
        ref, lead, low, high = self.views(g)
        y, x, c, both = self.my, self.mx, self.mc, slice(None)
        if step == 1:
            plan = [((y, x, c, low), "x", 0), ((y, x, c, high), "y", 1)]
        elif step == 2:
            plan = [((y, both, c, low), "y", 2), ((both, x, c, high), "x", 3)]
        else:
            plan = [((both, both, c), "c", 4)]
        sems = (self.r.g_send, self.r.g_recv)
        return [self.remote(ref.at[lead + at], ref.at[lead + at], sems, (GROUPS.index(g), n), w) for at, w, n in plan]

    def gather(self, g, step):
        if step == 0:
            for copy in self.gather_z(g):
                copy.start()
            return
        if step == 1:
            for copy in self.gather_z(g):
                copy.wait_recv()
            self.assemble(g)
        else:
            for copy in self.gather_copies(g, step - 1):
                copy.wait_recv()
        if step < 4:
            for copy in self.gather_copies(g, step):
                copy.start()
        else:
            for copy in self.gather_z(g) + [c for n in (1, 2, 3) for c in self.gather_copies(g, n)]:
                copy.wait_send()

    def vec_copies(self, way, step):
        r = self.r
        held, got = ((r.vsum, r.vgot), (r.gvec, r.ggot))[way]
        order = ("z", "x", "y", "c") if way == 0 else ("c", "x", "y", "z")
        kind = order[step]
        wheres = ["z%d" % d for d in range(1, self.depth)] if kind == "z" else [kind]
        out = []
        for where in wheres:
            n = {"c": 0, "x": 1, "y": 2}[kind] if kind != "z" else 2 + int(where[1])
            out.append(self.remote(held, got.at[n], (r.v_send, r.v_recv), (way, n), where))
        return out

    def vec_step(self, way, step):
        r = self.r
        held, got = ((r.vsum, r.vgot), (r.gvec, r.ggot))[way]
        if step > 0:
            copies = self.vec_copies(way, step - 1)
            for copy in copies:
                copy.wait()
            total = held[...].astype(F32)
            order = ("z", "x", "y", "c") if way == 0 else ("c", "x", "y", "z")
            kind = order[step - 1]
            places = [2 + d for d in range(1, self.depth)] if kind == "z" else [{"c": 0, "x": 1, "y": 2}[kind]]
            for n in places:
                total = total + got[n].astype(F32)
            if way == 0 and step == 4:
                r.vec[...] = total
            else:
                held[...] = total.astype(held.dtype)
        if step < 4:
            for copy in self.vec_copies(way, step):
                copy.start()

    def big(self, g):
        return g[0] in "CE"

    def grad_ref(self, g):
        if self.big(g):
            rows = FF // 8
            return self.r.gc if g[0] == "C" else self.r.ge, (int(g[1]),), pl.ds(0, rows // 2), pl.ds(rows // 2, rows // 2)
        a, b = GRAD_SPAN[g]
        return self.r.wall, (pl.ds(a, b - a),), pl.ds(0, SLAB // 2), pl.ds(SLAB // 2, SLAB // 2)

    def got_ref(self, g):
        r = self.r
        if self.big(g):
            return r.big_core, r.big_one, r.big_two, (int(g[1]),)
        a, b = GRAD_SPAN[g]
        return r.small_core, r.small_one, r.small_two, (pl.ds(a - 7, b - a),)

    def scatter_copies(self, g, step):
        ref, lead, low, high = self.grad_ref(g)
        core, one, two, mine = self.got_ref(g)
        y, x, c, both = self.my, self.mx, self.mc, slice(None)
        r, index = self.r, SUMS.index(g)
        if step == 0:
            plan = [((both, both, 1 - c), core.at[mine], "c", 0)]
        elif step == 1:
            plan = [
                ((both, 1 - x, c, low), one.at[0].at[mine], "x", 1),
                ((1 - y, both, c, high), one.at[1].at[mine], "y", 2),
            ]
        elif step == 2:
            plan = [
                ((1 - y, x, c, low), two.at[0].at[mine], "y", 3),
                ((y, 1 - x, c, high), two.at[1].at[mine], "x", 4),
            ]
        else:
            out = []
            for d in range(1, self.depth):
                far = self.far[d]
                if g[0] == "C":
                    parts = [(ref.at[lead + (y, x, c, rows_of(far, SLAB))], r.zc.at[int(g[1]), d - 1])]
                else:
                    stage, got, spans = self.stage(g)
                    parts = [(stage.at[far, :, a:b], got.at[d - 1, :, a:b]) for a, b in spans]
                for part, (source, target) in enumerate(parts):
                    place = (index, d - 1, part)
                    out.append(self.remote(source, target, (r.sz_send, r.sz_recv), place, "z%d" % d))
            return out
        sems = (r.s_send, r.s_recv)
        return [self.remote(ref.at[lead + at], target, sems, (index, n), w) for at, target, w, n in plan]

    def stage(self, g):
        r = self.r
        if g[0] == "J":
            return r.sj, r.zj, [(c, c + HALF) for c in (JOINT_COLS[0:3] if g == "J0" else JOINT_COLS[3:5])]
        if g[0] == "O":
            return r.so, r.zo, [(0, D)]
        h = int(g[1])
        return r.se, r.ze, [(h * 2 * D, (h + 1) * 2 * D)]

    def scatter(self, g, step):
        r = self.r
        ref, lead, low, high = self.grad_ref(g)
        core, one, two, _ = self.got_ref(g)
        y, x, c = self.my, self.mx, self.mc
        if step > 0:
            for copy in self.scatter_copies(g, step - 1):
                copy.wait_recv()

        def add(at, got):
            ref[at] = (ref[at].astype(F32) + got.astype(F32)).astype(BF)

        if self.big(g):
            leads = [(lead[0], lead[0])]
        else:
            a, b = GRAD_SPAN[g]
            leads = [(u, u - 7) for u in range(a, b)]
        if step == 1:
            for u, v in leads:
                def both_add(i, u=u, v=v):
                    add((u, i // 2, i % 2, c), core[v, i // 2, i % 2])

                loop(4, both_add)
        elif step == 2:
            for u, v in leads:
                def one_add(i, u=u, v=v):
                    add((u, i, x, c, low), one[0, v, i])
                    add((u, y, i, c, high), one[1, v, i])

                loop(2, one_add)
        elif step == 3:
            for n, (u, v) in enumerate(leads):
                if g[0] == "C":
                    add((u, y, x, c, low), two[0, v])
                    add((u, y, x, c, high), two[1, v])
                    continue
                final = jnp.concatenate(
                    [
                        ref[u, y, x, c, low, :].astype(F32) + two[0, v].astype(F32),
                        ref[u, y, x, c, high, :].astype(F32) + two[1, v].astype(F32),
                    ],
                    axis=0,
                )
                stage, _, spans = self.stage(g)
                starts = [s for a, b in spans for s in range(a, b, HALF)]
                share = SLAB // self.depth
                count = final.shape[0] // SLAB
                for s in range(count):
                    start = starts[n * count + s]
                    for z in range(self.depth):
                        rows = final[s * SLAB + z * share : s * SLAB + (z + 1) * share]
                        stage[z, :, start : start + HALF] = rows.astype(BF)
        elif step == 4:
            if g[0] == "C":
                h = int(g[1])
                total = r.gc[h, y, x, c, rows_of(self.mz, SLAB), :].astype(F32)
                for d in range(self.depth - 1):
                    total = total + r.zc[h, d].astype(F32)
                r.gc_out[:, h * HALF : (h + 1) * HALF] = total
            else:
                stage, got, spans = self.stage(g)
                out = {"J": r.gj_out, "O": r.go_out, "E": r.ge_out}[g[0]]
                for a, b in spans:
                    total = stage[self.mz, :, a:b].astype(F32)
                    for d in range(self.depth - 1):
                        total = total + got[d, :, a:b].astype(F32)
                    out[:, a:b] = total
            for n in range(4):
                for copy in self.scatter_copies(g, n):
                    copy.wait_send()
        turns = ([], [(0, "c")], [(1, "x"), (2, "y")], [(3, "y"), (4, "x")], [])
        if g[0] == "C":
            for n, where in turns[step]:
                pl.semaphore_signal(
                    r.free_sem.at[n, lead[0]], inc=1, device_id=self.peer[where], device_id_type=MESH
                )
        if g[0] == "E" and step < 3:
            for n, _ in turns[step + 1]:
                pl.semaphore_wait(r.free_sem.at[n, lead[0]], 1)
        if step < 4:
            for copy in self.scatter_copies(g, step):
                copy.start()

    def run(self, words):
        for word in words:
            name, step = word.split(".")
            if name == "vec":
                self.vec_step(0, int(step))
            elif name == "gvec":
                self.vec_step(1, int(step))
            elif name[0] == "g":
                self.gather(name[1:], int(step))
            elif name[0] == "s":
                self.scatter(name[1:], int(step))
            else:
                self.local(int(step)).wait()

    def local(self, n):
        r = self.r
        source, target = (
            (r.tokens_in, r.tokens),
            (r.first_in, r.v.at[:, HALF:D]),
            (r.cot_in, r.cot),
            (r.tokens_in, r.mixed),
            (r.act.at[:, 2 * D + HALF : 3 * D], r.grad_first),
            (r.leaving, r.block_output),
            (r.leaving, r.grad_tokens),
        )[n]
        return pltpu.make_async_copy(source, target, r.local_sem.at[n])

    def start(self):
        r = self.r
        for n in range(3):
            self.local(n).start()
        r.vsum[...] = r.vec_in[...]
        barrier = pltpu.get_barrier_semaphore()
        for where in self.peer:
            pl.semaphore_signal(barrier, inc=1, device_id=self.peer[where], device_id_type=MESH)
        pl.semaphore_wait(barrier, len(self.peer))
        self.run(PLAN["start"])

    def before(self, what):
        self.run(PLAN.get("before " + what, ()))

    def after(self, what):
        if what == "attend_back":
            self.local(3).start()
            self.local(4).start()
        elif what == "block_out":
            self.local(5).start()
        elif what == "grad_norm_one":
            self.local(6).start()
        self.run(PLAN.get("after " + what, ()))

    def tick(self, what, i):
        for n in range(8):
            words = PLAN.get("%s %d" % (what, n), ())
            if words:
                @pl.when(i == n)
                def _(words=words):
                    self.run(words)

    def finish(self):
        self.run(PLAN["finish"])


UNIT_SPAN = dict(J0=(0, 3), J1=(3, 5), O0=(5, 7), E0=(7, 9), E1=(9, 11), E2=(11, 13), E3=(13, 15))
GROUPS = ("J0", "J1", "O0", "E0", "E1", "E2", "E3", "C0", "C1")
GRAD_SPAN = dict(J0=(7, 10), J1=(10, 12), O0=(12, 14))
BIG = ("C0", "C1", "E0", "E1")
SUMS = BIG + ("O0", "J0", "J1")
PLAN = {
    "start": ("vec.0", "gJ0.0", "local.0", "vec.1", "gJ0.1", "gJ1.0", "gO0.0", "gE0.0", "gE1.0", "vec.2", "gJ0.2", "gE2.0", "gE3.0", "vec.3", "gJ1.1", "gC0.0", "gC1.0", "gJ0.3", "vec.4", "gO0.1",),
    "before project_a": ("gJ1.2", "gJ0.4",),
    "after project_a": ("gJ1.3", "gO0.2", "gE0.1", "local.1",),
    "attend 0": ("gE1.1",),
    "attend 1": ("gJ1.4", "gO0.3", "gE0.2",),
    "attend 2": ("gE2.1",),
    "attend 3": ("gE0.3", "gE1.2",),
    "attend 4": ("gE3.1", "gO0.4",),
    "attend 5": ("gE1.3", "gE2.2", "gC0.1",),
    "after out_project": ("gE0.4", "gE3.2", "gC1.1",),
    "expand 1": ("gE1.4", "gE2.3",),
    "expand 2": ("gE2.4", "gE3.3", "gC0.2",),
    "expand 3": ("gE3.4",),
    "before grad_contract": ("local.2",),
    "grad_contract 5": ("gC1.2", "gC0.3",),
    "after contract_bias": ("sC0.0", "sC1.0", "gC0.4", "gC1.3", "gC1.4",),
    "block_out 2": ("sC0.1",),
    "after block_out": ("sC1.1",),
    "grad_pre 3": ("sC0.2",),
    "grad_expand 1": ("sE0.0",),
    "after grad_expand": ("sE1.0", "sC1.2",),
    "grad_norm_two 2": ("sE0.1", "sC0.3",),
    "after grad_norm_two": ("sE1.1",),
    "after grad_output": ("sO0.0", "sC1.3",),
    "after grad_mixed": ("sE0.2", "sO0.1",),
    "attend_back 0": ("sE1.2", "sC0.4",),
    "attend_back 1": ("sE0.3", "sO0.2", "sC1.4",),
    "attend_back 2": ("sE1.3", "sJ0.0",),
    "attend_back 3": ("sJ0.1", "sO0.3", "sE0.4",),
    "attend_back 4": ("sE1.4", "sO0.4",),
    "attend_back 5": ("sJ0.2",),
    "after grad_joint": ("sJ1.0", "sJ0.3",),
    "before grad_norm_one": ("local.3", "local.4", "local.5",),
    "grad_norm_one 0": ("sJ1.1",),
    "grad_norm_one 2": ("sJ1.2",),
    "after grad_norm_one": ("gvec.0", "sJ1.3", "sJ0.4", "gvec.1", "gvec.2", "gvec.3",),
    "finish": ("sJ1.4", "gvec.4", "local.6",),
}


def linked_scratch(depth):
    share = SLAB // depth
    far = max(depth - 1, 1)
    dma = pltpu.SemaphoreType.DMA
    return dict(
        sj=pltpu.VMEM((depth, share, 2 * D + HALF), BF),
        so=pltpu.VMEM((depth, share, D), BF),
        se=pltpu.VMEM((depth, share, FF), BF),
        zj=pltpu.VMEM((far, share, 2 * D + HALF), BF),
        zo=pltpu.VMEM((far, share, D), BF),
        ze=pltpu.VMEM((far, share, FF), BF),
        zc=pltpu.VMEM((2, far, FF // 8 // depth, HALF), BF),
        big_core=pltpu.VMEM((2, 2, 2, FF // 8, HALF), BF),
        big_one=pltpu.VMEM((2, 2, 2, FF // 16, HALF), BF),
        big_two=pltpu.VMEM((2, 2, FF // 16, HALF), BF),
        small_core=pltpu.VMEM((7, 2, 2, SLAB, HALF), BF),
        small_one=pltpu.VMEM((2, 7, 2, SLAB // 2, HALF), BF),
        small_two=pltpu.VMEM((2, 7, SLAB // 2, HALF), BF),
        vsum=pltpu.VMEM((VROWS, D), BF),
        vgot=pltpu.VMEM((2 + depth, VROWS, D), BF),
        ggot=pltpu.VMEM((2 + depth, VROWS, D), F32),
        gz_send=dma((9, far, 3)), gz_recv=dma((9, far, 3)), g_send=dma((9, 5)), g_recv=dma((9, 5)),
        sz_send=dma((7, far, 3)), sz_recv=dma((7, far, 3)), s_send=dma((7, 5)), s_recv=dma((7, 5)),
        v_send=dma((2, 2 + depth)), v_recv=dma((2, 2 + depth)), local_sem=dma((7,)), free_sem=pltpu.SemaphoreType.REGULAR((5, 2)),
    )


def linked_kernel(depth, *refs):
    names = ["tokens_in", "first_in", "cot_in", "wj_in", "wo_in", "we_in", "wc_in", "vec_in"]
    names += ["block_output", "grad_tokens", "grad_first", "gj_out", "go_out", "ge_out", "gc_out", "gvec_out"]
    names += list(STATE) + list(linked_scratch(depth))
    r = Refs(**dict(zip(names, refs)))
    r.ge = r.wc
    compute(r, Linked(r, depth))
    r.gvec_out[...] = r.gvec[...]


def linked(depth, args):
    (tokens, first_values, cotangent, gain1, shift1, joint, qbias, vbias, output, obias,
     gain2, shift2, expand, ebias, contract, cbias) = args
    count = 8 * depth
    share = D // count
    me = lax.axis_index("wide") * depth + lax.axis_index("narrow")
    own = jnp.tile(jnp.stack([gain1, shift1, qbias, vbias, obias, gain2, shift2, cbias]), (1, count))
    place = lax.broadcasted_iota(jnp.int32, (8, D), 1)
    own = jnp.where(place // share == me, own, jnp.zeros((), BF))
    wide_bias = jnp.tile(ebias, count).reshape(4, D)
    place = lax.broadcasted_iota(jnp.int32, (4, D), 0) * D + lax.broadcasted_iota(jnp.int32, (4, D), 1)
    wide_bias = jnp.where(place // (4 * share) == me, wide_bias, jnp.zeros((), BF))
    vec = jnp.concatenate([own, wide_bias, jnp.zeros((VROWS - 12, D), BF)])
    sds = jax.ShapeDtypeStruct
    block_output, grad_tokens, grad_first, gj, go, ge, gc, gvec = pl.pallas_call(
        functools.partial(linked_kernel, depth),
        out_shape=(
            sds((LEN, D), BF), sds((LEN, D), BF), sds((LEN, HALF), BF), sds(joint.shape, F32), sds(output.shape, F32),
            sds(expand.shape, F32), sds(contract.shape, F32), sds((VROWS, D), F32),
        ),
        in_specs=[ANY] * 3 + [VMEM] * 5,
        out_specs=(ANY, ANY, ANY, VMEM, VMEM, VMEM, VMEM, VMEM),
        scratch_shapes=[pltpu.VMEM(*item) for item in STATE.values()] + list(linked_scratch(depth).values()),
        compiler_params=pltpu.CompilerParams(
            vmem_limit_bytes=64 * 2**20, collective_id=0, has_side_effects=True
        ),
    )(tokens, first_values, cotangent, joint, output, expand, contract, vec)
    small = lax.dynamic_slice(gvec, (0, me * share), (8, share))
    grad_ebias = lax.dynamic_slice(gvec[8:12].reshape(FF), (me * 4 * share,), (4 * share,))
    return (
        block_output, grad_tokens, grad_first, small[GAIN1], small[SHIFT1], gj, small[QBIAS], small[VBIAS],
        go, small[OBIAS], small[GAIN2], small[SHIFT2], ge, grad_ebias, gc, small[CBIAS],
    )


def solution(mesh):
    split, flat = P(AXES, None), P(AXES)
    wide, depth = mesh.shape["wide"], mesh.shape["narrow"]
    if wide == 8 and SLAB % (8 * depth) == 0:
        body = lambda *args: linked(depth, args)
    else:
        body = lambda *args: outside(args)
    return jax.shard_map(
        body,
        mesh=mesh,
        in_specs=(split, split, split, flat, flat, split, flat, flat, split, flat, flat, flat, split, flat, split, flat),
        out_specs=(split, split, split, flat, flat, split, flat, flat, split, flat, flat, flat, split, flat, split, flat),
        check_vma=False,
    )
```

```python
import functools

import jax
import jax.numpy as jnp
from jax import lax
from jax.experimental import pallas as pl
from jax.experimental.pallas import tpu as pltpu
from jax.sharding import PartitionSpec as P

D = 768
HEAD = 64
FF = 3072
LEN = 1024
HALF = D // 2
SLAB = D // 8
PAIRS = D // (2 * HEAD)
QB = 256
EPS = 1e-05
BF = jnp.bfloat16
F32 = jnp.float32
MESH = pl.DeviceIdType.MESH
AXES = ("wide", "narrow")

UNITS = 15
JOINT_COLS = (0, 768, 1536, 384, 1152)
GAIN1, SHIFT1, QBIAS, VBIAS, OBIAS, GAIN2, SHIFT2, CBIAS, EBIAS = range(9)
VROWS = 16
G_GAIN1, G_SHIFT1 = 0, 1
G_QBIAS, G_VBIAS, G_OBIAS, G_GAIN2, G_SHIFT2, G_CBIAS = range(8, 14)
G_EBIAS = 16
GROWS = 24


def dot(left, right, left_dim=1, right_dim=0):
    return lax.dot_general(left, right, (((left_dim,), (right_dim,)), ((), ())), preferred_element_type=F32)


def loop(count, step):
    lax.fori_loop(0, count, lambda i, c: (step(i), c)[1], 0)


def rows_of(index, size):
    return pl.ds(pl.multiple_of(index * size, size), size)


def norm_parts(values):
    center = values - jnp.mean(values, axis=-1, keepdims=True)
    inv = lax.rsqrt(jnp.mean(center * center, axis=-1, keepdims=True) + EPS)
    return center * inv, inv


def norm_back(values, grad, gain):
    unit, inv = norm_parts(values)
    scaled = grad * gain
    mean_one = jnp.mean(scaled, axis=-1, keepdims=True)
    mean_two = jnp.mean(scaled * unit, axis=-1, keepdims=True)
    grad_in = inv * (scaled - mean_one - unit * mean_two)
    return grad_in, jnp.sum(grad * unit, axis=0, keepdims=True), jnp.sum(grad, axis=0, keepdims=True)


class Nothing:
    def __getattr__(self, name):
        return lambda *a, **k: None


def two_units(ref, unit):
    return jnp.concatenate([ref[unit].reshape(D, HALF), ref[unit + 1].reshape(D, HALF)], axis=1)


def stages(r, comm):
    vec = r.vec

    def vrow(i):
        return vec[i : i + 1, :]

    order = []

    def stage(function):
        order.append(function)
        return function


    def norm_one(i):
        rows = rows_of(i, 128)
        unit, _ = norm_parts(r.tokens[rows, :].astype(F32))
        r.h1[rows, :] = (unit * vrow(GAIN1) + vrow(SHIFT1)).astype(BF)

    @stage
    def run_norm_one():
        r.gvec[...] = jnp.zeros_like(r.gvec)
        loop(LEN // 128, norm_one)

    def project(low, high):
        def step(i):
            rows = rows_of(i, 512)
            weights = jnp.concatenate([r.wall[u, :, :, :, :, low:high].reshape(D, high - low) for u in (0, 1, 2)], axis=1)
            q, k, v = jnp.split(dot(r.h1[rows, :], weights), 3, axis=1)
            q = (q + vec[QBIAS : QBIAS + 1, low:high]).astype(BF)
            r.q[rows, low:high] = (q * HEAD ** (-0.5)).astype(BF)
            r.k[rows, low:high] = k.astype(BF)
            r.v[rows, low:high] = (v + vec[VBIAS : VBIAS + 1, low:high]).astype(BF)

        loop(LEN // 512, step)

    @stage
    def run_project_a():
        project(0, 128)

    def project_b():
        project(128, HALF)

    def project_c(i):
        rows = rows_of(i, 512)
        out = dot(r.h1[rows, :], two_units(r.wall, 3))
        r.q[rows, HALF:D] = ((out[:, 0:HALF] + vec[QBIAS : QBIAS + 1, HALF:D]).astype(BF) * HEAD ** (-0.5)).astype(BF)
        r.k[rows, HALF:D] = out[:, HALF:D].astype(BF)
        r.v[rows, HALF:D] = (r.v[rows, HALF:D].astype(F32) + vec[VBIAS : VBIAS + 1, HALF:D]).astype(BF)

    first_lanes = lax.broadcasted_iota(jnp.int32, (QB, 128), 1) < HEAD
    lane_row = lax.broadcasted_iota(jnp.int32, (1, 128), 1)
    head_mask = [(lane_row < HEAD).astype(F32).astype(BF), (lane_row >= HEAD).astype(F32).astype(BF)]
    seen = lax.broadcasted_iota(jnp.int32, (QB, QB), 0) <= lax.broadcasted_iota(jnp.int32, (QB, QB), 1)
    seen = jnp.concatenate([seen, seen], axis=1)

    def both_heads(rows):
        return jnp.concatenate([rows * head_mask[0], rows * head_mask[1]], axis=0)

    def attend(pair):
        cols = rows_of(pair, 128)
        turned = jnp.transpose(r.v[:, cols])
        ones = jnp.ones((HEAD, LEN), BF)
        values = [jnp.concatenate([turned[:HEAD], ones], axis=0), jnp.concatenate([ones, turned[HEAD:]], axis=0)]
        for block in range(LEN // QB):
            first, finish = block * QB, (block + 1) * QB
            scores = dot(r.k[0:finish, cols], both_heads(r.q[first:finish, cols]), 1, 1)
            diag = jnp.where(seen, scores[first:finish], -jnp.inf)
            scores = diag if block == 0 else jnp.concatenate([scores[:first], diag], axis=0)
            peak = jnp.max(scores, axis=0, keepdims=True)
            raised = jnp.exp(scores - peak).astype(BF)
            parts = []
            for h in range(2):
                out = dot(values[h][:, 0:finish], raised[:, h * QB : (h + 1) * QB])
                total = out[HEAD : HEAD + 1] if h == 0 else out[0:1]
                parts.append(out[h * HEAD : (h + 1) * HEAD] * (1.0 / total))
                r.logs[pair, h : h + 1, first:finish] = peak[:, h * QB : (h + 1) * QB] + jnp.log(total)
            r.mixed[cols, first:finish] = jnp.concatenate(parts, axis=0).astype(BF)

    @stage
    def run_attend():
        def step(i):
            @pl.when(i == 1)
            def _():
                comm.before("project_b")
                project_b()

            @pl.when(i == PAIRS // 2)
            def _():
                comm.before("project_c")
                loop(LEN // 512, project_c)

            attend(i)
            comm.tick("attend", i)

        loop(PAIRS, step)

    def out_project(i):
        rows = rows_of(i, 256)
        resid = r.tokens[rows, :].astype(F32) + dot(r.mixed[:, rows], two_units(r.wall, 5), 0, 0) + vrow(OBIAS)
        r.resid[rows, :] = resid
        unit, _ = norm_parts(resid)
        r.tokens[rows, :] = (unit * vrow(GAIN2) + vrow(SHIFT2)).astype(BF)

    @stage
    def run_out_project():
        loop(LEN // 256, out_project)
    h2 = r.tokens

    alpha = 0.7978845608028654
    beta = alpha * 0.044715

    def expand(j):
        comm.tick("expand", j)
        cols = rows_of(j, D)
        bias = vec[pl.ds(EBIAS + j, 1), :]

        def step(i):
            rows = rows_of(i, 256)
            pre = dot(h2[rows, :], two_units(r.wall, 7 + 2 * j)) + bias
            square = pre * pre
            bent = jnp.tanh(pre * (alpha + beta * square))
            half = 0.5 * bent + 0.5
            slope = half + (pre * (0.5 - 0.5 * bent * bent)) * (alpha + (3.0 * beta) * square)
            r.act[rows, cols] = (pre * half).astype(BF)
            r.gp[rows, cols] = slope.astype(BF)

        loop(LEN // 256, step)

    @stage
    def run_expand():
        loop(4, expand)

    def grad_contract(w):
        y, x, c = w // 4, (w // 2) % 2, w % 2
        grad = dot(r.act[:, rows_of(w, HALF)], r.cot[...], 0, 0)
        r.gc[0, y, x, c] = grad[:, :HALF].astype(BF)
        r.gc[1, y, x, c] = grad[:, HALF:].astype(BF)
        comm.tick("grad_contract", w)

    @stage
    def run_grad_contract():
        loop(8, grad_contract)

    def column_sum(i, total):
        return total + jnp.sum(r.cot[rows_of(i, 128), :].astype(F32), axis=0, keepdims=True)

    @stage
    def run_contract_bias():
        r.gvec[G_CBIAS : G_CBIAS + 1, :] = lax.fori_loop(0, LEN // 128, column_sum, jnp.zeros((1, D), F32))

    def block_out(i):
        rows = rows_of(i, 256)
        weights = jnp.concatenate([r.wc[0].reshape(FF, HALF), r.wc[1].reshape(FF, HALF)], axis=1)
        r.leaving[rows, :] = (r.resid[rows, :] + dot(r.act[rows, :], weights) + vrow(CBIAS)).astype(BF)
        comm.tick("block_out", i)

    @stage
    def run_block_out():
        loop(LEN // 256, block_out)

    def grad_pre(j):
        y, x = j // 2, j % 2
        cols = rows_of(j, D)
        sums = jnp.zeros((1, D), F32)

        def step(i, sums):
            rows = rows_of(i, 512)
            weights = jnp.concatenate([r.wc[0, y, x].reshape(D, HALF), r.wc[1, y, x].reshape(D, HALF)], axis=1)
            grad = (dot(r.cot[rows, :], weights, 1, 1) * r.gp[rows, cols].astype(F32)).astype(BF)
            r.gp[rows, cols] = grad
            return sums + jnp.sum(grad.astype(F32), axis=0, keepdims=True)

        r.gvec[pl.ds(G_EBIAS + j, 1), :] = lax.fori_loop(0, LEN // 512, step, sums)
        comm.tick("grad_pre", j)

    @stage
    def run_grad_pre():
        loop(4, grad_pre)

    def grad_expand(j):
        grad = dot(h2[...], r.gp[:, rows_of(j, D)], 0, 0).astype(BF)
        for side in range(2):
            part = grad[:, side * HALF : (side + 1) * HALF].reshape(2, 2, 2, SLAB, HALF)
            r.ge[j // 2, :, :, :, rows_of(2 * (j % 2) + side, SLAB), :] = part
        comm.tick("grad_expand", j)

    @stage
    def run_grad_expand():
        loop(4, grad_expand)

    def grad_norm_two(i, sums):
        rows = rows_of(i, 256)
        weights = jnp.concatenate([r.wall[u].reshape(D, HALF) for u in range(7, 15)], axis=1)
        grad_in, gain, shift = norm_back(r.resid[rows, :], dot(r.gp[rows, :], weights, 1, 1), vrow(GAIN2))
        grad = r.cot[rows, :].astype(F32) + grad_in
        low = grad.astype(BF)
        r.resid[rows, :] = grad
        r.tokens[rows, :] = low
        comm.tick("grad_norm_two", i)
        return sums[0] + gain, sums[1] + shift, sums[2] + jnp.sum(low.astype(F32), axis=0, keepdims=True)

    @stage
    def run_grad_norm_two():
        zero = jnp.zeros((1, D), F32)
        gain, shift, obias = lax.fori_loop(0, LEN // 256, grad_norm_two, (zero, zero, zero))
        r.gvec[G_GAIN2 : G_GAIN2 + 1, :] = gain
        r.gvec[G_SHIFT2 : G_SHIFT2 + 1, :] = shift
        r.gvec[G_OBIAS : G_OBIAS + 1, :] = obias
    gattn = r.tokens

    def grad_output(i):
        grad = dot(r.mixed[rows_of(i, HALF), :], gattn[...]).astype(BF)
        for side in range(2):
            r.wall[12 + side, i] = grad[:, side * HALF : (side + 1) * HALF].reshape(2, 2, SLAB, HALF)

    @stage
    def run_grad_output():
        loop(2, grad_output)

    def grad_mixed(i):
        rows = rows_of(i, 512)
        grad = dot(gattn[rows, :], two_units(r.wall, 5), 1, 1).astype(BF)
        r.cot[rows, :] = grad

    @stage
    def run_grad_mixed():
        loop(LEN // 512, grad_mixed)

    def attend_back(pair):
        cols = rows_of(pair, 128)
        qsum = jnp.zeros((1, 128), F32)
        for block in reversed(range(LEN // QB)):
            first, finish = block * QB, (block + 1) * QB
            kp = r.k[0:finish, cols]
            gm = r.cot[first:finish, cols]
            qm, gh = both_heads(r.q[first:finish, cols]), both_heads(gm)
            inner = jnp.transpose(gm).astype(F32) * r.mixed[cols, first:finish].astype(F32)
            inner = [jnp.sum(inner[h * HEAD : (h + 1) * HEAD], axis=0, keepdims=True) for h in range(2)]
            log_total = jnp.concatenate([r.logs[pair, h : h + 1, first:finish] for h in range(2)], axis=1)
            probs = jnp.exp(dot(kp, qm, 1, 1) - log_total)
            diag = jnp.where(seen, probs[first:finish], 0.0)
            probs = diag if block == 0 else jnp.concatenate([probs[:first], diag], axis=0)
            grad_probs = dot(r.v[0:finish, cols], gh, 1, 1)
            grad_scores = (probs * (grad_probs - jnp.concatenate(inner, axis=1))).astype(BF)
            gq = dot(grad_scores, kp, 0, 0)
            gq = (jnp.where(first_lanes, gq[:QB], gq[QB:]) * HEAD ** (-0.5)).astype(BF)
            r.act[first:finish, cols] = gq
            qsum = qsum + jnp.sum(gq.astype(F32), axis=0, keepdims=True)
            gk = dot(grad_scores, qm)
            gv = dot(probs.astype(BF), gh)
            if finish == LEN:
                r.gk[...] = gk
                r.gv[...] = gv
            else:
                r.gk[0:finish, :] += gk
                r.gv[0:finish, :] += gv
        low = r.gv[...].astype(BF)
        r.act[:, rows_of(PAIRS + pair, 128)] = r.gk[...].astype(BF)
        r.act[:, rows_of(2 * PAIRS + pair, 128)] = low
        r.gvec[G_QBIAS : G_QBIAS + 1, cols] = qsum
        r.gvec[G_VBIAS : G_VBIAS + 1, cols] = jnp.sum(low.astype(F32), axis=0, keepdims=True)

    def grad_joint(unit, low, high):
        start = JOINT_COLS[unit]
        grad = dot(r.h1[...], r.act[:, start + low : start + high], 0, 0).astype(BF)
        r.wall[7 + unit, :, :, :, :, low:high] = grad.reshape(2, 2, 2, SLAB, high - low)

    @stage
    def run_attend_back():
        def step(i):
            attend_back(i)

            @pl.when(i == PAIRS // 2 - 1)
            def _():
                for unit in (0, 1, 2):
                    grad_joint(unit, 0, HALF)

            @pl.when(i == PAIRS - 2)
            def _():
                for unit in (3, 4):
                    grad_joint(unit, 0, 256)

            comm.tick("attend_back", i)

        loop(PAIRS, step)

    @stage
    def run_grad_joint():
        for unit in (3, 4):
            grad_joint(unit, 256, HALF)

    def grad_norm_one(i, sums):
        rows = rows_of(i, 256)
        weights = jnp.concatenate([r.wall[u].reshape(D, HALF) for u in (0, 3, 1, 4, 2)], axis=1)
        grad_hidden = dot(r.act[rows, 0 : 2 * D + HALF], weights, 1, 1)
        grad_in, gain, shift = norm_back(r.again[rows, :].astype(F32), grad_hidden, vrow(GAIN1))
        r.leaving[rows, :] = (r.resid[rows, :] + grad_in).astype(BF)
        comm.tick("grad_norm_one", i)
        return sums[0] + gain, sums[1] + shift

    @stage
    def run_grad_norm_one():
        zero = jnp.zeros((1, D), F32)
        gain, shift = lax.fori_loop(0, LEN // 256, grad_norm_one, (zero, zero))
        r.gvec[G_GAIN1 : G_GAIN1 + 1, :] = gain
        r.gvec[G_SHIFT1 : G_SHIFT1 + 1, :] = shift
    return order


def compute(r, comm):
    comm.start()
    for run in stages(r, comm):
        name = run.__name__.removeprefix("run_")
        comm.before(name)
        run()
        comm.after(name)
    comm.finish()


class Refs:
    def __init__(self, **refs):
        self.__dict__.update(refs)


STATE = dict(
    tokens=((LEN, D), BF),
    cot=((LEN, D), BF),
    wall=((UNITS, 2, 2, 2, SLAB, HALF), BF),
    wc=((2, 2, 2, 2, FF // 8, HALF), BF),
    vec=((VROWS, D), F32),
    gvec=((GROWS, D), F32),
    h1=((LEN, D), BF),
    q=((LEN, D), BF),
    k=((LEN, D), BF),
    v=((LEN, D), BF),
    mixed=((D, LEN), BF),
    logs=((PAIRS, 8, LEN), F32),
    resid=((LEN, D), F32),
    leaving=((LEN, D), BF),
    act=((LEN, FF), BF),
    gp=((LEN, FF), BF),
    gc=((2, 2, 2, 2, FF // 8, HALF), BF),
    gk=((LEN, 128), F32),
    gv=((LEN, 128), F32),
)
ANY = pl.BlockSpec(memory_space=pl.ANY)
VMEM = pl.BlockSpec(memory_space=pltpu.VMEM)


class Whole(Nothing):
    def __init__(self, r, sem):
        self.r, self.sem = r, sem

    def move(self, source, target):
        copy = pltpu.make_async_copy(source, target, self.sem)
        copy.start()
        copy.wait()

    def start(self):
        r = self.r
        for source, target in (
            (r.tokens_in, r.tokens), (r.first_in, r.v.at[:, HALF:D]), (r.cot_in, r.cot),
            (r.wall_in, r.wall), (r.wc_in, r.wc), (r.vec_in, r.vec),
        ):
            self.move(source, target)

    def before(self, what):
        if what == "grad_norm_one":
            self.move(self.r.tokens_in, self.r.again)

    def after(self, what):
        r = self.r
        if what == "block_out":
            self.move(r.leaving, r.block_output)
        elif what == "grad_norm_one":
            self.move(r.leaving, r.grad_tokens)
        elif what == "grad_contract":
            self.move(r.gc, r.gc_out)
        elif what == "grad_expand":
            self.move(r.ge, r.ge_out)
        elif what == "grad_output":
            self.move(r.wall.at[12:14], r.gjo_out.at[5:7])
        elif what == "grad_joint":
            self.move(r.wall.at[7:12], r.gjo_out.at[0:5])
            self.move(r.act.at[:, 2 * D + HALF : 3 * D], r.grad_first)

    def finish(self):
        self.move(self.r.gvec, self.r.gvec_out)


def whole_kernel(*refs):
    names = ["tokens_in", "first_in", "cot_in", "wall_in", "wc_in", "vec_in"]
    names += ["block_output", "grad_tokens", "grad_first", "gc_out", "ge_out", "gjo_out", "gvec_out"]
    names += list(STATE) + ["sem"]
    r = Refs(**dict(zip(names, refs)))
    r.ge = r.wc
    r.again = r.gp.at[:, 0:D]
    compute(r, Whole(r, r.sem))


def units_of(matrix):
    count = matrix.shape[1] // HALF
    return matrix.reshape(2, 2, 2, SLAB, count, HALF).transpose(4, 0, 1, 2, 3, 5)


def matrix_of(units):
    count = units.shape[0]
    return units.transpose(1, 2, 3, 4, 0, 5).reshape(D, count * HALF)


def outside(args):
    (tokens, first_values, cotangent, gain1, shift1, joint, qbias, vbias, output, obias,
     gain2, shift2, expand, ebias, contract, cbias) = args
    gather = functools.partial(lax.all_gather, axis_name=AXES, axis=0, tiled=True)
    scatter = functools.partial(lax.psum_scatter, axis_name=AXES, scatter_dimension=0, tiled=True)
    joint_units = units_of(gather(joint))
    wall = jnp.concatenate(
        [jnp.stack([joint_units[start // HALF] for start in JOINT_COLS]), units_of(gather(output)), units_of(gather(expand))]
    )
    wc = gather(contract).reshape(2, 2, 2, FF // 8, 2, HALF).transpose(4, 0, 1, 2, 3, 5)
    vec = jnp.stack([gather(v) for v in (gain1, shift1, qbias, vbias, obias, gain2, shift2, cbias)])
    vec = jnp.concatenate([vec, gather(ebias).reshape(4, D), jnp.zeros((4, D), BF)]).astype(F32)
    sds = jax.ShapeDtypeStruct
    block_output, grad_tokens, grad_first, gc, ge, gjo, gvec = pl.pallas_call(
        whole_kernel,
        out_shape=(
            sds((LEN, D), BF), sds((LEN, D), BF), sds((LEN, HALF), BF), sds(wc.shape, BF), sds(wc.shape, BF),
            sds((7,) + wall.shape[1:], BF), sds((GROWS, D), F32),
        ),
        in_specs=[ANY] * 6,
        out_specs=(ANY,) * 7,
        scratch_shapes=[pltpu.VMEM(*item) for item in STATE.values()] + [pltpu.SemaphoreType.DMA],
        compiler_params=pltpu.CompilerParams(vmem_limit_bytes=64 * 2**20),
    )(tokens, first_values, cotangent, wall, wc, vec)
    gc = gc.transpose(1, 2, 3, 4, 0, 5).reshape(FF, D).astype(F32)
    ge = ge.reshape(2, 8, 4, SLAB, HALF).transpose(1, 3, 0, 2, 4).reshape(D, FF).astype(F32)
    order = [JOINT_COLS.index(start * HALF) for start in range(5)]
    gj = jnp.concatenate([matrix_of(gjo[u : u + 1]) for u in order], axis=1).astype(F32)
    go = matrix_of(gjo[5:7]).astype(F32)
    small = [scatter(gvec[i]) for i in (0, 1, 8, 9, 10, 11, 12, 13)]
    return (
        block_output, grad_tokens, grad_first, small[GAIN1], small[SHIFT1], scatter(gj), small[QBIAS], small[VBIAS],
        scatter(go), small[OBIAS], small[GAIN2], small[SHIFT2], scatter(ge), scatter(gvec[G_EBIAS : G_EBIAS + 4].reshape(FF)),
        scatter(gc), small[CBIAS],
    )


class Linked:
    def __init__(self, r, depth):
        self.r, self.depth = r, depth
        wide, self.mz = lax.axis_index("wide"), lax.axis_index("narrow")
        self.my, self.mx, self.mc = wide // 4, (wide // 2) % 2, wide % 2
        self.peer = {
            "c": (wide + 1 - 2 * self.mc, self.mz),
            "x": (wide + 2 - 4 * self.mx, self.mz),
            "y": (wide + 4 - 8 * self.my, self.mz),
        }
        for d in range(1, depth):
            self.peer["z%d" % d] = (wide, lax.rem(self.mz + d, depth))
        self.far = [lax.rem(self.mz + d, depth) for d in range(depth)]
        self.share = SLAB // depth

    def remote(self, source, target, sems, place, where):
        send, recv = sems
        return pltpu.make_async_remote_copy(
            src_ref=source, dst_ref=target, send_sem=send.at[place], recv_sem=recv.at[place],
            device_id=self.peer[where], device_id_type=MESH,
        )

    def weights(self, g):
        if g[0] == "C":
            return self.r.wc, (int(g[1]),), slice(None)
        a, b, low, high = WEIGHT_SPAN[g]
        return self.r.wall, (pl.ds(a, b - a),), pl.ds(low, high - low)

    def source(self, g):
        r = self.r
        return {"J": (r.wj_in, r.sj), "O": (r.wo_in, r.so), "E": (r.we_in, r.se)}[g[0]] + (WEIGHT_COLS[g],)

    def gather_copies(self, g, step):
        r, y, x, c, both = self.r, self.my, self.mx, self.mc, slice(None)
        ref, lead, lanes = self.weights(g)
        index, late = GROUPS.index(g), g in LATE_Z
        phase = ("z", 1, 2, "c")[step] if not late else (1, 2, "z", "c")[step]
        if phase == "z":
            out = []
            for d in range(1, self.depth):
                if late:
                    view = ref.at[lead + (both, both, c, rows_of(self.mz, SLAB))]
                    parts = [(view, view)]
                elif g[0] == "C":
                    h = int(g[1])
                    parts = [(r.wc_in.at[:, h * HALF : (h + 1) * HALF], ref.at[lead + (y, x, c, rows_of(self.mz, SLAB))])]
                else:
                    rows, stage, spans = self.source(g)
                    parts = [(rows.at[:, a:b], stage.at[self.mz, :, a:b]) for a, b in spans]
                for part, (source, target) in enumerate(parts):
                    place = (index, d - 1, part)
                    out.append(self.remote(source, target, (r.gz_send, r.gz_recv), place, "z%d" % d))
            return out
        low, high = (pl.ds(0, FF // 16), pl.ds(FF // 16, FF // 16)) if g[0] == "C" else (
            pl.ds(0, SLAB // 2), pl.ds(SLAB // 2, SLAB // 2))
        if late:
            start = pl.multiple_of(self.mz * SLAB, SLAB)
            low, high = pl.ds(start, SLAB // 2), pl.ds(pl.multiple_of(start + SLAB // 2, SLAB // 2), SLAB // 2)
        if phase == 1:
            plan = [((y, x, c, low), "x", 0), ((y, x, c, high), "y", 1)]
        elif phase == 2:
            plan = [((y, both, c, low), "y", 2), ((both, x, c, high), "x", 3)]
        else:
            plan = [((both, both, c, both), "c", 4)]
        sems = (r.g_send, r.g_recv)
        views = [(ref.at[lead + at + (lanes,)], n, w) for at, w, n in plan]
        return [self.remote(view, view, sems, (index, n), w) for view, n, w in views]

    def assemble(self, g):
        r = self.r
        if g[0] == "C":
            h = int(g[1])
            r.wc[h, self.my, self.mx, self.mc, rows_of(self.mz, SLAB), :] = r.wc_in[:, h * HALF : (h + 1) * HALF]
            return
        source, stage, spans = self.source(g)
        first, _, low, high = WEIGHT_SPAN[g]
        for unit, start in enumerate(s for a, b in spans for s in range(a, b, high - low)):
            stop = start + high - low
            stage[self.mz, :, start:stop] = source[:, start:stop]
            rows = jnp.concatenate([stage[z, :, start:stop].astype(F32) for z in range(self.depth)], axis=0)
            r.wall[first + unit, self.my, self.mx, self.mc, :, low:high] = rows.astype(BF)

    def gather(self, g, step):
        if step > 0:
            for copy in self.gather_copies(g, step - 1):
                copy.wait_recv()
        if step == (0 if g in LATE_Z else 1):
            self.assemble(g)
        if step < 4:
            for copy in self.gather_copies(g, step):
                copy.start()
        else:
            for n in range(4):
                for copy in self.gather_copies(g, n):
                    copy.wait_send()

    def vec_copies(self, way, step):
        r = self.r
        held, got, kinds = self.vec_ways(way)
        kind = kinds[step]
        out = []
        for where in ["z%d" % d for d in range(1, self.depth)] if kind == "z" else [kind]:
            n = self.vec_place(where)
            out.append(self.remote(held, got(n), (r.v_send, r.v_recv), (way, n), where))
        return out

    def vec_place(self, where):
        return "cxy".index(where) if where in "cxy" else 2 + int(where[1])

    def vec_ways(self, way):
        r = self.r
        if way == 0:
            return r.vsum, lambda n: r.vgot.at[n], "zxyc"
        rows = slice(8, GROWS) if way == 1 else slice(0, 8)
        return r.gvec.at[rows, :], lambda n: r.ggot.at[n, rows, :], "cxyz"

    def vec_step(self, way, step):
        r = self.r
        held, got, kinds = self.vec_ways(way)
        if step > 0:
            for copy in self.vec_copies(way, step - 1):
                copy.wait()
            kind = kinds[step - 1]
            total = held[...].astype(F32)
            for where in ["z%d" % d for d in range(1, self.depth)] if kind == "z" else [kind]:
                total = total + got(self.vec_place(where))[...].astype(F32)
            if way == 0 and step == 4:
                r.vec[...] = total
            else:
                held[...] = total.astype(held.dtype)
        if step < 4:
            for copy in self.vec_copies(way, step):
                copy.start()

    def grads(self, g):
        r = self.r
        if g[0] in "CE":
            h = int(g[1])
            return (r.gc if g[0] == "C" else r.ge), [(h, h)], FF // 8, (0, HALF)
        a, b, low, high = GRAD_SPAN[g]
        return r.wall, [(u, u - 7) for u in range(a, b)], SLAB, (low, high)

    def scatter_copies(self, g, step):
        ref, leads, height, (left, right) = self.grads(g)
        r, index, late = self.r, SUMS.index(g), g in LATE_Z
        y, x, c, both = self.my, self.mx, self.mc, slice(None)
        lanes = pl.ds(left, right - left)
        if g[0] in "CE":
            core, one, two = r.big_core, r.big_one, r.big_two
            lead, mine = leads[0]
            if late:
                one, two = r.late_one, r.late_two
        else:
            core, one, two = r.small_core, r.small_one, r.small_two
            lead, mine = pl.ds(leads[0][0], len(leads)), pl.ds(leads[0][1], len(leads))
        phase = ("c", 1, 2, "z")[step] if not late else ("c", "z", 1, 2)[step]
        if phase == "z":
            out = []
            for d in range(1, self.depth):
                far = self.far[d]
                if late:
                    parts = [(ref.at[lead, both, both, c, rows_of(far, SLAB)], r.late.at[d - 1])]
                elif g[0] == "C":
                    parts = [(ref.at[lead, y, x, c, rows_of(far, SLAB)], r.zc.at[lead, d - 1])]
                else:
                    stage, got, spans = self.stage(g)
                    parts = [(stage.at[far, :, a:b], got.at[d - 1, :, a:b]) for a, b in spans]
                for part, (source, target) in enumerate(parts):
                    out.append(self.remote(source, target, (r.sz_send, r.sz_recv), (index, d - 1, part), "z%d" % d))
            return out
        low, high = pl.ds(0, height // 2), pl.ds(height // 2, height // 2)
        near = pl.ds(0, height // 2)
        if late:
            start = pl.multiple_of(self.mz * SLAB, SLAB)
            low, high = pl.ds(start, SLAB // 2), pl.ds(pl.multiple_of(start + SLAB // 2, SLAB // 2), SLAB // 2)
            near = pl.ds(0, SLAB // 2)
        near_mine = 0 if late else mine
        if phase == "c":
            plan = [((both, both, 1 - c, both), core.at[mine, :, :, :, lanes], "c", 0)]
        elif phase == 1:
            plan = [
                ((both, 1 - x, c, low), one.at[0, near_mine, :, near, lanes], "x", 1),
                ((1 - y, both, c, high), one.at[1, near_mine, :, near, lanes], "y", 2),
            ]
        else:
            plan = [
                ((1 - y, x, c, low), two.at[0, near_mine, near, lanes], "y", 3),
                ((y, 1 - x, c, high), two.at[1, near_mine, near, lanes], "x", 4),
            ]
        sems = (r.s_send, r.s_recv)
        return [self.remote(ref.at[(lead,) + at + (lanes,)], target, sems, (index, n), w) for at, target, w, n in plan]

    def stage(self, g):
        r = self.r
        stage, got = {"J": (r.sj, r.zj), "O": (r.so, r.zo), "E": (r.se, r.ze)}[g[0]]
        return stage, got, GRAD_COLS[g]

    def add_up(self, g, phase):
        r, y, x, c = self.r, self.my, self.mx, self.mc
        ref, leads, height, (left, right) = self.grads(g)
        late, lanes = g in LATE_Z, slice(left, right)
        core, one, two = (r.big_core, r.big_one, r.big_two) if g[0] in "CE" else (r.small_core, r.small_one, r.small_two)
        low, high, near = pl.ds(0, height // 2), pl.ds(height // 2, height // 2), slice(0, height // 2)
        if late:
            start = pl.multiple_of(self.mz * SLAB, SLAB)
            low, high = pl.ds(start, SLAB // 2), pl.ds(pl.multiple_of(start + SLAB // 2, SLAB // 2), SLAB // 2)
            near = slice(0, SLAB // 2)
            one, two = r.late_one, r.late_two

        def add(at, *got):
            total = ref[at].astype(F32)
            for item in got:
                total = total + item.astype(F32)
            ref[at] = total.astype(BF)

        for u, v in leads:
            w = 0 if late else v
            if phase == "c":
                def step(i, u=u, v=v):
                    add((u, i // 2, i % 2, c, slice(None), lanes), core[v, i // 2, i % 2, :, lanes])

                loop(4, step)
            elif phase == "z":
                def step(i, u=u):
                    rows = rows_of(self.mz, SLAB)
                    got = [r.late[d, i // 2, i % 2] for d in range(self.depth - 1)]
                    add((u, i // 2, i % 2, c, rows, lanes), *got)

                loop(4, step)
            elif phase == 1:
                def step(i, u=u, w=w):
                    add((u, i, x, c, low, lanes), one[0, w, i, near, lanes])
                    add((u, y, i, c, high, lanes), one[1, w, i, near, lanes])

                loop(2, step)
            elif g[0] == "C":
                if not late:
                    add((u, y, x, c, low), two[0, w])
                    add((u, y, x, c, high), two[1, w])
                else:
                    for part, (rows, half) in enumerate(((slice(0, SLAB // 2), low), (slice(SLAB // 2, SLAB), high))):
                        total = ref[u, y, x, c, half, :].astype(F32) + two[part, w, near, :].astype(F32)
                        r.gc_out[rows, u * HALF : (u + 1) * HALF] = total
        if phase == 2 and g[0] != "C":
            stage, _, spans = self.stage(g)
            places = iter([(s, s + right - left) for a, b in spans for s in range(a, b, right - left)])
            for u, v in leads:
                final = jnp.concatenate(
                    [
                        ref[u, y, x, c, half, lanes].astype(F32) + two[part, v, near, lanes].astype(F32)
                        for part, half in enumerate((low, high))
                    ],
                    axis=0,
                )
                for s in range(0, height, SLAB):
                    start, stop = next(places)
                    for z in range(self.depth):
                        rows = final[s + z * self.share : s + (z + 1) * self.share]
                        stage[z, :, start:stop] = rows.astype(BF)

    def put_out(self, g):
        r = self.r
        if g[0] == "C":
            h = int(g[1])
            total = r.gc[h, self.my, self.mx, self.mc, rows_of(self.mz, SLAB), :].astype(F32)
            for d in range(self.depth - 1):
                total = total + r.zc[h, d].astype(F32)
            r.gc_out[:, h * HALF : (h + 1) * HALF] = total
            return
        stage, got, spans = self.stage(g)
        out = {"J": r.gj_out, "O": r.go_out, "E": r.ge_out}[g[0]]
        for a, b in spans:
            total = stage[self.mz, :, a:b].astype(F32)
            for d in range(self.depth - 1):
                total = total + got[d, :, a:b].astype(F32)
            out[:, a:b] = total

    def scatter(self, g, step):
        r, late = self.r, g in LATE_Z
        phases = ("c", "z", 1, 2) if late else ("c", 1, 2, "z")
        if step > 0:
            for copy in self.scatter_copies(g, step - 1):
                copy.wait_recv()
            if phases[step - 1] == "z" and not late:
                self.put_out(g)
            else:
                self.add_up(g, phases[step - 1])
        turns = {"c": [(0, "c")], 1: [(1, "x"), (2, "y")], 2: [(3, "y"), (4, "x")], "z": []}
        if "C" + g[1] in LATE_Z:
            turns[1] = turns[2] = []
        if g[0] == "C" and step > 0:
            for n, where in turns[phases[step - 1]]:
                pl.semaphore_signal(
                    r.free_sem.at[n, int(g[1])], inc=1, device_id=self.peer[where], device_id_type=MESH
                )
        if step < 4:
            if g[0] == "E":
                for n, _ in turns[phases[step]]:
                    pl.semaphore_wait(r.free_sem.at[n, int(g[1])], 1)
            for copy in self.scatter_copies(g, step):
                copy.start()
        else:
            for n in range(4):
                for copy in self.scatter_copies(g, n):
                    copy.wait_send()

    def run(self, words):
        for word in words:
            name, step = word.split(".")
            step = int(step)
            if name[0] == "v":
                self.vec_step(int(name[1]), step)
            elif name[0] == "g":
                self.gather(name[1:], step)
            elif name[0] == "s":
                self.scatter(name[1:], step)
            elif step < 10:
                self.local(step).wait()
            else:
                self.local(step - 10).start()

    def local(self, n):
        r = self.r
        source, target = (
            (r.tokens_in, r.tokens),
            (r.first_in, r.v.at[:, HALF:D]),
            (r.cot_in, r.cot),
            (r.tokens_in, r.again),
            (r.act.at[:, 2 * D + HALF : 3 * D], r.grad_first),
            (r.leaving, r.block_output),
            (r.leaving, r.grad_tokens),
        )[n]
        return pltpu.make_async_copy(source, target, r.local_sem.at[n])

    def place_vectors(self):
        r, share = self.r, self.share
        me = lax.axis_index("wide") * self.depth + self.mz
        r.vec[...] = jnp.zeros_like(r.vec)
        for n in range(8):
            r.vec[n, 0:share] = getattr(r, "vec%d" % n)[...].astype(F32)
        r.vec[8, 0 : 4 * share] = r.vec8[...].astype(F32)
        r.vsum[0:8, :] = pltpu.roll(r.vec[0:8, :], me * share, 1).astype(BF)
        start = me * 4 * share
        wide_bias = pltpu.roll(r.vec[8:VROWS, :], lax.rem(start, D), 1)[0:1]
        rows = lax.broadcasted_iota(jnp.int32, (VROWS - 8, D), 0) == start // D
        r.vsum[8:VROWS, :] = jnp.where(rows, wide_bias, 0.0).astype(BF)

    def start(self):
        r = self.r
        for n in range(3):
            self.local(n).start()
        self.place_vectors()
        barrier = pltpu.get_barrier_semaphore()
        for where in self.peer:
            pl.semaphore_signal(barrier, inc=1, device_id=self.peer[where], device_id_type=MESH)
        pl.semaphore_wait(barrier, len(self.peer))
        self.run(PLAN["start"])

    def before(self, what):
        self.run(PLAN.get("before " + what, ()))

    def after(self, what):
        self.run(PLAN.get("after " + what, ()))

    def tick(self, what, i):
        for n in range(8):
            words = PLAN.get("%s %d" % (what, n), ())
            if words:
                @pl.when(i == n)
                def _(words=words):
                    self.run(words)

    def finish(self):
        self.run(PLAN["finish"])


WEIGHT_SPAN = dict(
    J0=(0, 3, 0, 128), J1=(0, 3, 128, 384), J2=(3, 5, 0, 384), O0=(5, 7, 0, 384),
    E0=(7, 9, 0, 384), E1=(9, 11, 0, 384), E2=(11, 13, 0, 384), E3=(13, 15, 0, 384),
)
WEIGHT_COLS = dict(
    J0=[(c, c + 128) for c in JOINT_COLS[0:3]], J1=[(c + 128, c + HALF) for c in JOINT_COLS[0:3]],
    J2=[(c, c + HALF) for c in JOINT_COLS[3:5]], O0=[(0, D)],
    E0=[(0, D)], E1=[(D, 2 * D)], E2=[(2 * D, 3 * D)], E3=[(3 * D, 4 * D)],
)
GROUPS = tuple(WEIGHT_SPAN) + ("C0", "C1")
GRAD_SPAN = dict(J0=(7, 10, 0, 384), J1=(10, 12, 0, 256), J2=(10, 12, 256, 384), O0=(12, 14, 0, 384))
GRAD_COLS = dict(
    J0=[(c, c + HALF) for c in JOINT_COLS[0:3]], J1=[(c, c + 256) for c in JOINT_COLS[3:5]],
    J2=[(c + 256, c + HALF) for c in JOINT_COLS[3:5]], O0=[(0, D)], E0=[(0, 2 * D)], E1=[(2 * D, 4 * D)],
)
SUMS = ("C0", "C1", "E0", "E1") + tuple(GRAD_SPAN)
LATE_Z = ("C1",)
PLAN = {
    "start": ("v0.0", "gC1.0", "gJ0.0", "gJ2.0", "gJ1.0", "gE0.0", "v0.1", "gO0.0", "gJ0.1", "gE3.0", "v0.2", "gC1.1", "gJ2.1", "v0.3", "local.0", "v0.4",),
    "before norm_one": ("gJ0.2", "gJ1.1", "gJ2.2", "gE2.0",),
    "after norm_one": ("gE1.0", "gJ1.2", "gJ0.3",),
    "before project_a": ("gC0.0", "gO0.1", "gJ0.4",),
    "after project_a": ("gJ2.3", "gE3.1", "gE0.1", "gE2.1",),
    "before attend": ("gJ1.3", "gO0.2",),
    "attend 0": ("gE1.1", "gJ1.4",),
    "before project_b": ("gJ2.4",),
    "attend 1": ("gC1.2", "gE2.2",),
    "attend 2": ("gO0.3", "gE0.2",),
    "before project_c": ("gE1.2", "local.1",),
    "attend 4": ("gE0.3", "gO0.4", "gC0.1",),
    "attend 5": ("gE3.2", "gE2.3",),
    "before out_project": ("gE1.3",),
    "after out_project": ("gE2.4",),
    "before expand": ("gC0.2", "gE0.4",),
    "expand 1": ("gE3.3", "gE1.4",),
    "expand 3": ("gE3.4",),
    "before grad_contract": ("local.2", "gC0.3",),
    "grad_contract 2": ("gC1.3",),
    "grad_contract 7": ("gC0.4",),
    "after grad_contract": ("sC0.0",),
    "after contract_bias": ("gC1.4",),
    "block_out 0": ("sC1.0",),
    "block_out 3": ("sC0.1",),
    "after block_out": ("local.15",),
    "before grad_expand": ("sC1.1",),
    "grad_expand 3": ("sE0.0",),
    "after grad_expand": ("sE1.0",),
    "grad_norm_two 0": ("sC0.2",),
    "after grad_norm_two": ("local.13", "sE0.1", "sE1.1",),
    "before attend_back": ("sO0.0",),
    "attend_back 0": ("sC0.3",),
    "attend_back 1": ("sO0.1", "sE0.2",),
    "attend_back 2": ("sE1.2", "sJ0.0", "sO0.2",),
    "attend_back 3": ("sJ0.1", "sE0.3", "sC1.2",),
    "attend_back 4": ("sJ1.0", "sE1.3", "sJ0.2",),
    "after attend_back": ("local.14", "v1.0", "sJ1.1",),
    "after grad_joint": ("sJ2.0", "sO0.3", "sJ0.3",),
    "before grad_norm_one": ("v1.1", "local.3", "local.4", "local.5",),
    "grad_norm_one 0": ("sJ2.1",),
    "grad_norm_one 1": ("v1.2",),
    "grad_norm_one 2": ("sC1.3", "sJ1.2",),
    "grad_norm_one 3": ("v1.3",),
    "after grad_norm_one": ("local.16", "v2.0", "v2.1", "sJ2.2", "sE0.4", "sJ1.3", "v2.2",),
    "finish": ("sJ0.4", "sE1.4", "local.6", "sJ2.3", "v1.4", "v2.3", "sC0.4", "sC1.4", "sJ2.4", "sO0.4", "sJ1.4", "v2.4",),
}


def linked_scratch(depth):
    share = SLAB // depth
    far = max(depth - 1, 1)
    dma = pltpu.SemaphoreType.DMA
    return dict(
        sj=pltpu.VMEM((depth, share, 2 * D + HALF), BF),
        so=pltpu.VMEM((depth, share, D), BF),
        se=pltpu.VMEM((depth, share, FF), BF),
        zj=pltpu.VMEM((far, share, 2 * D + HALF), BF),
        zo=pltpu.VMEM((far, share, D), BF),
        ze=pltpu.VMEM((far, share, FF), BF),
        zc=pltpu.VMEM((2 - len(LATE_Z), far, SLAB, HALF), BF),
        late=pltpu.VMEM((far, 2, 2, SLAB, HALF), BF),
        late_one=pltpu.VMEM((2, 1, 2, SLAB // 2, HALF), BF),
        late_two=pltpu.VMEM((2, 1, SLAB // 2, HALF), BF),
        big_core=pltpu.VMEM((2, 2, 2, FF // 8, HALF), BF),
        big_one=pltpu.VMEM((2, 2, 2, FF // 16, HALF), BF),
        big_two=pltpu.VMEM((2, 2, FF // 16, HALF), BF),
        small_core=pltpu.VMEM((7, 2, 2, SLAB, HALF), BF),
        small_one=pltpu.VMEM((2, 7, 2, SLAB // 2, HALF), BF),
        small_two=pltpu.VMEM((2, 7, SLAB // 2, HALF), BF),
        vsum=pltpu.VMEM((VROWS, D), BF),
        vgot=pltpu.VMEM((2 + depth, VROWS, D), BF),
        ggot=pltpu.VMEM((2 + depth, GROWS, D), F32),
        gz_send=dma((10, far, 3)), gz_recv=dma((10, far, 3)), g_send=dma((10, 5)), g_recv=dma((10, 5)),
        sz_send=dma((8, far, 3)), sz_recv=dma((8, far, 3)), s_send=dma((8, 5)), s_recv=dma((8, 5)),
        v_send=dma((3, 2 + depth)), v_recv=dma((3, 2 + depth)), local_sem=dma((7,)),
        free_sem=pltpu.SemaphoreType.REGULAR((5, 2)),
    )


def linked_kernel(depth, *refs):
    names = ["tokens_in", "first_in", "cot_in", "wj_in", "wo_in", "we_in", "wc_in"]
    names += ["vec%d" % n for n in range(9)]
    names += ["gvec_out", "block_output", "grad_tokens", "grad_first", "gj_out", "go_out", "ge_out", "gc_out"]
    names += list(STATE) + list(linked_scratch(depth))
    r = Refs(**dict(zip(names, refs)))
    r.ge = r.wc
    r.again = r.gp.at[:, 0:D]
    compute(r, Linked(r, depth))
    r.gvec_out[...] = r.gvec[...]


def closing_kernel(depth, *refs):
    gvec, moved, targets, vectors, sem = refs[0], refs[1:8], refs[8:15], refs[15:24], refs[24]
    passing = refs[25:32]
    arrive = [pltpu.make_async_copy(a, b, sem.at[0, n]) for n, (a, b) in enumerate(zip(moved, passing))]
    leave = [pltpu.make_async_copy(a, b, sem.at[1, n]) for n, (a, b) in enumerate(zip(passing, targets))]
    for copy in arrive:
        copy.start()
    me = lax.axis_index("wide") * depth + lax.axis_index("narrow")
    share = SLAB // depth
    small = pltpu.roll(gvec[0:G_EBIAS, :], lax.rem(D - me * share, D), 1)
    start = me * 4 * share
    rows = lax.broadcasted_iota(jnp.int32, (4, D), 0) == start // D
    wide_bias = jnp.sum(jnp.where(rows, gvec[G_EBIAS : G_EBIAS + 4, :], 0.0), axis=0, keepdims=True)
    wide_bias = pltpu.roll(jnp.broadcast_to(wide_bias, (8, D)), lax.rem(D - lax.rem(start, D), D), 1)
    for n, row in enumerate((G_GAIN1, G_SHIFT1, G_QBIAS, G_VBIAS, G_OBIAS, G_GAIN2, G_SHIFT2, G_CBIAS)):
        vectors[n][...] = small[row, 0:share]
    vectors[8][...] = wide_bias[0, 0 : 4 * share]
    for first, second in zip(arrive, leave):
        first.wait()
        second.start()
    for copy in leave:
        copy.wait()


def linked(depth, args):
    (tokens, first_values, cotangent, gain1, shift1, joint, qbias, vbias, output, obias,
     gain2, shift2, expand, ebias, contract, cbias) = args
    share = SLAB // depth
    sds = jax.ShapeDtypeStruct
    results = pl.pallas_call(
        functools.partial(linked_kernel, depth),
        out_shape=(
            sds((GROWS, D), F32), sds((LEN, D), BF), sds((LEN, D), BF), sds((LEN, HALF), BF), sds(joint.shape, F32),
            sds(output.shape, F32), sds(expand.shape, F32), sds(contract.shape, F32),
        ),
        in_specs=[ANY] * 3 + [VMEM] * 13,
        out_specs=(VMEM, ANY, ANY, ANY, VMEM, VMEM, VMEM, VMEM),
        scratch_shapes=[pltpu.VMEM(*item) for item in STATE.values()] + list(linked_scratch(depth).values()),
        compiler_params=pltpu.CompilerParams(
            vmem_limit_bytes=64 * 2**20, collective_id=0, has_side_effects=True
        ),
    )(tokens, first_values, cotangent, joint, output, expand, contract,
      gain1, shift1, qbias, vbias, obias, gain2, shift2, cbias, ebias)
    vectors = (sds((share,), F32),) * 8 + (sds((4 * share,), F32),)
    closed = pl.pallas_call(
        functools.partial(closing_kernel, depth),
        out_shape=tuple(sds(item.shape, item.dtype) for item in results[1:]) + vectors,
        in_specs=[VMEM] + [ANY] * 7,
        out_specs=(ANY,) * 7 + (VMEM,) * 9,
        scratch_shapes=[pltpu.SemaphoreType.DMA((2, 7))] + [pltpu.VMEM(item.shape, item.dtype) for item in results[1:]],
    )(*results)
    block_output, grad_tokens, grad_first, gj, go, ge, gc = closed[:7]
    gain1, shift1, qbias, vbias, obias, gain2, shift2, cbias, ebias = closed[7:]
    return (
        block_output, grad_tokens, grad_first, gain1, shift1, gj, qbias, vbias, go, obias, gain2, shift2, ge, ebias, gc, cbias
    )


def solution(mesh):
    split, flat = P(AXES, None), P(AXES)
    wide, depth = mesh.shape["wide"], mesh.shape["narrow"]
    if wide == 8 and SLAB % (8 * depth) == 0:
        body = lambda *args: linked(depth, args)
    else:
        body = lambda *args: outside(args)
    return jax.shard_map(
        body,
        mesh=mesh,
        in_specs=(split, split, split, flat, flat, split, flat, flat, split, flat, flat, flat, split, flat, split, flat),
        out_specs=(split, split, split, flat, flat, split, flat, flat, split, flat, flat, flat, split, flat, split, flat),
        check_vma=False,
    )
```

```python
import functools

import jax
import jax.numpy as jnp
from jax import lax
from jax.experimental import pallas as pl
from jax.experimental.pallas import tpu as pltpu
from jax.sharding import PartitionSpec as P

D = 768
HEAD = 64
FF = 3072
LEN = 1024
HALF = D // 2
SLAB = D // 8
PAIRS = D // (2 * HEAD)
QB = LEN // 4
EPS = 1e-05
BF = jnp.bfloat16
F32 = jnp.float32
MESH = pl.DeviceIdType.MESH
AXES = ("wide", "narrow")

UNITS = 15
JOINT_COLS = (0, 768, 1536, 384, 1152)
GAIN1, SHIFT1, QBIAS, VBIAS, OBIAS, GAIN2, SHIFT2, CBIAS, EBIAS = range(9)
VROWS = 16
G_GAIN1, G_SHIFT1 = 0, 1
G_QBIAS, G_VBIAS, G_OBIAS, G_GAIN2, G_SHIFT2, G_CBIAS = range(8, 14)
G_EBIAS = 16
GROWS = 24


def dot(left, right, left_dim=1, right_dim=0):
    return lax.dot_general(left, right, (((left_dim,), (right_dim,)), ((), ())), preferred_element_type=F32)


def loop(count, step):
    lax.fori_loop(0, count, lambda i, c: (step(i), c)[1], 0)


def loop_in_pairs(count, step):
    loop(count // 2, lambda i: (step(2 * i), step(2 * i + 1)))


def sum_in_pairs(count, step, start, after):
    def pair(i, sums):
        sums = step(2 * i + 1, step(2 * i, sums))
        after(2 * i + 1)
        return sums

    return lax.fori_loop(0, count // 2, pair, start)


def rows_of(index, size):
    return pl.ds(pl.multiple_of(index * size, size), size)


def norm_parts(values):
    center = values - jnp.mean(values, axis=-1, keepdims=True)
    inv = lax.rsqrt(jnp.mean(center * center, axis=-1, keepdims=True) + EPS)
    return center * inv, inv


def norm_back(values, grad, gain):
    unit, inv = norm_parts(values)
    scaled = grad * gain
    mean_one = jnp.mean(scaled, axis=-1, keepdims=True)
    mean_two = jnp.mean(scaled * unit, axis=-1, keepdims=True)
    grad_in = inv * (scaled - mean_one - unit * mean_two)
    return grad_in, jnp.sum(grad * unit, axis=0, keepdims=True), jnp.sum(grad, axis=0, keepdims=True)


class Nothing:
    def __getattr__(self, name):
        return lambda *a, **k: None


def two_units(ref, unit):
    return jnp.concatenate([ref[unit].reshape(D, HALF), ref[unit + 1].reshape(D, HALF)], axis=1)


def stages(r, comm):
    vec = r.vec

    def vrow(i):
        return vec[i : i + 1, :]

    order = []

    def stage(function):
        order.append(function)
        return function


    def norm_one(i):
        rows = rows_of(i, 128)
        unit, _ = norm_parts(r.tokens[rows, :].astype(F32))
        r.h1[rows, :] = (unit * vrow(GAIN1) + vrow(SHIFT1)).astype(BF)

    def column_sum(i, total):
        return total + jnp.sum(r.cot[rows_of(i, 128), :].astype(F32), axis=0, keepdims=True)

    @stage
    def run_contract_bias():
        r.gvec[...] = jnp.zeros_like(r.gvec)
        r.gvec[G_CBIAS : G_CBIAS + 1, :] = lax.fori_loop(0, LEN // 128, column_sum, jnp.zeros((1, D), F32))

    @stage
    def run_norm_one():
        loop_in_pairs(LEN // 128, norm_one)

    def project(low, high):
        def step(i):
            rows = rows_of(i, 512)
            weights = jnp.concatenate([r.wall[u, :, :, :, :, low:high].reshape(D, high - low) for u in (0, 1, 2)], axis=1)
            q, k, v = jnp.split(dot(r.h1[rows, :], weights), 3, axis=1)
            q = (q + vec[QBIAS : QBIAS + 1, low:high]).astype(BF)
            r.q[rows, low:high] = (q * HEAD ** (-0.5)).astype(BF)
            r.k[rows, low:high] = k.astype(BF)
            r.v[rows, low:high] = (v + vec[VBIAS : VBIAS + 1, low:high]).astype(BF)

        loop(LEN // 512, step)

    @stage
    def run_project_a():
        project(0, 128)

    def project_b():
        project(128, HALF)

    def project_c(i):
        rows = rows_of(i, 512)
        out = dot(r.h1[rows, :], two_units(r.wall, 3))
        r.q[rows, HALF:D] = ((out[:, 0:HALF] + vec[QBIAS : QBIAS + 1, HALF:D]).astype(BF) * HEAD ** (-0.5)).astype(BF)
        r.k[rows, HALF:D] = out[:, HALF:D].astype(BF)
        r.v[rows, HALF:D] = (r.v[rows, HALF:D].astype(F32) + vec[VBIAS : VBIAS + 1, HALF:D]).astype(BF)

    first_lanes = lax.broadcasted_iota(jnp.int32, (QB, 128), 1) < HEAD
    lane_row = lax.broadcasted_iota(jnp.int32, (1, 128), 1)
    head_mask = [(lane_row < HEAD).astype(F32).astype(BF), (lane_row >= HEAD).astype(F32).astype(BF)]
    seen = lax.broadcasted_iota(jnp.int32, (QB, QB), 0) <= lax.broadcasted_iota(jnp.int32, (QB, QB), 1)
    seen = jnp.concatenate([seen, seen], axis=1)

    def both_heads(rows):
        return jnp.concatenate([rows * head_mask[0], rows * head_mask[1]], axis=0)

    def attend(pair):
        cols = rows_of(pair, 128)
        turned = jnp.transpose(r.v[:, cols])
        ones = jnp.ones((HEAD, LEN), BF)
        values = [jnp.concatenate([turned[:HEAD], ones], axis=0), jnp.concatenate([ones, turned[HEAD:]], axis=0)]
        for block in (3, 2, 1, 0):
            if block == 2:
                comm.tick("attend_m", pair)
            first, finish = block * QB, (block + 1) * QB
            scores = dot(r.k[0:finish, cols], both_heads(r.q[first:finish, cols]), 1, 1)
            diag = jnp.where(seen, scores[first:finish], -jnp.inf)
            scores = diag if block == 0 else jnp.concatenate([scores[:first], diag], axis=0)
            peak = jnp.max(scores, axis=0, keepdims=True)
            raised = jnp.exp(scores - peak).astype(BF)
            parts = []
            for h in range(2):
                out = dot(values[h][:, 0:finish], raised[:, h * QB : (h + 1) * QB])
                total = out[HEAD : HEAD + 1] if h == 0 else out[0:1]
                parts.append(out[h * HEAD : (h + 1) * HEAD] * (1.0 / total))
                r.logs[pair, h : h + 1, first:finish] = peak[:, h * QB : (h + 1) * QB] + jnp.log(total)
            r.mixed[cols, first:finish] = jnp.concatenate(parts, axis=0).astype(BF)

    @stage
    def run_attend():
        def step(i):
            @pl.when(i == 1)
            def _():
                comm.before("project_b")
                project_b()

            @pl.when(i == PAIRS // 2)
            def _():
                comm.before("project_c")
                loop(LEN // 512, project_c)

            attend(i)
            comm.tick("attend", i)

        loop(PAIRS, step)

    def out_project(i):
        rows = rows_of(i, 256)
        resid = r.tokens[rows, :].astype(F32) + dot(r.mixed[:, rows], two_units(r.wall, 5), 0, 0) + vrow(OBIAS)
        r.resid[rows, :] = resid
        unit, _ = norm_parts(resid)
        r.tokens[rows, :] = (unit * vrow(GAIN2) + vrow(SHIFT2)).astype(BF)

    @stage
    def run_out_project():
        loop(LEN // 256, out_project)
    h2 = r.tokens

    alpha = 0.7978845608028654
    beta = alpha * 0.044715

    def expand(j):
        comm.tick("expand_a", j)
        cols = rows_of(j, D)
        bias = vec[pl.ds(EBIAS + j, 1), :]

        def step(i):
            rows = rows_of(i, 256)
            pre = dot(h2[rows, :], two_units(r.wall, 7 + 2 * j)) + bias
            square = pre * pre
            bent = jnp.tanh(pre * (alpha + beta * square))
            half = 0.5 * bent + 0.5
            slope = half + (pre * (0.5 - 0.5 * bent * bent)) * (alpha + (3.0 * beta) * square)
            r.act[rows, cols] = (pre * half).astype(BF)
            r.gp[rows, cols] = slope.astype(BF)

        loop_in_pairs(LEN // 256, step)
        comm.tick("expand_b", j)
        r.gc[j // 2, j % 2] = dot(r.act[:, cols], r.cot[...], 0, 0).astype(BF).reshape(2, FF // 8, D)
        comm.tick("expand_c", j)

    @stage
    def run_expand():
        loop(4, expand)

    def block_out(i):
        rows = rows_of(i, 256)
        out = r.resid[rows, :] + dot(r.act[rows, :], r.wc[...].reshape(FF, D)) + vrow(CBIAS)
        r.act[rows, 0:D] = out.astype(BF)
        comm.tick("block_out", i)

    @stage
    def run_block_out():
        loop(LEN // 256, block_out)

    def grad_pre(j):
        cols = rows_of(j, D)

        def step(i, sums):
            rows = rows_of(i, 512)
            grad = dot(r.cot[rows, :], r.wc[j // 2, j % 2].reshape(D, D), 1, 1) * r.gp[rows, cols].astype(F32)
            grad = grad.astype(BF)
            r.gp[rows, cols] = grad
            return sums + jnp.sum(grad.astype(F32), axis=0, keepdims=True)

        r.gvec[pl.ds(G_EBIAS + j, 1), :] = lax.fori_loop(0, LEN // 512, step, jnp.zeros((1, D), F32))
        comm.tick("grad_pre", j)
        grad = dot(h2[...], r.gp[:, cols], 0, 0).astype(BF)
        for side in range(2):
            part = grad[:, side * HALF : (side + 1) * HALF].reshape(2, 2, 2, SLAB, HALF)
            r.ge[:, :, :, rows_of(2 * (j % 2) + side, SLAB), pl.ds(pl.multiple_of(j // 2 * HALF, HALF), HALF)] = part
        comm.tick("grad_expand", j)

    @stage
    def run_grad_pre():
        loop(4, grad_pre)

    def grad_norm_two(i, sums):
        rows = rows_of(i, 256)
        weights = jnp.concatenate([r.wall[u].reshape(D, HALF) for u in range(7, 15)], axis=1)
        grad_in, gain, shift = norm_back(r.resid[rows, :], dot(r.gp[rows, :], weights, 1, 1), vrow(GAIN2))
        grad = r.cot[rows, :].astype(F32) + grad_in
        low = grad.astype(BF)
        r.resid[rows, :] = grad
        r.tokens[rows, :] = low
        return sums[0] + gain, sums[1] + shift, sums[2] + jnp.sum(low.astype(F32), axis=0, keepdims=True)

    @stage
    def run_grad_norm_two():
        zero = jnp.zeros((1, D), F32)
        gain, shift, obias = sum_in_pairs(LEN // 256, grad_norm_two, (zero, zero, zero), functools.partial(comm.tick, "grad_norm_two"))
        r.gvec[G_GAIN2 : G_GAIN2 + 1, :] = gain
        r.gvec[G_SHIFT2 : G_SHIFT2 + 1, :] = shift
        r.gvec[G_OBIAS : G_OBIAS + 1, :] = obias
    gattn = r.tokens

    def grad_output(i):
        grad = dot(r.mixed[rows_of(i, HALF), :], gattn[...]).astype(BF)
        for side in range(2):
            r.wall[12 + side, i] = grad[:, side * HALF : (side + 1) * HALF].reshape(2, 2, SLAB, HALF)

    @stage
    def run_grad_output():
        loop(2, grad_output)

    def grad_mixed(i):
        rows = rows_of(i, 512)
        grad = dot(gattn[rows, :], two_units(r.wall, 5), 1, 1).astype(BF)
        r.cot[rows, :] = grad

    @stage
    def run_grad_mixed():
        loop(LEN // 512, grad_mixed)

    def attend_back(pair):
        cols = rows_of(pair, 128)
        qsum = jnp.zeros((1, 128), F32)
        for block in (3, 2, 1, 0):
            if block == 2:
                comm.tick("back_m", pair)
            first, finish = block * QB, (block + 1) * QB
            kp = r.k[0:finish, cols]
            gm = r.cot[first:finish, cols]
            qm, gh = both_heads(r.q[first:finish, cols]), both_heads(gm)
            inner = jnp.transpose(gm).astype(F32) * r.mixed[cols, first:finish].astype(F32)
            inner = [jnp.sum(inner[h * HEAD : (h + 1) * HEAD], axis=0, keepdims=True) for h in range(2)]
            log_total = jnp.concatenate([r.logs[pair, h : h + 1, first:finish] for h in range(2)], axis=1)
            probs = jnp.exp(dot(kp, qm, 1, 1) - log_total)
            diag = jnp.where(seen, probs[first:finish], 0.0)
            probs = diag if block == 0 else jnp.concatenate([probs[:first], diag], axis=0)
            grad_probs = dot(r.v[0:finish, cols], gh, 1, 1)
            grad_scores = (probs * (grad_probs - jnp.concatenate(inner, axis=1))).astype(BF)
            gq = dot(grad_scores, kp, 0, 0)
            gq = (jnp.where(first_lanes, gq[:QB], gq[QB:]) * HEAD ** (-0.5)).astype(BF)
            r.act[first:finish, cols] = gq
            qsum = qsum + jnp.sum(gq.astype(F32), axis=0, keepdims=True)
            gk = dot(grad_scores, qm)
            gv = dot(probs.astype(BF), gh)
            if finish == LEN:
                r.gk[...] = gk
                r.gv[...] = gv
            else:
                r.gk[0:finish, :] += gk
                r.gv[0:finish, :] += gv
        low = r.gv[...].astype(BF)
        r.act[:, rows_of(PAIRS + pair, 128)] = r.gk[...].astype(BF)
        r.act[:, rows_of(2 * PAIRS + pair, 128)] = low
        r.gvec[G_QBIAS : G_QBIAS + 1, cols] = qsum
        r.gvec[G_VBIAS : G_VBIAS + 1, cols] = jnp.sum(low.astype(F32), axis=0, keepdims=True)

    def grad_joint(unit, low, high):
        start = JOINT_COLS[unit]
        grad = dot(r.h1[...], r.act[:, start + low : start + high], 0, 0).astype(BF)
        r.wall[7 + unit, :, :, :, :, low:high] = grad.reshape(2, 2, 2, SLAB, high - low)

    @stage
    def run_attend_back():
        def step(i):
            attend_back(i)

            @pl.when(i == PAIRS // 2 - 1)
            def _():
                for unit in (0, 1, 2):
                    grad_joint(unit, 0, HALF)

            @pl.when(i == PAIRS - 2)
            def _():
                for unit in (3, 4):
                    grad_joint(unit, 0, 256)

            comm.tick("attend_back", i)

        loop(PAIRS, step)

    @stage
    def run_grad_joint():
        for unit in (3, 4):
            grad_joint(unit, 256, HALF)

    def grad_norm_one(i, sums):
        rows = rows_of(i, 256)
        weights = jnp.concatenate([r.wall[u].reshape(D, HALF) for u in (0, 3, 1, 4, 2)], axis=1)
        grad_hidden = dot(r.act[rows, 0 : 2 * D + HALF], weights, 1, 1)
        grad_in, gain, shift = norm_back(r.again[rows, :].astype(F32), grad_hidden, vrow(GAIN1))
        r.cot[rows, :] = (r.resid[rows, :] + grad_in).astype(BF)
        return sums[0] + gain, sums[1] + shift

    @stage
    def run_grad_norm_one():
        zero = jnp.zeros((1, D), F32)
        gain, shift = sum_in_pairs(LEN // 256, grad_norm_one, (zero, zero), functools.partial(comm.tick, "grad_norm_one"))
        r.gvec[G_GAIN1 : G_GAIN1 + 1, :] = gain
        r.gvec[G_SHIFT1 : G_SHIFT1 + 1, :] = shift
    return order


def compute(r, comm):
    comm.start()
    for run in stages(r, comm):
        name = run.__name__.removeprefix("run_")
        comm.before(name)
        run()
        comm.after(name)
    comm.finish()


class Refs:
    def __init__(self, **refs):
        self.__dict__.update(refs)


STATE = dict(
    tokens=((LEN, D), BF),
    cot=((LEN, D), BF),
    wall=((UNITS, 2, 2, 2, SLAB, HALF), BF),
    wc=((2, 2, 2, FF // 8, D), BF),
    vec=((VROWS, D), F32),
    gvec=((GROWS, D), F32),
    h1=((LEN, D), BF),
    q=((LEN, D), BF),
    k=((LEN, D), BF),
    v=((LEN, D), BF),
    mixed=((D, LEN), BF),
    logs=((PAIRS, 8, LEN), F32),
    resid=((LEN, D), F32),
    act=((LEN, FF), BF),
    gp=((LEN, FF), BF),
    gc=((2, 2, 2, FF // 8, D), BF),
    ge=((2, 2, 2, FF // 8, D), BF),
    gk=((LEN, 128), F32),
    gv=((LEN, 128), F32),
)
ANY = pl.BlockSpec(memory_space=pl.ANY)
VMEM = pl.BlockSpec(memory_space=pltpu.VMEM)


class Whole(Nothing):
    def __init__(self, r, sem):
        self.r, self.sem = r, sem

    def move(self, source, target):
        copy = pltpu.make_async_copy(source, target, self.sem)
        copy.start()
        copy.wait()

    def start(self):
        r = self.r
        for source, target in (
            (r.tokens_in, r.tokens), (r.first_in, r.v.at[:, HALF:D]), (r.cot_in, r.cot),
            (r.wall_in, r.wall), (r.wc_in, r.wc), (r.vec_in, r.vec),
        ):
            self.move(source, target)

    def before(self, what):
        if what == "grad_norm_one":
            self.move(self.r.tokens_in, self.r.again)

    def after(self, what):
        r = self.r
        if what == "block_out":
            self.move(r.act.at[:, 0:D], r.block_output)
        elif what == "grad_norm_one":
            self.move(r.cot, r.grad_tokens)
        elif what == "grad_pre":
            self.move(r.gc, r.gc_out)
            self.move(r.ge, r.ge_out)
        elif what == "grad_output":
            self.move(r.wall.at[12:14], r.gjo_out.at[5:7])
        elif what == "grad_joint":
            self.move(r.wall.at[7:12], r.gjo_out.at[0:5])
            self.move(r.act.at[:, 2 * D + HALF : 3 * D], r.grad_first)

    def finish(self):
        self.move(self.r.gvec, self.r.gvec_out)


def whole_kernel(*refs):
    names = ["tokens_in", "first_in", "cot_in", "wall_in", "wc_in", "vec_in"]
    names += ["block_output", "grad_tokens", "grad_first", "gc_out", "ge_out", "gjo_out", "gvec_out"]
    names += list(STATE) + ["sem"]
    r = Refs(**dict(zip(names, refs)))
    r.again = r.gp.at[:, 0:D]
    compute(r, Whole(r, r.sem))


def units_of(matrix):
    count = matrix.shape[1] // HALF
    return matrix.reshape(2, 2, 2, SLAB, count, HALF).transpose(4, 0, 1, 2, 3, 5)


def matrix_of(units):
    count = units.shape[0]
    return units.transpose(1, 2, 3, 4, 0, 5).reshape(D, count * HALF)


def outside(args):
    (tokens, first_values, cotangent, gain1, shift1, joint, qbias, vbias, output, obias,
     gain2, shift2, expand, ebias, contract, cbias) = args
    gather = functools.partial(lax.all_gather, axis_name=AXES, axis=0, tiled=True)
    scatter = functools.partial(lax.psum_scatter, axis_name=AXES, scatter_dimension=0, tiled=True)
    joint_units = units_of(gather(joint))
    wall = jnp.concatenate(
        [jnp.stack([joint_units[start // HALF] for start in JOINT_COLS]), units_of(gather(output)), units_of(gather(expand))]
    )
    wc = gather(contract).reshape(2, 2, 2, FF // 8, D)
    vec = jnp.stack([gather(v) for v in (gain1, shift1, qbias, vbias, obias, gain2, shift2, cbias)])
    vec = jnp.concatenate([vec, gather(ebias).reshape(4, D), jnp.zeros((4, D), BF)]).astype(F32)
    sds = jax.ShapeDtypeStruct
    block_output, grad_tokens, grad_first, gc, ge, gjo, gvec = pl.pallas_call(
        whole_kernel,
        out_shape=(
            sds((LEN, D), BF), sds((LEN, D), BF), sds((LEN, HALF), BF), sds(wc.shape, BF), sds(wc.shape, BF),
            sds((7,) + wall.shape[1:], BF), sds((GROWS, D), F32),
        ),
        in_specs=[ANY] * 6,
        out_specs=(ANY,) * 7,
        scratch_shapes=[pltpu.VMEM(*item) for item in STATE.values()] + [pltpu.SemaphoreType.DMA],
        compiler_params=pltpu.CompilerParams(vmem_limit_bytes=64 * 2**20),
    )(tokens, first_values, cotangent, wall, wc, vec)
    gc = gc.reshape(FF, D).astype(F32)
    ge = ge.reshape(8, 4, SLAB, 2, HALF).transpose(0, 2, 3, 1, 4).reshape(D, FF).astype(F32)
    order = [JOINT_COLS.index(start * HALF) for start in range(5)]
    gj = jnp.concatenate([matrix_of(gjo[u : u + 1]) for u in order], axis=1).astype(F32)
    go = matrix_of(gjo[5:7]).astype(F32)
    small = [scatter(gvec[i]) for i in (0, 1, 8, 9, 10, 11, 12, 13)]
    return (
        block_output, grad_tokens, grad_first, small[GAIN1], small[SHIFT1], scatter(gj), small[QBIAS], small[VBIAS],
        scatter(go), small[OBIAS], small[GAIN2], small[SHIFT2], scatter(ge), scatter(gvec[G_EBIAS : G_EBIAS + 4].reshape(FF)),
        scatter(gc), small[CBIAS],
    )


class Linked:
    def __init__(self, r, depth):
        self.r, self.depth = r, depth
        wide, self.mz = lax.axis_index("wide"), lax.axis_index("narrow")
        self.my, self.mx, self.mc = wide // 4, (wide // 2) % 2, wide % 2
        self.peer = {
            "c": (wide + 1 - 2 * self.mc, self.mz),
            "x": (wide + 2 - 4 * self.mx, self.mz),
            "y": (wide + 4 - 8 * self.my, self.mz),
            "d": (wide + 4 - 8 * self.my + 2 - 4 * self.mx, self.mz),
        }
        for d in range(1, depth):
            self.peer["z%d" % d] = (wide, lax.rem(self.mz + d, depth))
        self.far = [lax.rem(self.mz + d, depth) for d in range(depth)]
        self.share = SLAB // depth

    def remote(self, source, target, sems, place, where):
        send, recv = sems
        return pltpu.make_async_remote_copy(
            src_ref=source, dst_ref=target, send_sem=send.at[place], recv_sem=recv.at[place],
            device_id=self.peer[where], device_id_type=MESH,
        )

    def weights(self, g):
        if g[0] == "C":
            return self.r.wc, (), pl.ds(C_LANES[g][0], C_LANES[g][1] - C_LANES[g][0])
        a, b, low, high = WEIGHT_SPAN[g]
        return self.r.wall, (pl.ds(a, b - a),), pl.ds(low, high - low)

    def source(self, g):
        r = self.r
        return {"J": (r.wj_in, r.sj), "O": (r.wo_in, r.so), "E": (r.we_in, r.se)}[g[0]] + (WEIGHT_COLS[g],)

    def gather_copies(self, g, step):
        r, y, x, c, both = self.r, self.my, self.mx, self.mc, slice(None)
        ref, lead, lanes = self.weights(g)
        index, late = GROUPS.index(g), g in LATE_Z
        phase = ("z", 1, 2, "c")[step] if not late else (1, 2, "z", "c")[step]
        if phase == "z":
            out = []
            for d in range(1, self.depth):
                if late:
                    view = ref.at[lead + (both, both, c, rows_of(self.mz, SLAB), lanes)]
                    parts = [(view, view)]
                elif g[0] == "C":
                    parts = [(r.wc_in.at[:, lanes], ref.at[lead + (y, x, c, rows_of(self.mz, SLAB), lanes)])]
                else:
                    rows, stage, spans = self.source(g)
                    parts = [(rows.at[:, a:b], stage.at[self.mz, :, a:b]) for a, b in spans]
                for part, (source, target) in enumerate(parts):
                    place = (index, d - 1, part)
                    out.append(self.remote(source, target, (r.gz_send, r.gz_recv), place, "z%d" % d))
            return out
        low, high = (pl.ds(0, FF // 16), pl.ds(FF // 16, FF // 16)) if g[0] == "C" else (
            pl.ds(0, SLAB // 2), pl.ds(SLAB // 2, SLAB // 2))
        if late:
            start = pl.multiple_of(self.mz * SLAB, SLAB)
            low, high = pl.ds(start, SLAB // 2), pl.ds(pl.multiple_of(start + SLAB // 2, SLAB // 2), SLAB // 2)
        if phase == 1:
            plan = [((y, x, c, low), "x", 0), ((y, x, c, high), "y", 1)]
        elif phase == 2:
            plan = [((y, both, c, low), "y", 2), ((both, x, c, high), "x", 3)]
        else:
            plan = [((both, both, c, both), "c", 4)]
        sems = (r.g_send, r.g_recv)
        views = [(ref.at[lead + at + (lanes,)], n, w) for at, w, n in plan]
        return [self.remote(view, view, sems, (index, n), w) for view, n, w in views]

    def assemble(self, g):
        r = self.r
        if g[0] == "C":
            low, high = C_LANES[g]
            r.wc[self.my, self.mx, self.mc, rows_of(self.mz, SLAB), low:high] = r.wc_in[:, low:high]
            return
        source, stage, spans = self.source(g)
        first, _, low, high = WEIGHT_SPAN[g]
        for unit, start in enumerate(s for a, b in spans for s in range(a, b, high - low)):
            stop = start + high - low
            stage[self.mz, :, start:stop] = source[:, start:stop]
            rows = jnp.concatenate([stage[z, :, start:stop].astype(F32) for z in range(self.depth)], axis=0)
            r.wall[first + unit, self.my, self.mx, self.mc, :, low:high] = rows.astype(BF)

    def gather(self, g, step):
        if step > 0:
            for copy in self.gather_copies(g, step - 1):
                copy.wait_recv()
        if step == (0 if g in LATE_Z else 1):
            self.assemble(g)
        if step < 4:
            for copy in self.gather_copies(g, step):
                copy.start()
        else:
            for n in range(4):
                for copy in self.gather_copies(g, n):
                    copy.wait_send()

    def vec_wheres(self, kind):
        return {"c": ["c"], "p": ["x", "y", "d"], "z": ["z%d" % d for d in range(1, self.depth)]}[kind]

    def vec_copies(self, way, step):
        r = self.r
        held, got, kinds = self.vec_ways(way)
        out = []
        for where in self.vec_wheres(kinds[step]):
            n = self.vec_place(where)
            out.append(self.remote(held, got(n), (r.v_send, r.v_recv), (way, n), where))
        return out

    def vec_place(self, where):
        return "cxyd".index(where) if where in "cxyd" else 3 + int(where[1])

    def vec_ways(self, way):
        r = self.r
        if way in (0, 3):
            return r.vsum.at[way // 3], lambda n: r.vgot.at[way // 3, n], "zpc"
        if way == 1:
            return r.gvec.at[8:GROWS, :], lambda n: r.ggot.at[n], "cpz"
        return r.last, lambda n: r.lgot.at[n], "cpz"

    def vec_step(self, way, step):
        r = self.r
        held, got, kinds = self.vec_ways(way)
        if way == 2 and step == 0:
            for row in range(2):
                for side in range(2):
                    r.last[2 * row + side : 2 * row + side + 1, :] = r.gvec[row : row + 1, side * HALF : (side + 1) * HALF]
        if step > 0:
            for copy in self.vec_copies(way, step - 1):
                copy.wait()
            kind = kinds[step - 1]
            total = held[...].astype(F32)
            for where in self.vec_wheres(kind):
                total = total + got(self.vec_place(where))[...].astype(F32)
            if step == 3 and way in (0, 3):
                rows = slice(0, 8) if way == 0 else slice(8, 16)
                r.vec[rows, 0:HALF] = total[0:8]
                r.vec[rows, HALF:D] = total[8:16]
            elif step == 3 and way == 2:
                for row in range(2):
                    for side in range(2):
                        r.gvec[row : row + 1, side * HALF : (side + 1) * HALF] = total[2 * row + side : 2 * row + side + 1]
            else:
                held[...] = total.astype(held.dtype)
        if step < 3:
            for copy in self.vec_copies(way, step):
                copy.start()

    def grads(self, g):
        r = self.r
        if g[0] in "CE":
            low, high = C_LANES[g] if g[0] == "C" else (int(g[1]) * HALF, int(g[1]) * HALF + HALF)
            return [(r.gc if g[0] == "C" else r.ge, (), 0, low)], FF // 8, (low, high)
        a, b, low, high = GRAD_SPAN[g]
        units = [(r.wall, (u,), (u - 7) % 4 * SLAB, (u - 7) // 4 * HALF + low) for u in range(a, b)]
        return units, SLAB, (low, high)

    def slices(self, g, height, rows_at, lanes_at, wide):
        r = self.r
        if g in LATE_Z:
            start, half = pl.multiple_of(self.mz * SLAB, SLAB), SLAB // 2
            low, high = pl.ds(start, half), pl.ds(pl.multiple_of(start + half, half), half)
            return low, high, pl.ds(0, half), pl.ds(0, wide), r.late_one, r.late_two
        half = height // 2
        return pl.ds(0, half), pl.ds(half, half), pl.ds(rows_at // 2, half), pl.ds(lanes_at, wide), r.near_one, r.near_two

    def scatter_copies(self, g, step):
        units, height, (left, right) = self.grads(g)
        r, index, late = self.r, SUMS.index(g), g in LATE_Z
        y, x, c, both = self.my, self.mx, self.mc, slice(None)
        lanes = pl.ds(left, right - left)
        phase = ("c", 1, 2, "z")[step] if not late else ("c", "z", 1, 2)[step]
        out = []
        if phase == "z":
            for d in range(1, self.depth):
                far = self.far[d]
                ref = units[0][0]
                if late:
                    parts = [(ref.at[both, both, c, rows_of(far, SLAB), lanes], r.late.at[d - 1])]
                elif g[0] == "C":
                    parts = [(ref.at[y, x, c, rows_of(far, SLAB), lanes], r.zc.at[d - 1])]
                else:
                    stage, got, spans = self.stage(g)
                    parts = [(stage.at[far, :, a:b], got.at[d - 1, :, a:b]) for a, b in spans]
                for part, (source, target) in enumerate(parts):
                    out.append(self.remote(source, target, (r.sz_send, r.sz_recv), (index, d - 1, part), "z%d" % d))
            return out
        for part, (ref, lead, rows_at, lanes_at) in enumerate(units):
            low, high, near, near_lanes, one, two = self.slices(g, height, rows_at, lanes_at, right - left)
            if phase == "c":
                target = r.core.at[:, :, pl.ds(rows_at, height), pl.ds(lanes_at, right - left)]
                plan = [((both, both, 1 - c, both), target, "c", 0)]
            elif phase == 1:
                plan = [
                    ((both, 1 - x, c, low), one.at[0, :, near, near_lanes], "x", 1),
                    ((1 - y, both, c, high), one.at[1, :, near, near_lanes], "y", 2),
                ]
            else:
                plan = [
                    ((1 - y, x, c, low), two.at[0, near, near_lanes], "y", 3),
                    ((y, 1 - x, c, high), two.at[1, near, near_lanes], "x", 4),
                ]
            for at, target, where, n in plan:
                out.append(self.remote(ref.at[lead + at + (lanes,)], target, (r.s_send, r.s_recv), (index, n, part), where))
        return out

    def stage(self, g):
        r = self.r
        stage, got = {"J": (r.sj, r.zj), "O": (r.so, r.zo), "E": (r.se, r.ze)}[g[0]]
        return stage, got, GRAD_COLS[g]

    def add_up(self, g, phase):
        r, y, x, c = self.r, self.my, self.mx, self.mc
        units, height, (left, right) = self.grads(g)
        late, lanes = g in LATE_Z, pl.ds(left, right - left)
        if phase == 2 and g[0] != "C":
            stage, _, spans = self.stage(g)
            places = iter([(s, s + right - left) for a, b in spans for s in range(a, b, right - left)])
        for ref, lead, rows_at, lanes_at in units:
            low, high, near, near_lanes, one, two = self.slices(g, height, rows_at, lanes_at, right - left)

            def add(at, *got, ref=ref, lead=lead):
                at = lead + at + (lanes,)
                if len(got) == 1:
                    ref[at] = ref[at] + got[0]
                    return
                total = ref[at].astype(F32)
                for item in got:
                    total = total + item.astype(F32)
                ref[at] = total.astype(BF)

            if phase == "c":
                def step(i, rows_at=rows_at, lanes_at=lanes_at, add=add):
                    got = r.core[i // 2, i % 2, pl.ds(rows_at, height), pl.ds(lanes_at, right - left)]
                    add((i // 2, i % 2, c, slice(None)), got)

                loop(4, step)
            elif phase == "z":
                def step(i, add=add):
                    got = [r.late[d, i // 2, i % 2] for d in range(self.depth - 1)]
                    add((i // 2, i % 2, c, rows_of(self.mz, SLAB)), *got)

                loop(4, step)
            elif phase == 1:
                def step(i, add=add, low=low, high=high, near=near, near_lanes=near_lanes, one=one):
                    add((i, x, c, low), one[0, i, near, near_lanes])
                    add((y, i, c, high), one[1, i, near, near_lanes])

                loop(2, step)
            elif g[0] == "C" and not late:
                add((y, x, c, low), two[0, near, near_lanes])
                add((y, x, c, high), two[1, near, near_lanes])
            else:
                final = [
                    ref[lead + (y, x, c, half, lanes)].astype(F32) + two[part, near, near_lanes].astype(F32)
                    for part, half in enumerate((low, high))
                ]
                if late:
                    r.gc_out[0 : SLAB // 2, left:right] = final[0]
                    r.gc_out[SLAB // 2 : SLAB, left:right] = final[1]
                    continue
                final = jnp.concatenate(final, axis=0)
                for s in range(0, height, SLAB):
                    start, stop = next(places)
                    for z in range(self.depth):
                        rows = final[s + z * self.share : s + (z + 1) * self.share]
                        stage[z, :, start:stop] = rows.astype(BF)

    def put_out(self, g):
        r = self.r
        if g[0] == "C":
            left, right = C_LANES[g]
            total = r.gc[self.my, self.mx, self.mc, rows_of(self.mz, SLAB), left:right].astype(F32)
            for d in range(self.depth - 1):
                total = total + r.zc[d].astype(F32)
            r.gc_out[:, left:right] = total
            return
        stage, got, spans = self.stage(g)
        out = {"J": r.gj_out, "O": r.go_out, "E": r.ge_out}[g[0]]
        for a, b in spans:
            total = stage[self.mz, :, a:b].astype(F32)
            for d in range(self.depth - 1):
                total = total + got[d, :, a:b].astype(F32)
            out[:, a:b] = total

    def scatter(self, g, step):
        r, late = self.r, g in LATE_Z
        phases = ("c", "z", 1, 2) if late else ("c", 1, 2, "z")
        if step > 0:
            for copy in self.scatter_copies(g, step - 1):
                copy.wait_recv()
            if phases[step - 1] == "z" and not late:
                self.put_out(g)
            else:
                self.add_up(g, phases[step - 1])
        turns = {"c": [(0, "c")], 1: [(1, "x"), (2, "y")], 2: [(3, "y"), (4, "x")], "z": []}
        own = {"c": turns["c"]} if late else turns
        if g in OWNERS and step > 0:
            for n, where in own.get(phases[step - 1], []):
                pl.semaphore_signal(
                    r.free_sem.at[n, OWNERS.index(g)], inc=1, device_id=self.peer[where], device_id_type=MESH
                )
        if step < 4:
            for before in {"E0": ("C0",), "E1": ("C1",), "O0": ("E0", "E1")}.get(g, ()):
                for n, _ in turns[phases[step]]:
                    if before not in LATE_Z or n == 0:
                        pl.semaphore_wait(r.free_sem.at[n, OWNERS.index(before)], 1)
            for copy in self.scatter_copies(g, step):
                copy.start()
        else:
            for n in range(4):
                for copy in self.scatter_copies(g, n):
                    copy.wait_send()
            for copy in self.leaving(g):
                copy.start()

    def leaving(self, g):
        r = self.r
        source, target = {"J": (r.gj_out, r.gj_to), "O": (r.go_out, r.go_to), "E": (r.ge_out, r.ge_to), "C": (r.gc_out, r.gc_to)}[g[0]]
        spans = [C_LANES[g]] if g[0] == "C" else GRAD_COLS[g]
        return [
            pltpu.make_async_copy(source.at[:, a:b], target.at[:, a:b], r.out_sem.at[SUMS.index(g), n])
            for n, (a, b) in enumerate(spans)
        ]

    def run(self, words):
        for word in words:
            name, step = word.split(".")
            step = int(step)
            if name[0] == "v":
                self.vec_step(int(name[1]), step)
            elif name[0] == "g":
                self.gather(name[1:], step)
            elif name[0] == "s":
                self.scatter(name[1:], step)
            elif step < 10:
                self.local(step).wait()
            else:
                self.local(step - 10).start()

    def local(self, n):
        r = self.r
        source, target = (
            (r.tokens_in, r.tokens),
            (r.first_in, r.v.at[:, HALF:D]),
            (r.cot_in, r.cot),
            (r.tokens_in, r.again),
            (r.act.at[:, 2 * D + HALF : 3 * D], r.grad_first),
            (r.act.at[:, 0:D], r.block_output),
            (r.cot, r.grad_tokens),
            (r.wj_from, r.wj_in), (r.wo_from, r.wo_in), (r.we_from, r.we_in), (r.wc_from, r.wc_in),
        )[n]
        return pltpu.make_async_copy(source, target, r.local_sem.at[n])

    def place_vectors(self):
        r, share = self.r, self.share
        me = lax.axis_index("wide") * self.depth + self.mz
        r.vec[...] = jnp.zeros_like(r.vec)
        for n in range(8):
            r.vec[n, 0:share] = getattr(r, "vec%d" % n)[...].astype(F32)
        r.vec[8, 0 : 4 * share] = r.vec8[...].astype(F32)
        placed = pltpu.roll(r.vec[0:8, :], me * share, 1)
        r.vsum[0] = jnp.concatenate([placed[:, :HALF], placed[:, HALF:]], axis=0).astype(BF)
        start = me * 4 * share
        wide_bias = pltpu.roll(r.vec[8:VROWS, :], lax.rem(start, D), 1)[0:1]
        rows = lax.broadcasted_iota(jnp.int32, (VROWS - 8, D), 0) == start // D
        placed = jnp.where(rows, wide_bias, 0.0)
        r.vsum[1] = jnp.concatenate([placed[:, :HALF], placed[:, HALF:]], axis=0).astype(BF)

    def start(self):
        r = self.r
        barrier = pltpu.get_barrier_semaphore()
        for where in self.peer:
            pl.semaphore_signal(barrier, inc=1, device_id=self.peer[where], device_id_type=MESH)
        for n in (7, 8, 9, 10, 0, 2, 1):
            self.local(n).start()
        self.place_vectors()
        for n in (7, 8, 9, 10):
            self.local(n).wait()
        pl.semaphore_wait(barrier, len(self.peer))
        self.run(PLAN["start"])

    def before(self, what):
        self.run(PLAN.get("before " + what, ()))

    def after(self, what):
        self.run(PLAN.get("after " + what, ()))

    def tick(self, what, i):
        for n in range(8):
            words = PLAN.get("%s %d" % (what, n), ())
            if words:
                @pl.when(i == n)
                def _(words=words):
                    self.run(words)

    def finish(self):
        self.run(PLAN["finish"])
        for g in SUMS:
            for copy in self.leaving(g):
                copy.wait()


WEIGHT_SPAN = dict(
    J0=(0, 3, 0, 128), J1=(0, 3, 128, 384), J2=(3, 5, 0, 384), O0=(5, 7, 0, 384),
    E0=(7, 9, 0, 384), E1=(9, 11, 0, 384), E2=(11, 13, 0, 384), E3=(13, 15, 0, 384),
)
WEIGHT_COLS = dict(
    J0=[(c, c + 128) for c in JOINT_COLS[0:3]], J1=[(c + 128, c + HALF) for c in JOINT_COLS[0:3]],
    J2=[(c, c + HALF) for c in JOINT_COLS[3:5]], O0=[(0, D)],
    E0=[(0, D)], E1=[(D, 2 * D)], E2=[(2 * D, 3 * D)], E3=[(3 * D, 4 * D)],
)
GROUPS = tuple(WEIGHT_SPAN) + ("C0", "C1")
GRAD_SPAN = dict(J0=(7, 10, 0, 384), J1=(10, 12, 0, 256), J2=(10, 12, 256, 384), O0=(12, 14, 0, 384))
GRAD_COLS = dict(
    J0=[(c, c + HALF) for c in JOINT_COLS[0:3]], J1=[(c, c + 256) for c in JOINT_COLS[3:5]],
    J2=[(c + 256, c + HALF) for c in JOINT_COLS[3:5]], O0=[(0, D)], E0=[(0, 2 * D)], E1=[(2 * D, 4 * D)],
)
SUMS = ("C0", "C1", "E0", "E1") + tuple(GRAD_SPAN)
C_LANES = dict(C0=(0, 512), C1=(512, 768))
OWNERS = ("C0", "C1", "E0", "E1")
LATE_Z = ("C1",)
PLAN = {
    "start": ("gJ0.0", "v0.0", "gC1.0", "gJ1.0", "gJ0.1", "gC1.1", "v0.1", "local.0", "gO0.0", "gJ1.1", "gE1.0",),
    "before contract_bias": ("v0.2", "gJ0.2", "gJ2.0", "v0.3", "local.2", "gO0.1",),
    "after contract_bias": ("gE0.0", "gJ1.2",),
    "before norm_one": ("gJ0.3", "gO0.2",),
    "after norm_one": ("gJ2.1", "gE1.1", "gE3.0",),
    "before project_a": ("gJ0.4",),
    "before attend": ("gE0.1", "v3.0", "gJ1.3", "gE2.0",),
    "attend 0": ("gC0.0", "gO0.3", "gJ2.2",),
    "before project_b": ("gJ1.4",),
    "attend_m 1": ("gE1.2",),
    "attend_m 2": ("gE3.1",),
    "attend 2": ("gE0.2",),
    "before project_c": ("gJ2.3", "v3.1", "gJ2.4", "local.1",),
    "attend_m 3": ("gC1.2", "gO0.4", "gE3.2",),
    "attend 3": ("gE2.1", "gE1.3",),
    "attend_m 4": ("gC0.1", "gE0.3",),
    "attend_m 5": ("v3.2",),
    "attend 5": ("gE0.4",),
    "after attend": ("gE3.3",),
    "after out_project": ("gE2.2",),
    "before expand": ("v3.3", "gE3.4",),
    "expand_b 0": ("gC0.2", "gE1.4",),
    "expand_b 1": ("gE2.3",),
    "expand_a 2": ("gE2.4",),
    "expand_b 2": ("gC1.3",),
    "expand_b 3": ("gC0.3",),
    "expand_c 3": ("sC1.0", "gC1.4",),
    "after expand": ("sC0.0", "gC0.4",),
    "block_out 2": ("sC0.1",),
    "after block_out": ("local.15",),
    "grad_pre 2": ("sE0.0",),
    "grad_expand 2": ("sC0.2",),
    "grad_pre 3": ("sC1.1",),
    "grad_expand 3": ("sE0.1",),
    "grad_norm_two 1": ("sE1.0",),
    "after grad_norm_two": ("local.13", "sE1.1",),
    "after grad_output": ("sC0.3",),
    "before attend_back": ("sO0.0", "local.5",),
    "back_m 0": ("sE0.2",),
    "back_m 1": ("sE1.2",),
    "attend_back 2": ("sO0.1", "sJ0.0", "sE1.3",),
    "back_m 3": ("sE0.3", "sJ0.1",),
    "back_m 4": ("sO0.2",),
    "attend_back 4": ("sJ1.0", "sJ0.2",),
    "back_m 5": ("sJ1.1", "sO0.3",),
    "after attend_back": ("local.14",),
    "before grad_joint": ("v1.0",),
    "after grad_joint": ("sJ0.3", "v1.1",),
    "before grad_norm_one": ("local.3", "sJ2.0", "local.4",),
    "grad_norm_one 1": ("sJ1.2", "sJ2.1", "v1.2",),
    "grad_norm_one 3": ("sE0.4", "sJ2.2", "sJ1.3",),
    "after grad_norm_one": ("sC1.2", "v2.0", "v2.1", "local.16", "sJ2.3", "sC1.3",),
    "finish": ("v1.3", "sC0.4", "sJ0.4", "sE1.4", "v2.2", "sC1.4", "sO0.4", "sJ2.4", "sJ1.4", "local.6", "v2.3",),
}


def linked_scratch(depth):
    share = SLAB // depth
    far = max(depth - 1, 1)
    dma = pltpu.SemaphoreType.DMA
    return dict(
        wj_in=pltpu.VMEM((share, 2 * D + HALF), BF), wo_in=pltpu.VMEM((share, D), BF),
        we_in=pltpu.VMEM((share, FF), BF), wc_in=pltpu.VMEM((SLAB, D), BF),
        gj_out=pltpu.VMEM((share, 2 * D + HALF), F32), go_out=pltpu.VMEM((share, D), F32),
        ge_out=pltpu.VMEM((share, FF), F32), gc_out=pltpu.VMEM((SLAB, D), F32),
        sj=pltpu.VMEM((depth, share, 2 * D + HALF), BF),
        so=pltpu.VMEM((depth, share, D), BF),
        se=pltpu.VMEM((depth, share, FF), BF),
        zj=pltpu.VMEM((far, share, 2 * D + HALF), BF),
        zo=pltpu.VMEM((far, share, D), BF),
        ze=pltpu.VMEM((far, share, FF), BF),
        zc=pltpu.VMEM((far, SLAB, C_LANES["C0"][1]), BF),
        late=pltpu.VMEM((far, 2, 2, SLAB, D - C_LANES["C1"][0]), BF),
        late_one=pltpu.VMEM((2, 2, SLAB // 2, D - C_LANES["C1"][0]), BF),
        late_two=pltpu.VMEM((2, SLAB // 2, D - C_LANES["C1"][0]), BF),
        core=pltpu.VMEM((2, 2, FF // 8, D), BF),
        near_one=pltpu.VMEM((2, 2, FF // 16, D), BF),
        near_two=pltpu.VMEM((2, FF // 16, D), BF),
        vsum=pltpu.VMEM((2, 16, HALF), BF),
        vgot=pltpu.VMEM((2, 3 + depth, 16, HALF), BF),
        ggot=pltpu.VMEM((3 + depth, GROWS - 8, D), F32),
        last=pltpu.VMEM((8, HALF), F32),
        lgot=pltpu.VMEM((3 + depth, 8, HALF), F32),
        gz_send=dma((10, far, 3)), gz_recv=dma((10, far, 3)), g_send=dma((10, 5)), g_recv=dma((10, 5)),
        sz_send=dma((8, far, 3)), sz_recv=dma((8, far, 3)), s_send=dma((8, 5, 3)), s_recv=dma((8, 5, 3)),
        v_send=dma((4, 3 + depth)), v_recv=dma((4, 3 + depth)), local_sem=dma((11,)), out_sem=dma((8, 3)),
        free_sem=pltpu.SemaphoreType.REGULAR((5, 4)),
    )


def linked_kernel(depth, *refs):
    names = ["tokens_in", "first_in", "cot_in", "wj_from", "wo_from", "we_from", "wc_from"]
    names += ["vec%d" % n for n in range(9)]
    names += ["gvec_out", "block_output", "grad_tokens", "grad_first", "gj_to", "go_to", "ge_to", "gc_to"]
    names += list(STATE) + list(linked_scratch(depth))
    r = Refs(**dict(zip(names, refs)))
    r.again = r.gp.at[:, 0:D]
    compute(r, Linked(r, depth))
    r.gvec_out[...] = r.gvec[...]


def closing_kernel(depth, *refs):
    gvec, moved, targets, vectors, sem = refs[0], refs[1:8], refs[8:15], refs[15:24], refs[24]
    passing = refs[25:32]
    arrive = [pltpu.make_async_copy(a, b, sem.at[0, n]) for n, (a, b) in enumerate(zip(moved, passing))]
    leave = [pltpu.make_async_copy(a, b, sem.at[1, n]) for n, (a, b) in enumerate(zip(passing, targets))]
    for copy in arrive:
        copy.start()
    me = lax.axis_index("wide") * depth + lax.axis_index("narrow")
    share = SLAB // depth
    small = pltpu.roll(gvec[0:G_EBIAS, :], lax.rem(D - me * share, D), 1)
    start = me * 4 * share
    rows = lax.broadcasted_iota(jnp.int32, (4, D), 0) == start // D
    wide_bias = jnp.sum(jnp.where(rows, gvec[G_EBIAS : G_EBIAS + 4, :], 0.0), axis=0, keepdims=True)
    wide_bias = pltpu.roll(jnp.broadcast_to(wide_bias, (8, D)), lax.rem(D - lax.rem(start, D), D), 1)
    for n, row in enumerate((G_GAIN1, G_SHIFT1, G_QBIAS, G_VBIAS, G_OBIAS, G_GAIN2, G_SHIFT2, G_CBIAS)):
        vectors[n][...] = small[row, 0:share]
    vectors[8][...] = wide_bias[0, 0 : 4 * share]
    for first, second in zip(arrive, leave):
        first.wait()
        second.start()
    for copy in leave:
        copy.wait()


def linked(depth, args):
    (tokens, first_values, cotangent, gain1, shift1, joint, qbias, vbias, output, obias,
     gain2, shift2, expand, ebias, contract, cbias) = args
    share = SLAB // depth
    sds = jax.ShapeDtypeStruct
    results = pl.pallas_call(
        functools.partial(linked_kernel, depth),
        out_shape=(
            sds((GROWS, D), F32), sds((LEN, D), BF), sds((LEN, D), BF), sds((LEN, HALF), BF), sds(joint.shape, F32),
            sds(output.shape, F32), sds(expand.shape, F32), sds(contract.shape, F32),
        ),
        in_specs=[ANY] * 7 + [VMEM] * 9,
        out_specs=(VMEM,) + (ANY,) * 7,
        scratch_shapes=[pltpu.VMEM(*item) for item in STATE.values()] + list(linked_scratch(depth).values()),
        compiler_params=pltpu.CompilerParams(
            vmem_limit_bytes=64 * 2**20, collective_id=0, has_side_effects=True
        ),
    )(tokens, first_values, cotangent, joint, output, expand, contract,
      gain1, shift1, qbias, vbias, obias, gain2, shift2, cbias, ebias)
    vectors = (sds((share,), F32),) * 8 + (sds((4 * share,), F32),)
    closed = pl.pallas_call(
        functools.partial(closing_kernel, depth),
        out_shape=tuple(sds(item.shape, item.dtype) for item in results[1:]) + vectors,
        in_specs=[VMEM] + [ANY] * 7,
        out_specs=(ANY,) * 7 + (VMEM,) * 9,
        scratch_shapes=[pltpu.SemaphoreType.DMA((2, 7))] + [pltpu.VMEM(item.shape, item.dtype) for item in results[1:]],
    )(*results)
    block_output, grad_tokens, grad_first, gj, go, ge, gc = closed[:7]
    gain1, shift1, qbias, vbias, obias, gain2, shift2, cbias, ebias = closed[7:]
    return (
        block_output, grad_tokens, grad_first, gain1, shift1, gj, qbias, vbias, go, obias, gain2, shift2, ge, ebias, gc, cbias
    )


def solution(mesh):
    split, flat = P(AXES, None), P(AXES)
    wide, depth = mesh.shape["wide"], mesh.shape["narrow"]
    if wide == 8 and SLAB % (8 * depth) == 0:
        body = lambda *args: linked(depth, args)
    else:
        body = lambda *args: outside(args)
    return jax.shard_map(
        body,
        mesh=mesh,
        in_specs=(split, split, split, flat, flat, split, flat, flat, split, flat, flat, flat, split, flat, split, flat),
        out_specs=(split, split, split, flat, flat, split, flat, flat, split, flat, flat, flat, split, flat, split, flat),
        check_vma=False,
    )
```

```python
import functools

import jax
import jax.numpy as jnp
from jax import lax
from jax.experimental import pallas as pl
from jax.experimental.pallas import tpu as pltpu
from jax.sharding import PartitionSpec as P

D = 768
HEAD = 64
FF = 3072
LEN = 1024
HALF = D // 2
SLAB = D // 8
PAIRS = D // (2 * HEAD)
QB = LEN // 4
EPS = 1e-05
BF = jnp.bfloat16
F32 = jnp.float32
MESH = pl.DeviceIdType.MESH
AXES = ("wide", "narrow")

UNITS = 15
JOINT_COLS = (0, 768, 1536, 384, 1152)
GAIN1, SHIFT1, QBIAS, VBIAS, OBIAS, GAIN2, SHIFT2, CBIAS, EBIAS = range(9)
VROWS = 16
G_GAIN1, G_SHIFT1 = 0, 1
G_QBIAS, G_VBIAS, G_OBIAS, G_GAIN2, G_SHIFT2, G_CBIAS = range(8, 14)
G_EBIAS = 16
GROWS = 24


def dot(left, right, left_dim=1, right_dim=0):
    return lax.dot_general(left, right, (((left_dim,), (right_dim,)), ((), ())), preferred_element_type=F32)


def loop(count, step):
    lax.fori_loop(0, count, lambda i, c: (step(i), c)[1], 0)


def loop_in_pairs(count, step):
    loop(count // 2, lambda i: (step(2 * i), step(2 * i + 1)))


def sum_in_pairs(count, step, start, after):
    def pair(i, sums):
        sums = step(2 * i + 1, step(2 * i, sums))
        after(2 * i + 1)
        return sums

    return lax.fori_loop(0, count // 2, pair, start)


def rows_of(index, size):
    return pl.ds(pl.multiple_of(index * size, size), size)


def norm_parts(values):
    center = values - jnp.mean(values, axis=-1, keepdims=True)
    inv = lax.rsqrt(jnp.mean(center * center, axis=-1, keepdims=True) + EPS)
    return center * inv, inv


def norm_back(values, grad, gain):
    unit, inv = norm_parts(values)
    scaled = grad * gain
    mean_one = jnp.mean(scaled, axis=-1, keepdims=True)
    mean_two = jnp.mean(scaled * unit, axis=-1, keepdims=True)
    grad_in = inv * (scaled - mean_one - unit * mean_two)
    return grad_in, jnp.sum(grad * unit, axis=0, keepdims=True), jnp.sum(grad, axis=0, keepdims=True)


class Nothing:
    def __getattr__(self, name):
        return lambda *a, **k: None


def two_units(ref, unit):
    return jnp.concatenate([ref[unit].reshape(D, HALF), ref[unit + 1].reshape(D, HALF)], axis=1)


def stages(r, comm):
    vec = r.vec

    def vrow(i):
        return vec[i : i + 1, :]

    order = []

    def stage(function):
        order.append(function)
        return function


    def norm_one(i):
        rows = rows_of(i, 128)
        unit, _ = norm_parts(r.tokens[rows, :].astype(F32))
        r.h1[rows, :] = (unit * vrow(GAIN1) + vrow(SHIFT1)).astype(BF)

    def column_sum(i, total):
        return total + jnp.sum(r.cot[rows_of(i, 128), :].astype(F32), axis=0, keepdims=True)

    @stage
    def run_contract_bias():
        r.gvec[...] = jnp.zeros_like(r.gvec)
        r.gvec[G_CBIAS : G_CBIAS + 1, :] = lax.fori_loop(0, LEN // 128, column_sum, jnp.zeros((1, D), F32))

    @stage
    def run_norm_one():
        loop_in_pairs(LEN // 128, norm_one)

    def project(low, high):
        def step(i):
            rows = rows_of(i, 512)
            weights = jnp.concatenate([r.wall[u, :, :, :, :, low:high].reshape(D, high - low) for u in (0, 1, 2)], axis=1)
            q, k, v = jnp.split(dot(r.h1[rows, :], weights), 3, axis=1)
            q = (q + vec[QBIAS : QBIAS + 1, low:high]).astype(BF)
            r.q[rows, low:high] = (q * HEAD ** (-0.5)).astype(BF)
            r.k[rows, low:high] = k.astype(BF)
            r.v[rows, low:high] = (v + vec[VBIAS : VBIAS + 1, low:high]).astype(BF)

        loop(LEN // 512, step)

    @stage
    def run_project_a():
        project(0, 128)

    def project_b():
        project(128, HALF)

    def project_c(i):
        rows = rows_of(i, 512)
        out = dot(r.h1[rows, :], two_units(r.wall, 3))
        r.q[rows, HALF:D] = ((out[:, 0:HALF] + vec[QBIAS : QBIAS + 1, HALF:D]).astype(BF) * HEAD ** (-0.5)).astype(BF)
        r.k[rows, HALF:D] = out[:, HALF:D].astype(BF)
        r.v[rows, HALF:D] = (r.v[rows, HALF:D].astype(F32) + vec[VBIAS : VBIAS + 1, HALF:D]).astype(BF)

    first_lanes = lax.broadcasted_iota(jnp.int32, (QB, 128), 1) < HEAD
    lane_row = lax.broadcasted_iota(jnp.int32, (1, 128), 1)
    head_mask = [(lane_row < HEAD).astype(F32).astype(BF), (lane_row >= HEAD).astype(F32).astype(BF)]
    seen = lax.broadcasted_iota(jnp.int32, (QB, QB), 0) <= lax.broadcasted_iota(jnp.int32, (QB, QB), 1)
    seen = jnp.concatenate([seen, seen], axis=1)

    def both_heads(rows):
        return jnp.concatenate([rows * head_mask[0], rows * head_mask[1]], axis=0)

    def attend(pair):
        cols = rows_of(pair, 128)
        turned = jnp.transpose(r.v[:, cols])
        ones = jnp.ones((HEAD, LEN), BF)
        values = [jnp.concatenate([turned[:HEAD], ones], axis=0), jnp.concatenate([ones, turned[HEAD:]], axis=0)]
        for block in (3, 2, 1, 0):
            if block == 2:
                comm.tick("attend_m", pair)
            first, finish = block * QB, (block + 1) * QB
            scores = dot(r.k[0:finish, cols], both_heads(r.q[first:finish, cols]), 1, 1)
            diag = jnp.where(seen, scores[first:finish], -jnp.inf)
            scores = diag if block == 0 else jnp.concatenate([scores[:first], diag], axis=0)
            peak = jnp.max(scores, axis=0, keepdims=True)
            raised = jnp.exp(scores - peak).astype(BF)
            parts = []
            for h in range(2):
                out = dot(values[h][:, 0:finish], raised[:, h * QB : (h + 1) * QB])
                total = out[HEAD : HEAD + 1] if h == 0 else out[0:1]
                parts.append(out[h * HEAD : (h + 1) * HEAD] * (1.0 / total))
                r.logs[pair, h : h + 1, first:finish] = peak[:, h * QB : (h + 1) * QB] + jnp.log(total)
            r.mixed[cols, first:finish] = jnp.concatenate(parts, axis=0).astype(BF)

    @stage
    def run_attend():
        def step(i):
            @pl.when(i == 1)
            def _():
                comm.before("project_b")
                project_b()

            @pl.when(i == PAIRS // 2)
            def _():
                comm.before("project_c")
                loop(LEN // 512, project_c)

            attend(i)
            comm.tick("attend", i)

        loop(PAIRS, step)

    def out_project(i):
        rows = rows_of(i, 256)
        resid = r.tokens[rows, :].astype(F32) + dot(r.mixed[:, rows], two_units(r.wall, 5), 0, 0) + vrow(OBIAS)
        r.resid[rows, :] = resid
        unit, _ = norm_parts(resid)
        r.tokens[rows, :] = (unit * vrow(GAIN2) + vrow(SHIFT2)).astype(BF)

    @stage
    def run_out_project():
        loop(LEN // 256, out_project)
    h2 = r.tokens

    alpha = 0.7978845608028654
    beta = alpha * 0.044715

    def expand(j):
        comm.tick("expand_a", j)
        cols = rows_of(j, D)
        bias = vec[pl.ds(EBIAS + j, 1), :]

        def step(i):
            rows = rows_of(i, 256)
            pre = dot(h2[rows, :], two_units(r.wall, 7 + 2 * j)) + bias
            square = pre * pre
            bent = jnp.tanh(pre * (alpha + beta * square))
            half = 0.5 * bent + 0.5
            slope = half + (pre * (0.5 - 0.5 * bent * bent)) * (alpha + (3.0 * beta) * square)
            r.act[rows, cols] = (pre * half).astype(BF)
            r.gp[rows, cols] = slope.astype(BF)

        loop_in_pairs(LEN // 256, step)
        comm.tick("expand_b", j)
        r.gc[j // 2, j % 2] = dot(r.act[:, cols], r.cot[...], 0, 0).astype(BF).reshape(2, FF // 8, D)
        comm.tick("expand_c", j)

    @stage
    def run_expand():
        loop(4, expand)

    def block_out(i):
        rows = rows_of(i, 256)
        out = r.resid[rows, :] + dot(r.act[rows, :], r.wc[...].reshape(FF, D)) + vrow(CBIAS)
        r.act[rows, 0:D] = out.astype(BF)
        comm.tick("block_out", i)

    @stage
    def run_block_out():
        loop(LEN // 256, block_out)

    def grad_pre(j):
        cols = rows_of(j, D)

        def step(i, sums):
            rows = rows_of(i, 512)
            grad = dot(r.cot[rows, :], r.wc[j // 2, j % 2].reshape(D, D), 1, 1) * r.gp[rows, cols].astype(F32)
            grad = grad.astype(BF)
            r.gp[rows, cols] = grad
            return sums + jnp.sum(grad.astype(F32), axis=0, keepdims=True)

        r.gvec[pl.ds(G_EBIAS + j, 1), :] = step(1, step(0, jnp.zeros((1, D), F32)))
        comm.tick("grad_pre", j)
        grad = dot(h2[...], r.gp[:, cols], 0, 0).astype(BF)
        for side in range(2):
            part = grad[:, side * HALF : (side + 1) * HALF].reshape(2, 2, 2, SLAB, HALF)
            r.ge[:, :, :, rows_of(2 * (j % 2) + side, SLAB), pl.ds(pl.multiple_of(j // 2 * HALF, HALF), HALF)] = part
        comm.tick("grad_expand", j)

    @stage
    def run_grad_pre():
        loop(4, grad_pre)

    def grad_norm_two(i, sums):
        rows = rows_of(i, 256)
        weights = jnp.concatenate([r.wall[u].reshape(D, HALF) for u in range(7, 15)], axis=1)
        grad_in, gain, shift = norm_back(r.resid[rows, :], dot(r.gp[rows, :], weights, 1, 1), vrow(GAIN2))
        grad = r.cot[rows, :].astype(F32) + grad_in
        low = grad.astype(BF)
        r.resid[rows, :] = grad
        r.tokens[rows, :] = low
        return sums[0] + gain, sums[1] + shift, sums[2] + jnp.sum(low.astype(F32), axis=0, keepdims=True)

    @stage
    def run_grad_norm_two():
        zero = jnp.zeros((1, D), F32)
        gain, shift, obias = sum_in_pairs(LEN // 256, grad_norm_two, (zero, zero, zero), functools.partial(comm.tick, "grad_norm_two"))
        r.gvec[G_GAIN2 : G_GAIN2 + 1, :] = gain
        r.gvec[G_SHIFT2 : G_SHIFT2 + 1, :] = shift
        r.gvec[G_OBIAS : G_OBIAS + 1, :] = obias
    gattn = r.tokens

    def grad_output(i):
        grad = dot(r.mixed[rows_of(i, HALF), :], gattn[...]).astype(BF)
        for side in range(2):
            r.wall[12 + side, i] = grad[:, side * HALF : (side + 1) * HALF].reshape(2, 2, SLAB, HALF)

    @stage
    def run_grad_output():
        loop_in_pairs(2, grad_output)

    def grad_mixed(i):
        rows = rows_of(i, 512)
        grad = dot(gattn[rows, :], two_units(r.wall, 5), 1, 1).astype(BF)
        r.cot[rows, :] = grad

    @stage
    def run_grad_mixed():
        loop_in_pairs(LEN // 512, grad_mixed)

    def attend_back(pair):
        cols = rows_of(pair, 128)
        qsum = jnp.zeros((1, 128), F32)
        for block in (3, 2, 1, 0):
            if block == 2:
                comm.tick("back_m", pair)
            first, finish = block * QB, (block + 1) * QB
            kp = r.k[0:finish, cols]
            gm = r.cot[first:finish, cols]
            qm, gh = both_heads(r.q[first:finish, cols]), both_heads(gm)
            inner = jnp.transpose(gm).astype(F32) * r.mixed[cols, first:finish].astype(F32)
            inner = [jnp.sum(inner[h * HEAD : (h + 1) * HEAD], axis=0, keepdims=True) for h in range(2)]
            log_total = jnp.concatenate([r.logs[pair, h : h + 1, first:finish] for h in range(2)], axis=1)
            probs = jnp.exp(dot(kp, qm, 1, 1) - log_total)
            diag = jnp.where(seen, probs[first:finish], 0.0)
            probs = diag if block == 0 else jnp.concatenate([probs[:first], diag], axis=0)
            grad_probs = dot(r.v[0:finish, cols], gh, 1, 1)
            grad_scores = (probs * (grad_probs - jnp.concatenate(inner, axis=1))).astype(BF)
            gq = dot(grad_scores, kp, 0, 0)
            gq = (jnp.where(first_lanes, gq[:QB], gq[QB:]) * HEAD ** (-0.5)).astype(BF)
            r.act[first:finish, cols] = gq
            qsum = qsum + jnp.sum(gq.astype(F32), axis=0, keepdims=True)
            gk = dot(grad_scores, qm)
            gv = dot(probs.astype(BF), gh)
            if finish == LEN:
                r.gk[...] = gk
                r.gv[...] = gv
            else:
                r.gk[0:finish, :] += gk
                r.gv[0:finish, :] += gv
        low = r.gv[...].astype(BF)
        r.act[:, rows_of(PAIRS + pair, 128)] = r.gk[...].astype(BF)
        r.act[:, rows_of(2 * PAIRS + pair, 128)] = low
        r.gvec[G_QBIAS : G_QBIAS + 1, cols] = qsum
        r.gvec[G_VBIAS : G_VBIAS + 1, cols] = jnp.sum(low.astype(F32), axis=0, keepdims=True)

    def grad_joint(unit, low, high):
        start = JOINT_COLS[unit]
        grad = dot(r.h1[...], r.act[:, start + low : start + high], 0, 0).astype(BF)
        r.wall[7 + unit, :, :, :, :, low:high] = grad.reshape(2, 2, 2, SLAB, high - low)

    @stage
    def run_attend_back():
        def step(i):
            attend_back(i)

            @pl.when(i == PAIRS // 2 - 1)
            def _():
                for unit in (0, 1, 2):
                    grad_joint(unit, 0, HALF)

            @pl.when(i == PAIRS - 2)
            def _():
                for unit in (3, 4):
                    grad_joint(unit, 0, 256)

            comm.tick("attend_back", i)

        loop(PAIRS, step)

    @stage
    def run_grad_joint():
        for unit in (3, 4):
            grad_joint(unit, 256, HALF)

    def grad_norm_one(i, sums):
        rows = rows_of(i, 256)
        weights = jnp.concatenate([r.wall[u].reshape(D, HALF) for u in (0, 3, 1, 4, 2)], axis=1)
        grad_hidden = dot(r.act[rows, 0 : 2 * D + HALF], weights, 1, 1)
        grad_in, gain, shift = norm_back(r.again[rows, :].astype(F32), grad_hidden, vrow(GAIN1))
        r.cot[rows, :] = (r.resid[rows, :] + grad_in).astype(BF)
        return sums[0] + gain, sums[1] + shift

    @stage
    def run_grad_norm_one():
        zero = jnp.zeros((1, D), F32)
        gain, shift = sum_in_pairs(LEN // 256, grad_norm_one, (zero, zero), functools.partial(comm.tick, "grad_norm_one"))
        r.gvec[G_GAIN1 : G_GAIN1 + 1, :] = gain
        r.gvec[G_SHIFT1 : G_SHIFT1 + 1, :] = shift
    return order


def compute(r, comm):
    comm.start()
    for run in stages(r, comm):
        name = run.__name__.removeprefix("run_")
        comm.before(name)
        run()
        comm.after(name)
    comm.finish()


class Refs:
    def __init__(self, **refs):
        self.__dict__.update(refs)


STATE = dict(
    tokens=((LEN, D), BF),
    cot=((LEN, D), BF),
    wall=((UNITS, 2, 2, 2, SLAB, HALF), BF),
    wc=((2, 2, 2, FF // 8, D), BF),
    vec=((VROWS, D), F32),
    gvec=((GROWS, D), F32),
    h1=((LEN, D), BF),
    q=((LEN, D), BF),
    k=((LEN, D), BF),
    v=((LEN, D), BF),
    mixed=((D, LEN), BF),
    logs=((PAIRS, 8, LEN), F32),
    resid=((LEN, D), F32),
    act=((LEN, FF), BF),
    gp=((LEN, FF), BF),
    gc=((2, 2, 2, FF // 8, D), BF),
    ge=((2, 2, 2, FF // 8, D), BF),
    gk=((LEN, 128), F32),
    gv=((LEN, 128), F32),
)
ANY = pl.BlockSpec(memory_space=pl.ANY)
VMEM = pl.BlockSpec(memory_space=pltpu.VMEM)


class Whole(Nothing):
    def __init__(self, r, sem):
        self.r, self.sem = r, sem

    def move(self, source, target):
        copy = pltpu.make_async_copy(source, target, self.sem)
        copy.start()
        copy.wait()

    def start(self):
        r = self.r
        for source, target in (
            (r.tokens_in, r.tokens), (r.first_in, r.v.at[:, HALF:D]), (r.cot_in, r.cot),
            (r.wall_in, r.wall), (r.wc_in, r.wc), (r.vec_in, r.vec),
        ):
            self.move(source, target)

    def before(self, what):
        if what == "grad_norm_one":
            self.move(self.r.tokens_in, self.r.again)

    def after(self, what):
        r = self.r
        if what == "block_out":
            self.move(r.act.at[:, 0:D], r.block_output)
        elif what == "grad_norm_one":
            self.move(r.cot, r.grad_tokens)
        elif what == "grad_pre":
            self.move(r.gc, r.gc_out)
            self.move(r.ge, r.ge_out)
        elif what == "grad_output":
            self.move(r.wall.at[12:14], r.gjo_out.at[5:7])
        elif what == "grad_joint":
            self.move(r.wall.at[7:12], r.gjo_out.at[0:5])
            self.move(r.act.at[:, 2 * D + HALF : 3 * D], r.grad_first)

    def finish(self):
        self.move(self.r.gvec, self.r.gvec_out)


def whole_kernel(*refs):
    names = ["tokens_in", "first_in", "cot_in", "wall_in", "wc_in", "vec_in"]
    names += ["block_output", "grad_tokens", "grad_first", "gc_out", "ge_out", "gjo_out", "gvec_out"]
    names += list(STATE) + ["sem"]
    r = Refs(**dict(zip(names, refs)))
    r.again = r.gp.at[:, 0:D]
    compute(r, Whole(r, r.sem))


def units_of(matrix):
    count = matrix.shape[1] // HALF
    return matrix.reshape(2, 2, 2, SLAB, count, HALF).transpose(4, 0, 1, 2, 3, 5)


def matrix_of(units):
    count = units.shape[0]
    return units.transpose(1, 2, 3, 4, 0, 5).reshape(D, count * HALF)


def outside(args):
    (tokens, first_values, cotangent, gain1, shift1, joint, qbias, vbias, output, obias,
     gain2, shift2, expand, ebias, contract, cbias) = args
    gather = functools.partial(lax.all_gather, axis_name=AXES, axis=0, tiled=True)
    scatter = functools.partial(lax.psum_scatter, axis_name=AXES, scatter_dimension=0, tiled=True)
    joint_units = units_of(gather(joint))
    wall = jnp.concatenate(
        [jnp.stack([joint_units[start // HALF] for start in JOINT_COLS]), units_of(gather(output)), units_of(gather(expand))]
    )
    wc = gather(contract).reshape(2, 2, 2, FF // 8, D)
    vec = jnp.stack([gather(v) for v in (gain1, shift1, qbias, vbias, obias, gain2, shift2, cbias)])
    vec = jnp.concatenate([vec, gather(ebias).reshape(4, D), jnp.zeros((4, D), BF)]).astype(F32)
    sds = jax.ShapeDtypeStruct
    block_output, grad_tokens, grad_first, gc, ge, gjo, gvec = pl.pallas_call(
        whole_kernel,
        out_shape=(
            sds((LEN, D), BF), sds((LEN, D), BF), sds((LEN, HALF), BF), sds(wc.shape, BF), sds(wc.shape, BF),
            sds((7,) + wall.shape[1:], BF), sds((GROWS, D), F32),
        ),
        in_specs=[ANY] * 6,
        out_specs=(ANY,) * 7,
        scratch_shapes=[pltpu.VMEM(*item) for item in STATE.values()] + [pltpu.SemaphoreType.DMA],
        compiler_params=pltpu.CompilerParams(vmem_limit_bytes=64 * 2**20),
    )(tokens, first_values, cotangent, wall, wc, vec)
    gc = gc.reshape(FF, D).astype(F32)
    ge = ge.reshape(8, 4, SLAB, 2, HALF).transpose(0, 2, 3, 1, 4).reshape(D, FF).astype(F32)
    order = [JOINT_COLS.index(start * HALF) for start in range(5)]
    gj = jnp.concatenate([matrix_of(gjo[u : u + 1]) for u in order], axis=1).astype(F32)
    go = matrix_of(gjo[5:7]).astype(F32)
    small = [scatter(gvec[i]) for i in (0, 1, 8, 9, 10, 11, 12, 13)]
    return (
        block_output, grad_tokens, grad_first, small[GAIN1], small[SHIFT1], scatter(gj), small[QBIAS], small[VBIAS],
        scatter(go), small[OBIAS], small[GAIN2], small[SHIFT2], scatter(ge), scatter(gvec[G_EBIAS : G_EBIAS + 4].reshape(FF)),
        scatter(gc), small[CBIAS],
    )


class Linked:
    def __init__(self, r, depth):
        self.r, self.depth = r, depth
        wide, self.mz = lax.axis_index("wide"), lax.axis_index("narrow")
        self.my, self.mx, self.mc = wide // 4, (wide // 2) % 2, wide % 2
        self.peer = {
            "c": (wide + 1 - 2 * self.mc, self.mz),
            "x": (wide + 2 - 4 * self.mx, self.mz),
            "y": (wide + 4 - 8 * self.my, self.mz),
            "d": (wide + 4 - 8 * self.my + 2 - 4 * self.mx, self.mz),
        }
        for d in range(1, depth):
            self.peer["z%d" % d] = (wide, lax.rem(self.mz + d, depth))
        self.far = [lax.rem(self.mz + d, depth) for d in range(depth)]
        self.share = SLAB // depth

    def remote(self, source, target, sems, place, where):
        send, recv = sems
        return pltpu.make_async_remote_copy(
            src_ref=source, dst_ref=target, send_sem=send.at[place], recv_sem=recv.at[place],
            device_id=self.peer[where], device_id_type=MESH,
        )

    def weights(self, g):
        if g[0] == "C":
            return self.r.wc, (), pl.ds(C_LANES[g][0], C_LANES[g][1] - C_LANES[g][0])
        a, b, low, high = WEIGHT_SPAN[g]
        return self.r.wall, (pl.ds(a, b - a),), pl.ds(low, high - low)

    def source(self, g):
        r = self.r
        return {"J": (r.wj_in, r.sj), "O": (r.wo_in, r.so), "E": (r.we_in, r.se)}[g[0]] + (WEIGHT_COLS[g],)

    def gather_copies(self, g, step):
        r, y, x, c, both = self.r, self.my, self.mx, self.mc, slice(None)
        ref, lead, lanes = self.weights(g)
        index, late = GROUPS.index(g), g in LATE_Z
        phase = ("z", 1, 2, "c")[step] if not late else (1, 2, "z", "c")[step]
        if phase == "z":
            out = []
            for d in range(1, self.depth):
                if late:
                    view = ref.at[lead + (both, both, c, rows_of(self.mz, SLAB), lanes)]
                    parts = [(view, view)]
                elif g[0] == "C":
                    parts = [(r.wc_in.at[:, lanes], ref.at[lead + (y, x, c, rows_of(self.mz, SLAB), lanes)])]
                else:
                    rows, stage, spans = self.source(g)
                    parts = [(rows.at[:, a:b], stage.at[self.mz, :, a:b]) for a, b in spans]
                for part, (source, target) in enumerate(parts):
                    place = (index, d - 1, part)
                    out.append(self.remote(source, target, (r.gz_send, r.gz_recv), place, "z%d" % d))
            return out
        low, high = (pl.ds(0, FF // 16), pl.ds(FF // 16, FF // 16)) if g[0] == "C" else (
            pl.ds(0, SLAB // 2), pl.ds(SLAB // 2, SLAB // 2))
        if late:
            start = pl.multiple_of(self.mz * SLAB, SLAB)
            low, high = pl.ds(start, SLAB // 2), pl.ds(pl.multiple_of(start + SLAB // 2, SLAB // 2), SLAB // 2)
        if phase == 1:
            plan = [((y, x, c, low), "x", 0), ((y, x, c, high), "y", 1)]
        elif phase == 2:
            plan = [((y, both, c, low), "y", 2), ((both, x, c, high), "x", 3)]
        else:
            plan = [((both, both, c, both), "c", 4)]
        sems = (r.g_send, r.g_recv)
        views = [(ref.at[lead + at + (lanes,)], n, w) for at, w, n in plan]
        return [self.remote(view, view, sems, (index, n), w) for view, n, w in views]

    def assemble(self, g):
        r = self.r
        if g[0] == "C":
            low, high = C_LANES[g]
            r.wc[self.my, self.mx, self.mc, rows_of(self.mz, SLAB), low:high] = r.wc_in[:, low:high]
            return
        source, stage, spans = self.source(g)
        first, _, low, high = WEIGHT_SPAN[g]
        for unit, start in enumerate(s for a, b in spans for s in range(a, b, high - low)):
            stop = start + high - low
            stage[self.mz, :, start:stop] = source[:, start:stop]
            rows = jnp.concatenate([stage[z, :, start:stop].astype(F32) for z in range(self.depth)], axis=0)
            r.wall[first + unit, self.my, self.mx, self.mc, :, low:high] = rows.astype(BF)

    def gather(self, g, step):
        if step > 0:
            for copy in self.gather_copies(g, step - 1):
                copy.wait_recv()
        if step == (0 if g in LATE_Z else 1):
            self.assemble(g)
        if step < 4:
            for copy in self.gather_copies(g, step):
                copy.start()
        else:
            for n in range(4):
                for copy in self.gather_copies(g, n):
                    copy.wait_send()

    def vec_wheres(self, kind):
        return {"c": ["c"], "p": ["x", "y", "d"], "z": ["z%d" % d for d in range(1, self.depth)]}[kind]

    def vec_copies(self, way, step):
        r = self.r
        held, got, kinds = self.vec_ways(way)
        out = []
        for where in self.vec_wheres(kinds[step]):
            n = self.vec_place(where)
            out.append(self.remote(held, got(n), (r.v_send, r.v_recv), (way, n), where))
        return out

    def vec_place(self, where):
        return "cxyd".index(where) if where in "cxyd" else 3 + int(where[1])

    def vec_ways(self, way):
        r = self.r
        if way in (0, 3):
            return r.vsum.at[way // 3], lambda n: r.vgot.at[way // 3, n], "zpc"
        if way == 1:
            return r.gvec.at[8:GROWS, :], lambda n: r.ggot.at[n], "cpz"
        return r.last, lambda n: r.lgot.at[n], "cpz"

    def vec_step(self, way, step):
        r = self.r
        held, got, kinds = self.vec_ways(way)
        if way == 2 and step == 0:
            for row in range(2):
                for side in range(2):
                    r.last[2 * row + side : 2 * row + side + 1, :] = r.gvec[row : row + 1, side * HALF : (side + 1) * HALF]
        if step > 0:
            for copy in self.vec_copies(way, step - 1):
                copy.wait()
            kind = kinds[step - 1]
            total = held[...].astype(F32)
            for where in self.vec_wheres(kind):
                total = total + got(self.vec_place(where))[...].astype(F32)
            if step == 3 and way in (0, 3):
                rows = slice(0, 8) if way == 0 else slice(8, 16)
                r.vec[rows, 0:HALF] = total[0:8]
                r.vec[rows, HALF:D] = total[8:16]
            elif step == 3 and way == 2:
                for row in range(2):
                    for side in range(2):
                        r.gvec[row : row + 1, side * HALF : (side + 1) * HALF] = total[2 * row + side : 2 * row + side + 1]
            else:
                held[...] = total.astype(held.dtype)
        if step < 3:
            for copy in self.vec_copies(way, step):
                copy.start()

    def grads(self, g):
        r = self.r
        if g[0] in "CE":
            low, high = C_LANES[g] if g[0] == "C" else (int(g[1]) * HALF, int(g[1]) * HALF + HALF)
            return [(r.gc if g[0] == "C" else r.ge, (), 0, low)], FF // 8, (low, high)
        a, b, low, high = GRAD_SPAN[g]
        units = [(r.wall, (u,), (u - 7) % 4 * SLAB, (u - 7) // 4 * HALF + low) for u in range(a, b)]
        return units, SLAB, (low, high)

    def slices(self, g, height, rows_at, lanes_at, wide):
        r = self.r
        if g in LATE_Z:
            start, half = pl.multiple_of(self.mz * SLAB, SLAB), SLAB // 2
            low, high = pl.ds(start, half), pl.ds(pl.multiple_of(start + half, half), half)
            return low, high, pl.ds(0, half), pl.ds(0, wide), r.late_one, r.late_two
        half = height // 2
        return pl.ds(0, half), pl.ds(half, half), pl.ds(rows_at // 2, half), pl.ds(lanes_at, wide), r.near_one, r.near_two

    def scatter_copies(self, g, step):
        units, height, (left, right) = self.grads(g)
        r, index, late = self.r, SUMS.index(g), g in LATE_Z
        y, x, c, both = self.my, self.mx, self.mc, slice(None)
        lanes = pl.ds(left, right - left)
        phase = ("c", 1, 2, "z")[step] if not late else ("c", "z", 1, 2)[step]
        out = []
        if phase == "z":
            for d in range(1, self.depth):
                far = self.far[d]
                ref = units[0][0]
                if late:
                    parts = [(ref.at[both, both, c, rows_of(far, SLAB), lanes], r.late.at[d - 1])]
                elif g[0] == "C":
                    parts = [(ref.at[y, x, c, rows_of(far, SLAB), lanes], r.zc.at[d - 1])]
                else:
                    stage, got, spans = self.stage(g)
                    parts = [(stage.at[far, :, a:b], got.at[d - 1, :, a:b]) for a, b in spans]
                for part, (source, target) in enumerate(parts):
                    out.append(self.remote(source, target, (r.sz_send, r.sz_recv), (index, d - 1, part), "z%d" % d))
            return out
        for part, (ref, lead, rows_at, lanes_at) in enumerate(units):
            low, high, near, near_lanes, one, two = self.slices(g, height, rows_at, lanes_at, right - left)
            if phase == "c":
                target = r.core.at[:, :, pl.ds(rows_at, height), pl.ds(lanes_at, right - left)]
                plan = [((both, both, 1 - c, both), target, "c", 0)]
            elif phase == 1:
                plan = [
                    ((both, 1 - x, c, low), one.at[0, :, near, near_lanes], "x", 1),
                    ((1 - y, both, c, high), one.at[1, :, near, near_lanes], "y", 2),
                ]
            else:
                plan = [
                    ((1 - y, x, c, low), two.at[0, near, near_lanes], "y", 3),
                    ((y, 1 - x, c, high), two.at[1, near, near_lanes], "x", 4),
                ]
            for at, target, where, n in plan:
                out.append(self.remote(ref.at[lead + at + (lanes,)], target, (r.s_send, r.s_recv), (index, n, part), where))
        return out

    def stage(self, g):
        r = self.r
        stage, got = {"J": (r.sj, r.zj), "O": (r.so, r.zo), "E": (r.se, r.ze)}[g[0]]
        return stage, got, GRAD_COLS[g]

    def add_up(self, g, phase):
        r, y, x, c = self.r, self.my, self.mx, self.mc
        units, height, (left, right) = self.grads(g)
        late, lanes = g in LATE_Z, pl.ds(left, right - left)
        if phase == 2 and g[0] != "C":
            stage, _, spans = self.stage(g)
            places = iter([(s, s + right - left) for a, b in spans for s in range(a, b, right - left)])
        for ref, lead, rows_at, lanes_at in units:
            low, high, near, near_lanes, one, two = self.slices(g, height, rows_at, lanes_at, right - left)

            def add(at, *got, ref=ref, lead=lead):
                at = lead + at + (lanes,)
                if len(got) == 1:
                    ref[at] = ref[at] + got[0]
                    return
                total = ref[at].astype(F32)
                for item in got:
                    total = total + item.astype(F32)
                ref[at] = total.astype(BF)

            if phase == "c":
                def step(i, rows_at=rows_at, lanes_at=lanes_at, add=add):
                    got = r.core[i // 2, i % 2, pl.ds(rows_at, height), pl.ds(lanes_at, right - left)]
                    add((i // 2, i % 2, c, slice(None)), got)

                loop(4, step)
            elif phase == "z":
                def step(i, add=add):
                    got = [r.late[d, i // 2, i % 2] for d in range(self.depth - 1)]
                    add((i // 2, i % 2, c, rows_of(self.mz, SLAB)), *got)

                loop(4, step)
            elif phase == 1:
                def step(i, add=add, low=low, high=high, near=near, near_lanes=near_lanes, one=one):
                    add((i, x, c, low), one[0, i, near, near_lanes])
                    add((y, i, c, high), one[1, i, near, near_lanes])

                loop(2, step)
            elif g[0] == "C" and not late:
                add((y, x, c, low), two[0, near, near_lanes])
                add((y, x, c, high), two[1, near, near_lanes])
            else:
                final = [
                    ref[lead + (y, x, c, half, lanes)].astype(F32) + two[part, near, near_lanes].astype(F32)
                    for part, half in enumerate((low, high))
                ]
                if late:
                    r.gc_out[0 : SLAB // 2, left:right] = final[0]
                    r.gc_out[SLAB // 2 : SLAB, left:right] = final[1]
                    continue
                final = jnp.concatenate(final, axis=0)
                for s in range(0, height, SLAB):
                    start, stop = next(places)
                    for z in range(self.depth):
                        rows = final[s + z * self.share : s + (z + 1) * self.share]
                        stage[z, :, start:stop] = rows.astype(BF)

    def put_out(self, g):
        r = self.r
        if g[0] == "C":
            left, right = C_LANES[g]
            total = r.gc[self.my, self.mx, self.mc, rows_of(self.mz, SLAB), left:right].astype(F32)
            for d in range(self.depth - 1):
                total = total + r.zc[d].astype(F32)
            r.gc_out[:, left:right] = total
            return
        stage, got, spans = self.stage(g)
        out = {"J": r.gj_out, "O": r.go_out, "E": r.ge_out}[g[0]]
        for a, b in spans:
            total = stage[self.mz, :, a:b].astype(F32)
            for d in range(self.depth - 1):
                total = total + got[d, :, a:b].astype(F32)
            out[:, a:b] = total

    def scatter(self, g, step):
        r, late = self.r, g in LATE_Z
        phases = ("c", "z", 1, 2) if late else ("c", 1, 2, "z")
        if step > 0:
            for copy in self.scatter_copies(g, step - 1):
                copy.wait_recv()
            if phases[step - 1] == "z" and not late:
                self.put_out(g)
            else:
                self.add_up(g, phases[step - 1])
        turns = {"c": [(0, "c")], 1: [(1, "x"), (2, "y")], 2: [(3, "y"), (4, "x")], "z": []}
        own = {"c": turns["c"]} if late else turns
        if g in OWNERS and step > 0:
            for n, where in own.get(phases[step - 1], []):
                pl.semaphore_signal(
                    r.free_sem.at[n, OWNERS.index(g)], inc=1, device_id=self.peer[where], device_id_type=MESH
                )
        if step < 4:
            for before in {"E0": ("C0",), "E1": ("C1",), "O0": ("E0", "E1")}.get(g, ()):
                for n, _ in turns[phases[step]]:
                    if before not in LATE_Z or n == 0:
                        pl.semaphore_wait(r.free_sem.at[n, OWNERS.index(before)], 1)
            for copy in self.scatter_copies(g, step):
                copy.start()
        else:
            for n in range(4):
                for copy in self.scatter_copies(g, n):
                    copy.wait_send()
            for copy in self.leaving(g):
                copy.start()

    def leaving(self, g):
        r = self.r
        source, target = {"J": (r.gj_out, r.gj_to), "O": (r.go_out, r.go_to), "E": (r.ge_out, r.ge_to), "C": (r.gc_out, r.gc_to)}[g[0]]
        spans = [C_LANES[g]] if g[0] == "C" else GRAD_COLS[g]
        return [
            pltpu.make_async_copy(source.at[:, a:b], target.at[:, a:b], r.out_sem.at[SUMS.index(g), n])
            for n, (a, b) in enumerate(spans)
        ]

    def run(self, words):
        for word in words:
            name, step = word.split(".")
            step = int(step)
            if name[0] == "v":
                self.vec_step(int(name[1]), step)
            elif name[0] == "g":
                self.gather(name[1:], step)
            elif name[0] == "s":
                self.scatter(name[1:], step)
            elif step < 10:
                self.local(step).wait()
            else:
                self.local(step - 10).start()

    def local(self, n):
        r = self.r
        source, target = (
            (r.tokens_in, r.tokens),
            (r.first_in, r.v.at[:, HALF:D]),
            (r.cot_in, r.cot),
            (r.tokens_in, r.again),
            (r.act.at[:, 2 * D + HALF : 3 * D], r.grad_first),
            (r.act.at[:, 0:D], r.block_output),
            (r.cot, r.grad_tokens),
            (r.wj_from, r.wj_in), (r.wo_from, r.wo_in), (r.we_from, r.we_in), (r.wc_from, r.wc_in),
        )[n]
        return pltpu.make_async_copy(source, target, r.local_sem.at[n])

    def place_vectors(self):
        r, share = self.r, self.share
        me = lax.axis_index("wide") * self.depth + self.mz
        r.vec[...] = jnp.zeros_like(r.vec)
        for n in range(8):
            r.vec[n, 0:share] = getattr(r, "vec%d" % n)[...].astype(F32)
        r.vec[8, 0 : 4 * share] = r.vec8[...].astype(F32)
        placed = pltpu.roll(r.vec[0:8, :], me * share, 1)
        r.vsum[0] = jnp.concatenate([placed[:, :HALF], placed[:, HALF:]], axis=0).astype(BF)
        start = me * 4 * share
        wide_bias = pltpu.roll(r.vec[8:VROWS, :], lax.rem(start, D), 1)[0:1]
        rows = lax.broadcasted_iota(jnp.int32, (VROWS - 8, D), 0) == start // D
        placed = jnp.where(rows, wide_bias, 0.0)
        r.vsum[1] = jnp.concatenate([placed[:, :HALF], placed[:, HALF:]], axis=0).astype(BF)

    def start(self):
        r = self.r
        barrier = pltpu.get_barrier_semaphore()
        for where in self.peer:
            pl.semaphore_signal(barrier, inc=1, device_id=self.peer[where], device_id_type=MESH)
        for n in (7, 8, 9, 10, 0, 2, 1):
            self.local(n).start()
        self.place_vectors()
        for n in (7, 8, 9, 10):
            self.local(n).wait()
        pl.semaphore_wait(barrier, len(self.peer))
        self.run(PLAN["start"])

    def before(self, what):
        self.run(PLAN.get("before " + what, ()))

    def after(self, what):
        self.run(PLAN.get("after " + what, ()))

    def tick(self, what, i):
        for n in range(8):
            words = PLAN.get("%s %d" % (what, n), ())
            if words:
                @pl.when(i == n)
                def _(words=words):
                    self.run(words)

    def finish(self):
        self.run(PLAN["finish"])
        for g in SUMS:
            for copy in self.leaving(g):
                copy.wait()


WEIGHT_SPAN = dict(
    J0=(0, 3, 0, 128), J1=(0, 3, 128, 384), J2=(3, 5, 0, 384), O0=(5, 7, 0, 384),
    E0=(7, 9, 0, 384), E1=(9, 11, 0, 384), E2=(11, 13, 0, 384), E3=(13, 15, 0, 384),
)
WEIGHT_COLS = dict(
    J0=[(c, c + 128) for c in JOINT_COLS[0:3]], J1=[(c + 128, c + HALF) for c in JOINT_COLS[0:3]],
    J2=[(c, c + HALF) for c in JOINT_COLS[3:5]], O0=[(0, D)],
    E0=[(0, D)], E1=[(D, 2 * D)], E2=[(2 * D, 3 * D)], E3=[(3 * D, 4 * D)],
)
GROUPS = tuple(WEIGHT_SPAN) + ("C0", "C1")
GRAD_SPAN = dict(J0=(7, 10, 0, 384), J1=(10, 12, 0, 256), J2=(10, 12, 256, 384), O0=(12, 14, 0, 384))
GRAD_COLS = dict(
    J0=[(c, c + HALF) for c in JOINT_COLS[0:3]], J1=[(c, c + 256) for c in JOINT_COLS[3:5]],
    J2=[(c + 256, c + HALF) for c in JOINT_COLS[3:5]], O0=[(0, D)], E0=[(0, 2 * D)], E1=[(2 * D, 4 * D)],
)
SUMS = ("C0", "C1", "E0", "E1") + tuple(GRAD_SPAN)
C_LANES = dict(C0=(0, 512), C1=(512, 768))
OWNERS = ("C0", "C1", "E0", "E1")
LATE_Z = ("C1",)
PLAN = {
    "start": ("gJ0.0", "v0.0", "gC1.0", "gJ1.0", "gJ0.1", "gC1.1", "v0.1", "local.0", "gO0.0", "gJ1.1", "gE1.0",),
    "before contract_bias": ("v0.2", "gJ0.2", "gJ2.0", "v0.3", "local.2", "gO0.1",),
    "after contract_bias": ("gE0.0", "gJ1.2",),
    "before norm_one": ("gJ0.3", "gO0.2",),
    "after norm_one": ("gJ2.1", "gE1.1", "gE3.0",),
    "before project_a": ("gJ0.4",),
    "before attend": ("gE0.1", "v3.0", "gJ1.3", "gE2.0",),
    "attend 0": ("gC0.0", "gO0.3", "gJ2.2",),
    "before project_b": ("gJ1.4",),
    "attend_m 1": ("gE1.2",),
    "attend_m 2": ("gE3.1",),
    "attend 2": ("gE0.2",),
    "before project_c": ("gJ2.3", "v3.1", "gJ2.4", "local.1",),
    "attend_m 3": ("gC1.2", "gO0.4", "gE3.2",),
    "attend 3": ("gE2.1", "gE1.3",),
    "attend_m 4": ("gC0.1", "gE0.3",),
    "attend_m 5": ("v3.2",),
    "attend 5": ("gE0.4",),
    "after attend": ("gE3.3",),
    "after out_project": ("gE2.2",),
    "before expand": ("v3.3", "gE3.4",),
    "expand_b 0": ("gC0.2", "gE1.4",),
    "expand_b 1": ("gE2.3",),
    "expand_a 2": ("gE2.4",),
    "expand_b 2": ("gC1.3",),
    "expand_b 3": ("gC0.3",),
    "expand_c 3": ("sC1.0", "gC1.4",),
    "after expand": ("sC0.0", "gC0.4",),
    "block_out 2": ("sC0.1",),
    "after block_out": ("local.15", "sC1.1",),
    "grad_expand 1": ("sE0.0",),
    "grad_expand 2": ("sC0.2",),
    "grad_expand 3": ("sE0.1", "sE1.0",),
    "after grad_norm_two": ("local.13", "sE1.1",),
    "after grad_output": ("sC0.3",),
    "before attend_back": ("sO0.0", "local.5",),
    "back_m 0": ("sE0.2",),
    "back_m 1": ("sE1.2",),
    "attend_back 2": ("sO0.1", "sJ0.0", "sE1.3",),
    "back_m 3": ("sE0.3", "sJ0.1",),
    "back_m 4": ("sO0.2",),
    "attend_back 4": ("sJ1.0", "sJ0.2",),
    "back_m 5": ("sJ1.1", "sO0.3",),
    "after attend_back": ("local.14",),
    "before grad_joint": ("v1.0",),
    "after grad_joint": ("sJ0.3", "v1.1",),
    "before grad_norm_one": ("local.3", "sJ2.0", "local.4",),
    "grad_norm_one 1": ("sJ1.2", "sJ2.1", "v1.2",),
    "grad_norm_one 3": ("sE0.4", "sJ2.2", "sJ1.3",),
    "after grad_norm_one": ("sC1.2", "v2.0", "v2.1", "local.16", "sJ2.3", "sC1.3",),
    "finish": ("v1.3", "sC0.4", "sJ0.4", "sE1.4", "v2.2", "sC1.4", "sO0.4", "sJ2.4", "sJ1.4", "local.6", "v2.3",),
}


def linked_scratch(depth):
    share = SLAB // depth
    far = max(depth - 1, 1)
    dma = pltpu.SemaphoreType.DMA
    return dict(
        wj_in=pltpu.VMEM((share, 2 * D + HALF), BF), wo_in=pltpu.VMEM((share, D), BF),
        we_in=pltpu.VMEM((share, FF), BF), wc_in=pltpu.VMEM((SLAB, D), BF),
        gj_out=pltpu.VMEM((share, 2 * D + HALF), F32), go_out=pltpu.VMEM((share, D), F32),
        ge_out=pltpu.VMEM((share, FF), F32), gc_out=pltpu.VMEM((SLAB, D), F32),
        sj=pltpu.VMEM((depth, share, 2 * D + HALF), BF),
        so=pltpu.VMEM((depth, share, D), BF),
        se=pltpu.VMEM((depth, share, FF), BF),
        zj=pltpu.VMEM((far, share, 2 * D + HALF), BF),
        zo=pltpu.VMEM((far, share, D), BF),
        ze=pltpu.VMEM((far, share, FF), BF),
        zc=pltpu.VMEM((far, SLAB, C_LANES["C0"][1]), BF),
        late=pltpu.VMEM((far, 2, 2, SLAB, D - C_LANES["C1"][0]), BF),
        late_one=pltpu.VMEM((2, 2, SLAB // 2, D - C_LANES["C1"][0]), BF),
        late_two=pltpu.VMEM((2, SLAB // 2, D - C_LANES["C1"][0]), BF),
        core=pltpu.VMEM((2, 2, FF // 8, D), BF),
        near_one=pltpu.VMEM((2, 2, FF // 16, D), BF),
        near_two=pltpu.VMEM((2, FF // 16, D), BF),
        vsum=pltpu.VMEM((2, 16, HALF), BF),
        vgot=pltpu.VMEM((2, 3 + depth, 16, HALF), BF),
        ggot=pltpu.VMEM((3 + depth, GROWS - 8, D), F32),
        last=pltpu.VMEM((8, HALF), F32),
        lgot=pltpu.VMEM((3 + depth, 8, HALF), F32),
        gz_send=dma((10, far, 3)), gz_recv=dma((10, far, 3)), g_send=dma((10, 5)), g_recv=dma((10, 5)),
        sz_send=dma((8, far, 3)), sz_recv=dma((8, far, 3)), s_send=dma((8, 5, 3)), s_recv=dma((8, 5, 3)),
        v_send=dma((4, 3 + depth)), v_recv=dma((4, 3 + depth)), local_sem=dma((11,)), out_sem=dma((8, 3)),
        free_sem=pltpu.SemaphoreType.REGULAR((5, 4)),
    )


def linked_kernel(depth, *refs):
    names = ["tokens_in", "first_in", "cot_in", "wj_from", "wo_from", "we_from", "wc_from"]
    names += ["vec%d" % n for n in range(9)]
    names += ["gvec_out", "block_output", "grad_tokens", "grad_first", "gj_to", "go_to", "ge_to", "gc_to"]
    names += list(STATE) + list(linked_scratch(depth))
    r = Refs(**dict(zip(names, refs)))
    r.again = r.gp.at[:, 0:D]
    compute(r, Linked(r, depth))
    r.gvec_out[...] = r.gvec[...]


def closing_kernel(depth, *refs):
    gvec, moved, targets, vectors, sem = refs[0], refs[1:8], refs[8:15], refs[15:24], refs[24]
    passing = refs[25:32]
    arrive = [pltpu.make_async_copy(a, b, sem.at[0, n]) for n, (a, b) in enumerate(zip(moved, passing))]
    leave = [pltpu.make_async_copy(a, b, sem.at[1, n]) for n, (a, b) in enumerate(zip(passing, targets))]
    for copy in arrive:
        copy.start()
    me = lax.axis_index("wide") * depth + lax.axis_index("narrow")
    share = SLAB // depth
    small = pltpu.roll(gvec[0:G_EBIAS, :], lax.rem(D - me * share, D), 1)
    start = me * 4 * share
    rows = lax.broadcasted_iota(jnp.int32, (4, D), 0) == start // D
    wide_bias = jnp.sum(jnp.where(rows, gvec[G_EBIAS : G_EBIAS + 4, :], 0.0), axis=0, keepdims=True)
    wide_bias = pltpu.roll(jnp.broadcast_to(wide_bias, (8, D)), lax.rem(D - lax.rem(start, D), D), 1)
    for n, row in enumerate((G_GAIN1, G_SHIFT1, G_QBIAS, G_VBIAS, G_OBIAS, G_GAIN2, G_SHIFT2, G_CBIAS)):
        vectors[n][...] = small[row, 0:share]
    vectors[8][...] = wide_bias[0, 0 : 4 * share]
    for first, second in zip(arrive, leave):
        first.wait()
        second.start()
    for copy in leave:
        copy.wait()


def linked(depth, args):
    (tokens, first_values, cotangent, gain1, shift1, joint, qbias, vbias, output, obias,
     gain2, shift2, expand, ebias, contract, cbias) = args
    share = SLAB // depth
    sds = jax.ShapeDtypeStruct
    results = pl.pallas_call(
        functools.partial(linked_kernel, depth),
        out_shape=(
            sds((GROWS, D), F32), sds((LEN, D), BF), sds((LEN, D), BF), sds((LEN, HALF), BF), sds(joint.shape, F32),
            sds(output.shape, F32), sds(expand.shape, F32), sds(contract.shape, F32),
        ),
        in_specs=[ANY] * 7 + [VMEM] * 9,
        out_specs=(VMEM,) + (ANY,) * 7,
        scratch_shapes=[pltpu.VMEM(*item) for item in STATE.values()] + list(linked_scratch(depth).values()),
        compiler_params=pltpu.CompilerParams(
            vmem_limit_bytes=64 * 2**20, collective_id=0, has_side_effects=True
        ),
    )(tokens, first_values, cotangent, joint, output, expand, contract,
      gain1, shift1, qbias, vbias, obias, gain2, shift2, cbias, ebias)
    vectors = (sds((share,), F32),) * 8 + (sds((4 * share,), F32),)
    closed = pl.pallas_call(
        functools.partial(closing_kernel, depth),
        out_shape=tuple(sds(item.shape, item.dtype) for item in results[1:]) + vectors,
        in_specs=[VMEM] + [ANY] * 7,
        out_specs=(ANY,) * 7 + (VMEM,) * 9,
        scratch_shapes=[pltpu.SemaphoreType.DMA((2, 7))] + [pltpu.VMEM(item.shape, item.dtype) for item in results[1:]],
    )(*results)
    block_output, grad_tokens, grad_first, gj, go, ge, gc = closed[:7]
    gain1, shift1, qbias, vbias, obias, gain2, shift2, cbias, ebias = closed[7:]
    return (
        block_output, grad_tokens, grad_first, gain1, shift1, gj, qbias, vbias, go, obias, gain2, shift2, ge, ebias, gc, cbias
    )


def solution(mesh):
    split, flat = P(AXES, None), P(AXES)
    wide, depth = mesh.shape["wide"], mesh.shape["narrow"]
    if wide == 8 and SLAB % (8 * depth) == 0:
        body = lambda *args: linked(depth, args)
    else:
        body = lambda *args: outside(args)
    return jax.shard_map(
        body,
        mesh=mesh,
        in_specs=(split, split, split, flat, flat, split, flat, flat, split, flat, flat, flat, split, flat, split, flat),
        out_specs=(split, split, split, flat, flat, split, flat, flat, split, flat, flat, flat, split, flat, split, flat),
        check_vma=False,
    )
```
